256 devices in a mesh: narrow: 8 (over y_hi, x), wide: 32 (over y_lo, z, core).
Axes of the slice: x: 4, y: 4 (y_hi: 2, y_lo: 2; y = y_hi * 2 + y_lo), z: 8, core: 2. Of those that a mesh axis runs over, the one named last changes fastest.
Arguments:
- order_and_alloy_stack: float32 [2, 32, 2048, 512], P(None, 'narrow', 'wide'), may hold values from -1 to 1
- crystal_identifier: int32 [8, 512, 128], P('narrow', 'wide'), may hold values from 0 to 63
- frozen_indicator: int32 [8, 512, 128], P('narrow', 'wide'), may hold values 0 or 1
- supercool_grid: float32 [8, 512, 128], P('narrow', 'wide'), may hold values from -5 to 5
- crystal_rotation_radians: float32 [64], replicated, may hold values from -3.140625 to 3.140625
Outputs:
- state_new: float32 [2, 32, 2048, 512], P(None, 'narrow', 'wide')
- adjusted_supercool: float32 [8, 512, 128], P('narrow', 'wide')
The draws below stay inside these ranges and needn't reach their ends.
Inputs may be any that keep to these rules, and one draw needn't show every extreme that they name: `crystal_identifier`: grain ids index crystal_rotation_radians.
All inputs are finite; a program needn't handle non-finite values. No bound on the sum of `frozen_indicator` on one device may be relied on, other than what follows from the above.
Results may differ from the reference program's by a relative error of at most 0.0003.
Values sent between devices are 32-bit elements; how exact they have to be, the bound alone decides.
No kernel may reach another device: no remote copies, remote signals or barrier semaphores. Data moves between devices by JAX's collectives and lax.ppermute only.
A program may use at most 192 MiB of HBM per device.

```python
import jax
import jax.numpy as jnp
from jax import lax

BX = 64
NY = 512
COARSEN = 4
FRINGE_BINS = 4
GRAINS = 64
NZ = 32
NX = 2048
ROUGH_SHEETS_UP = 8
ROUGH_BINS_WIDTH = 512
ROUGH_BINS_DEPTH = 128
KERNEL_BINS_WIDE = 16
SUBX = 24
N_WIDE = 32


def place_ends(entries, stream_key, smallest, largest):
    longest = entries.shape.index(max(entries.shape))
    spots = []
    for shift in (0, 1):
        where = [jax.random.randint(jax.random.fold_in(stream_key, axis), (), 0, length) for axis, length in enumerate(entries.shape)]
        where[longest] = (where[longest] + shift) % entries.shape[longest]
        spots.append(tuple(where))
    return entries.at[spots[0]].set(smallest).at[spots[1]].set(largest)


def block_scale(own_key, extent, split, smallest, top_value):
    def one(position, parts):
        draws = jax.random.uniform(jax.random.fold_in(jax.random.fold_in(own_key, 6), position), (parts,), jnp.float32, smallest / len(split), top_value / len(split))
        return jnp.repeat(jnp.exp(draws), extent[position] // parts).reshape((-1,) + (1,) * (len(extent) - position - 1))

    gain = one(*split[0])
    for cut in split[1:]:
        gain = gain * one(*cut)
    return gain


def scatter_about(rng, dims, deviation, bound, shards=(), kind=jnp.bfloat16):
    gain = block_scale(rng, dims, shards, -0.22, 0.18) if shards else 1.0
    drawn = jax.random.normal(rng, dims, jnp.float32) * deviation * gain
    return jnp.minimum(jnp.maximum(drawn, -bound), bound).astype(kind)


def setup_inputs(seed: int = 0) -> dict:
    key_of = jax.random.split(jax.random.key(seed), 6)
    return {
        "order_and_alloy_stack": jnp.clip(jax.random.uniform(key_of[0], (2, NZ, NX, NY), jnp.float32, -1.0, 1.0) * block_scale(key_of[0], (2, NZ, NX, NY), ((1, 8), (2, 32)), -0.4, 0.0), -1.0, 1.0),
        "crystal_identifier": place_ends(jax.random.randint(key_of[1], (ROUGH_SHEETS_UP, ROUGH_BINS_WIDTH, ROUGH_BINS_DEPTH), 0, GRAINS), jax.random.fold_in(key_of[1], 1), 0, GRAINS - 1).astype(jnp.int32),
        "frozen_indicator": place_ends((jax.random.randint(key_of[2], (ROUGH_SHEETS_UP, ROUGH_BINS_WIDTH, ROUGH_BINS_DEPTH), 0, 2) < 1).astype(jnp.int32), jax.random.fold_in(key_of[2], 1), 0, 1),
        "supercool_grid": scatter_about(key_of[3], (ROUGH_SHEETS_UP, ROUGH_BINS_WIDTH, ROUGH_BINS_DEPTH), 1.0, 5.0, ((0, 8), (1, 32)), jnp.float32),
        "crystal_rotation_radians": jnp.clip(jax.random.uniform(key_of[4], (GRAINS,), jnp.float32, -3.140625, 3.140625), -3.140625, 3.140625),
    }


DT = 0.15
EPS4 = 0.15
COUPLING_FACTOR = 1.5
DLIQ = 1.0
DSOL = 0.05
KPART = 0.15
KLIQ = 1.0
KSOL = 0.5
SIGMA = 0.05
KBAR = 0.75
HIGHEST = lax.Precision.HIGHEST

def shift_last(values, offset):
    filler = jnp.zeros_like(values[..., :1])
    if offset > 0:
        return jnp.concatenate([values[..., 1:], filler], -1)
    return jnp.concatenate([filler, values[..., :-1]], -1)

def orient(grain_ids, crystal_rotation_radians):
    labels = jnp.arange(crystal_rotation_radians.shape[0], dtype=jnp.int32)
    matches = grain_ids[..., None] == labels
    cos_c = lax.optimization_barrier(jnp.sum(jnp.where(matches, jnp.cos(crystal_rotation_radians), 0.0), -1))
    sin_c = lax.optimization_barrier(jnp.sum(jnp.where(matches, jnp.sin(crystal_rotation_radians), 0.0), -1))
    return (cos_c, sin_c)

def refine_onto_grid(coarse):
    rough_sheets, rough_verticals, length = coarse.shape
    tiled_up = jnp.broadcast_to(coarse[:, None, :, None, :, None], (rough_sheets, COARSEN, rough_verticals, COARSEN, length, COARSEN))
    return tiled_up.reshape(rough_sheets * COARSEN, rough_verticals * COARSEN, length * COARSEN)

def restrict(fine_field):
    planes_f, columns_f, length = fine_field.shape
    blocks = fine_field.reshape(planes_f // COARSEN, COARSEN, columns_f // COARSEN, COARSEN, length // COARSEN, COARSEN)
    return lax.optimization_barrier(jnp.mean(blocks, axis=(1, 3, 5)))

def flux_of(order_parameter_padded, cosine, sine_t):
    centre = order_parameter_padded[1:-1, 1:-1]
    grad_z = 0.5 * (order_parameter_padded[2:, 1:-1] - order_parameter_padded[:-2, 1:-1])
    grad_x = 0.5 * (order_parameter_padded[1:-1, 2:] - order_parameter_padded[1:-1, :-2])
    grad_y = 0.5 * (shift_last(centre, 1) - shift_last(centre, -1))
    rotated_u = cosine * grad_x + sine_t * grad_y
    rotated_v = cosine * grad_y - sine_t * grad_x
    square = grad_z * grad_z + grad_x * grad_x + grad_y * grad_y
    quartic = (grad_z ** 4 + rotated_u ** 4 + rotated_v ** 4) / (square + 1.0) ** 2
    anisotropy = 1.0 + EPS4 * (4.0 * quartic - 3.0)
    blending_factor = anisotropy * anisotropy
    return ((blending_factor * grad_z, blending_factor * grad_x, blending_factor * grad_y), blending_factor)

def divergence(transport_third, transport_first, transport_second):
    return 0.5 * (transport_third[2:, 1:-1] - transport_third[:-2, 1:-1]) + 0.5 * (transport_first[1:-1, 2:] - transport_first[1:-1, :-2]) + 0.5 * (shift_last(transport_second, 1) - shift_last(transport_second, -1))

def diffuse(order_parameter_padded, alloy_padded):
    order_parameter = order_parameter_padded[1:-1, 1:-1]
    alloy_concentration = alloy_padded[1:-1, 1:-1]
    mobile = DSOL + 0.5 * DLIQ * (1.0 - order_parameter)
    neighbours = [(order_parameter_padded[2:, 1:-1], alloy_padded[2:, 1:-1]), (order_parameter_padded[:-2, 1:-1], alloy_padded[:-2, 1:-1]), (order_parameter_padded[1:-1, 2:], alloy_padded[1:-1, 2:]), (order_parameter_padded[1:-1, :-2], alloy_padded[1:-1, :-2]), (shift_last(order_parameter, 1), shift_last(alloy_concentration, 1)), (shift_last(order_parameter, -1), shift_last(alloy_concentration, -1))]
    accumulated_pieces = jnp.zeros_like(alloy_concentration)
    for near_phase, near_solute in neighbours:
        accumulated_pieces = accumulated_pieces + 0.5 * (mobile + DSOL + 0.5 * DLIQ * (1.0 - near_phase)) * (near_solute - alloy_concentration)
    return accumulated_pieces

def march_forward(order_parameter_padded, alloy_padded, transport_third, transport_first, transport_second, blending_factor, supercool_refined):
    order_parameter = order_parameter_padded[1:-1, 1:-1]
    alloy_concentration = alloy_padded[1:-1, 1:-1]
    distribute_values = divergence(transport_third, transport_first, transport_second)
    driving_force = distribute_values + order_parameter - order_parameter ** 3 - COUPLING_FACTOR * (alloy_concentration + supercool_refined) * (1.0 - order_parameter * order_parameter) ** 2
    order_parameter_next = order_parameter + DT * driving_force / blending_factor
    alloy_next = alloy_concentration + DT * diffuse(order_parameter_padded, alloy_padded) + 0.5 * (1.0 + (1.0 - KPART) * alloy_concentration) * (order_parameter_next - order_parameter)
    return (order_parameter_next, alloy_next)

def interior_refresh(padded_region, cosine_widened, sine_widened, supercool_refined, interior_region):
    transport_rates, blending_factor = flux_of(padded_region[0], cosine_widened, sine_widened)
    transport_third = transport_rates[0] * interior_region
    transport_first = transport_rates[1] * interior_region
    adjacent_values = padded_region[:, 1:-1, 1:-1]
    return march_forward(adjacent_values[0], adjacent_values[1], transport_third, transport_first, transport_rates[2][1:-1, 1:-1], blending_factor[1:-1, 1:-1], supercool_refined)

def diffusive_contribution(temp_p, extra_p):
    inner = (slice(1, -1), slice(1, -1), slice(1, -1))
    centre_t = temp_p[inner]
    centre_k = extra_p[inner]
    accumulated_pieces = jnp.zeros_like(centre_t)
    for direction in range(3):
        for offset in (0, 2):
            window = [slice(1, -1), slice(1, -1), slice(1, -1)]
            window[direction] = slice(offset, offset + centre_t.shape[direction])
            window = tuple(window)
            accumulated_pieces = accumulated_pieces + (KLIQ + 0.5 * (centre_k + extra_p[window])) * (temp_p[window] - centre_t)
    return accumulated_pieces

def sine_basis(points):
    ordinal = jnp.arange(points, dtype=jnp.float32) + 1.0
    angles = jnp.pi * ordinal[:, None] * ordinal[None, :] / (points + 1.0)
    basis = jnp.sqrt(2.0 / (points + 1.0)) * jnp.sin(angles)
    levels = 2.0 - 2.0 * jnp.cos(jnp.pi * ordinal / (points + 1.0))
    return (basis, levels)

def transform(values, basis_z, basis_x, basis_y):
    values = jnp.einsum('ab,bxy->axy', basis_z, values, precision=HIGHEST)
    values = jnp.einsum('ab,zby->zay', basis_x, values, precision=HIGHEST)
    return jnp.einsum('zxb,ab->zxa', values, basis_y, precision=HIGHEST)

def fdm_solve(right_side):
    basis_z, level_z = sine_basis(right_side.shape[0])
    basis_x, level_x = sine_basis(right_side.shape[1])
    basis_y, level_y = sine_basis(right_side.shape[2])
    divisor = SIGMA + KBAR * (level_z[:, None, None] + level_x[None, :, None] + level_y[None, None, :])
    spectral = transform(right_side, basis_z, basis_x, basis_y) / divisor
    return transform(spectral, basis_z, basis_x, basis_y)

def reference(order_and_alloy_stack, crystal_identifier, frozen_indicator, supercool_grid, crystal_rotation_radians):
    cos_c, sin_c = orient(crystal_identifier, crystal_rotation_radians)
    coarse_rim = ((1, 1), (1, 1), (0, 0))
    cos_p = jnp.pad(cos_c, coarse_rim)
    sin_p = jnp.pad(sin_c, coarse_rim)
    state_p = jnp.pad(order_and_alloy_stack, ((0, 0), (2, 2), (2, 2), (0, 0)))
    starting_bin = jnp.int32(0)

    def fine_block(block_at):
        first_col = block_at * BX
        padded_region = lax.dynamic_slice(state_p, (starting_bin, starting_bin, first_col, starting_bin), (2, NZ + 4, BX + 4, NY))
        vertical_index_table = block_at * KERNEL_BINS_WIDE
        cos_blk = lax.dynamic_slice(cos_p, (starting_bin, vertical_index_table, starting_bin), (ROUGH_SHEETS_UP + 2, KERNEL_BINS_WIDE + 2, ROUGH_BINS_DEPTH))
        sin_blk = lax.dynamic_slice(sin_p, (starting_bin, vertical_index_table, starting_bin), (ROUGH_SHEETS_UP + 2, KERNEL_BINS_WIDE + 2, ROUGH_BINS_DEPTH))
        supercool_piece = lax.dynamic_slice(supercool_grid, (starting_bin, vertical_index_table, starting_bin), (ROUGH_SHEETS_UP, KERNEL_BINS_WIDE, ROUGH_BINS_DEPTH))
        cosine_widened = refine_onto_grid(cos_blk)[COARSEN - 1:COARSEN + 1 + NZ, COARSEN - 1:COARSEN + 1 + BX]
        sine_widened = refine_onto_grid(sin_blk)[COARSEN - 1:COARSEN + 1 + NZ, COARSEN - 1:COARSEN + 1 + BX]
        plane_pos = jnp.arange(NZ + 2, dtype=jnp.int32) - 1
        column_pos = jnp.arange(BX + 2, dtype=jnp.int32) + first_col - 1
        in_grid = ((plane_pos >= 0) & (plane_pos < NZ))[:, None] & ((column_pos >= 0) & (column_pos < NX))[None, :]
        interior_region = jnp.where(in_grid, 1.0, 0.0).astype(jnp.float32)[:, :, None]
        order_parameter_next, alloy_next = interior_refresh(padded_region, cosine_widened, sine_widened, refine_onto_grid(supercool_piece), interior_region)
        return (jnp.stack([order_parameter_next, alloy_next]), restrict(order_parameter_next - padded_region[0, 2:-2, 2:-2]))
    blocks, sources = lax.map(fine_block, jnp.arange(N_WIDE, dtype=jnp.int32))
    state_new = jnp.transpose(blocks, (1, 2, 0, 3, 4)).reshape(2, NZ, NX, NY)
    latent_release = jnp.transpose(sources, (1, 0, 2, 3)).reshape(ROUGH_SHEETS_UP, ROUGH_BINS_WIDTH, ROUGH_BINS_DEPTH)
    diffusive_fringe = (KSOL - KLIQ) * frozen_indicator.astype(jnp.float32)
    energy_imbalance = latent_release + diffusive_contribution(jnp.pad(supercool_grid, 1), jnp.pad(diffusive_fringe, 1))
    resid_p = jnp.pad(energy_imbalance, ((0, 0), (FRINGE_BINS, FRINGE_BINS), (0, 0)))

    def add_part(block_at, accumulated_pieces):
        vertical_index_table = block_at.astype(jnp.int32) * KERNEL_BINS_WIDE
        subdomain = lax.dynamic_slice(resid_p, (starting_bin, vertical_index_table, starting_bin), (ROUGH_SHEETS_UP, SUBX, ROUGH_BINS_DEPTH))
        current = lax.dynamic_slice(accumulated_pieces, (starting_bin, vertical_index_table, starting_bin), (ROUGH_SHEETS_UP, SUBX, ROUGH_BINS_DEPTH))
        return lax.dynamic_update_slice(accumulated_pieces, current + fdm_solve(subdomain), (starting_bin, vertical_index_table, starting_bin))
    accumulated_pieces = lax.fori_loop(0, N_WIDE, add_part, jnp.zeros((ROUGH_SHEETS_UP, ROUGH_BINS_WIDTH + 2 * FRINGE_BINS, ROUGH_BINS_DEPTH), jnp.float32))
    adjusted_supercool = supercool_grid + accumulated_pieces[:, FRINGE_BINS:FRINGE_BINS + ROUGH_BINS_WIDTH]
    return (state_new, adjusted_supercool)
```

```python
import functools

import jax
import jax.numpy as jnp
import numpy as np
from jax import lax
from jax.experimental import pallas as pl
from jax.experimental.pallas import tpu as pltpu
from jax.sharding import PartitionSpec as P

F32 = jnp.float32
HI = lax.Precision.HIGHEST
NNAR, NWIDE = 8, 32
NPL, BX, NY = 4, 64, 512
CX, CY = 16, 128
SUBX = 24
SIGMA, KBAR = 0.05, 0.75
DT = 0.15
VMEM = pl.BlockSpec(memory_space=pltpu.VMEM)
HBM = pl.BlockSpec(memory_space=pl.ANY)


def sds(*shape):
    return jax.ShapeDtypeStruct(shape, F32)


def params():
    return pltpu.CompilerParams(vmem_limit_bytes=32 * 1024 * 1024)


def sine(points):
    k = np.arange(1, points + 1)
    return np.sqrt(2.0 / (points + 1)) * np.sin(np.pi * np.outer(k, k) / (points + 1))


def level(points):
    return 2.0 - 2.0 * np.cos(np.pi * np.arange(1, points + 1) / (points + 1))


SZ, SY = sine(8), sine(CY)
SPREAD_Y = np.kron(np.eye(CY), np.ones((1, 4)))
SUM_X = np.kron(np.eye(CX), np.ones((1, 4)))
MEAN_Y = SPREAD_Y.T @ SY / 64.0
SZ_ROWS = np.repeat(SZ[:, :, None], CY, 2)


def elimination():
    diag = SIGMA + KBAR * (level(8)[:, None] + level(CY)[None, :] + 2.0)
    inv = [1.0 / diag]
    for _ in range(SUBX - 1):
        inv.append(1.0 / (diag - KBAR * KBAR * inv[-1]))
    return np.stack(inv)


INVERSE = elimination()


def wide_ring(k):
    return [(i, (i + k) % NWIDE) for i in range(NWIDE)]


PAIR_A = [(i, i ^ 1) for i in range(NNAR)]
PAIR_B = [(i, (((i + 1) ^ 1) - 1) % NNAR) for i in range(NNAR)]
CORES = [(i, i ^ 1) for i in range(NWIDE)]


def lanes(v):
    return lax.broadcasted_iota(jnp.int32, v.shape, v.ndim - 1)


def rows_of(v):
    return lax.broadcasted_iota(jnp.int32, v.shape, v.ndim - 2)


def y_up(v):
    n = v.shape[-1]
    return jnp.where(lanes(v) == n - 1, 0.0, pltpu.roll(v, n - 1, v.ndim - 1))


def y_down(v):
    return jnp.where(lanes(v) == 0, 0.0, pltpu.roll(v, 1, v.ndim - 1))


def x_up(v, after):
    return pltpu.roll(jnp.where(rows_of(v) == 0, after, v), 7, v.ndim - 2)


def x_down(v, before):
    return pltpu.roll(jnp.where(rows_of(v) == 7, before, v), 1, v.ndim - 2)


def inverse(v):
    guess = pl.reciprocal(v, approx=True)
    guess = guess * (2.0 - v * guess)
    return guess * (2.0 - v * guess)


def weigh(gz, gx, gy, c2, s2):
    q0, a, b = gz * gz, gx * gx, gy * gy
    r = a + b
    uv = s2 * (b - a) + c2 * (gx * gy)
    num = q0 * q0 + r * r - 2.0 * (uv * uv)
    over = inverse(q0 + r + 1.0)
    return 0.55 + 0.6 * (num * (over * over))


def flag(cond):
    return jnp.where(cond, 1.0, 0.0).astype(F32)


def dot(a, b):
    return jnp.dot(a, b, precision=HI, preferred_element_type=F32)


def pack_kernel(state, ids, frozen, temp, angles, za, zb, xr, xl, coarse):
    n = lax.axis_index("narrow")
    even = lax.rem(n, 2) == 0
    for ref, top in ((za, even), (zb, jnp.logical_not(even))):
        first = jnp.where(top, 2, 0)
        last = jnp.where(top, 3, 0)
        ref[0:2] = state[0, pl.ds(first, 2)]
        ref[2] = state[1, last]
    table = jnp.broadcast_to(angles[...], (CX, CY))
    cos_t, sin_t = jnp.cos(table), jnp.sin(table)
    ident = ids[0]
    c = jnp.take_along_axis(cos_t, ident, axis=1)
    s = jnp.take_along_axis(sin_t, ident, axis=1)
    coarse[0] = c * c - s * s
    coarse[1] = c * s
    coarse[2] = temp[0]
    coarse[3] = -0.5 * frozen[0].astype(F32)
    for ref, edge, inner, cell in ((xr, BX - 1, BX - 2, CX - 1), (xl, 0, 1, 0)):
        for z in range(NPL):
            ref[z : z + 1] = state[0, z, edge : edge + 1]
            ref[4 + z : 5 + z] = state[0, z, inner : inner + 1]
            ref[8 + z : 9 + z] = state[1, z, edge : edge + 1]
        for k in range(4):
            ref[12:13, k * CY : (k + 1) * CY] = coarse[k, cell : cell + 1]
        ref[13:16] = jnp.zeros((3, NY), F32)


def corner_kernel(coarse, left, right, ca, cb):
    n = lax.axis_index("narrow")
    even = lax.rem(n, 2) == 0
    for ref, top in ((ca, even), (cb, jnp.logical_not(even))):
        pick = jnp.where(top, 1.0, 0.0).astype(F32)
        for row, side in ((0, left), (1, right)):
            ref[row : row + 1] = jnp.where(pick > 0.5, side[3:4], side[0:1])
        ref[2:8] = jnp.zeros((6, NY), F32)
        for k in range(4):
            ref[8:24, k * CY : (k + 1) * CY] = coarse[k]


def widen(ref, at, rough):
    for k in range(CX):
        ref[at, 4 * k : 4 * k + 4] = jnp.broadcast_to(rough[k : k + 1], (4, NY))


def prepare_kernel(state, coarse, left, right, spread_y, own, fine, rims):
    w = lax.axis_index("wide")
    has_left, has_right = flag(w > 0), flag(w < NWIDE - 1)
    for z in range(NPL):
        own[z, 8 : 8 + BX] = state[0, z]
        own[z, 7:8] = left[z : z + 1] * has_left
        own[z, 8 + BX : 9 + BX] = right[z : z + 1] * has_right
    for k in range(3):
        widen(fine, k, dot(coarse[k], spread_y[...]))
    rows = [side[12:13, k * CY : (k + 1) * CY] for side in (left, right) for k in (0, 1)]
    rims[...] = dot(jnp.concatenate(rows + rows, 0), spread_y[...])


def edge_kernel(coarse, left, right, ca, cb, spread_y, sy, sides, base):
    n, w = lax.axis_index("narrow"), lax.axis_index("wide")
    even = lax.rem(n, 2) == 0
    has_left, has_right = flag(w > 0), flag(w < NWIDE - 1)
    has_low, has_high = flag(n > 0), flag(n < NNAR - 1)
    low = jnp.where(even, cb[8:24], ca[8:24])
    high = jnp.where(even, ca[8:24], cb[8:24])
    for at, message in ((0, low), (2, high)):
        for k in range(2):
            widen(sides, at + k, dot(message[:, k * CY : (k + 1) * CY], spread_y[...]))
    t, e = coarse[2], coarse[3]
    near = []
    for message, there in ((low, has_low), (high, has_high)):
        near.append((message[:, 2 * CY : 3 * CY] * there, message[:, 3 * CY :] * there))
    row = rows_of(t)
    down, up = [], []
    for k, own in ((2, t), (3, e)):
        before = left[12:13, k * CY : (k + 1) * CY] * has_left
        after = right[12:13, k * CY : (k + 1) * CY] * has_right
        down.append(jnp.where(row == 0, before, pltpu.roll(own, 1, 0)))
        up.append(jnp.where(row == CX - 1, after, pltpu.roll(own, CX - 1, 0)))
    near += [tuple(down), tuple(up), (y_up(t), y_up(e)), (y_down(t), y_down(e))]
    total = jnp.zeros_like(t)
    for tn, en in near:
        total = total + (1.0 + 0.5 * (e + en)) * (tn - t)
    base[...] = dot(total, sy[...])


def phase_kernel(
    state, own, fine, rims, sides, left, right, za, zb, ca, cb, base, sum_x, mean_y,
    fresh, spectral,
    halo, fx, fz, known, scale, change,
):
    n, w = lax.axis_index("narrow"), lax.axis_index("wide")
    even = lax.rem(n, 2) == 0
    has_left, has_right = flag(w > 0), flag(w < NWIDE - 1)
    has_low, has_high = flag(n > 0), flag(n < NNAR - 1)
    for message, corner, at, there in (
        (za, ca, jnp.where(even, 2, 0), jnp.where(even, has_high, has_low)),
        (zb, cb, jnp.where(even, 0, 2), jnp.where(even, has_low, has_high)),
    ):
        for k in range(2):
            halo[at + k, 8 : 8 + BX] = message[k] * there
            halo[at + k, 7:8] = corner[0:1] * (there * has_left)
            halo[at + k, 8 + BX : 9 + BX] = corner[1:2] * (there * has_right)
    planes = [(halo, 0), (halo, 1), (own, 0), (own, 1), (own, 2), (own, 3), (halo, 2), (halo, 3)]

    def get(k, rows):
        ref, z = planes[k]
        return ref[z, rows]

    def fluxes(c, carry):
        r0 = pl.multiple_of(c * 8, 8)
        here, at, after = pl.ds(r0, 8), pl.ds(r0 + 8, 8), pl.ds(r0 + 16, 8)
        for zz in range(6):
            v = get(zz + 1, at)
            gz = 0.5 * (get(zz + 2, at) - get(zz, at))
            gx = 0.5 * (x_up(v, get(zz + 1, after)) - x_down(v, get(zz + 1, here)))
            gy = 0.5 * (y_up(v) - y_down(v))
            if zz in (0, 5):
                k = 0 if zz == 0 else 2
                an = weigh(gz, gx, gy, sides[k, here], sides[k + 1, here])
                fz[zz, here] = (has_low if zz == 0 else has_high) * (an * an * gz)
                continue
            an = weigh(gz, gx, gy, fine[0, here], fine[1, here])
            wt = an * an
            fz[zz, here] = wt * gz
            fx[zz - 1, at] = wt * gx
            fy = wt * gy
            m = 1.0 - v * v
            drive = m * (v - 1.5 * (state[1, zz - 1, here] + fine[2, here]) * m)
            known[zz - 1, here] = 0.5 * (y_up(fy) - y_down(fy)) + drive
            scale[zz - 1, here] = DT * inverse(wt)
        return carry

    lax.fori_loop(0, BX // 8, fluxes, 0)

    def column(pick):
        return jnp.concatenate([pick(z, s) for s in (0, 1) for z in range(NPL)], 0)

    rim = (slice(7, 8), slice(8 + BX, 9 + BX))
    centre = column(lambda z, s: get(z + 2, rim[s]))
    below = column(lambda z, s: get(z + 1, rim[s]))
    above = column(lambda z, s: get(z + 3, rim[s]))
    x_hi = column(lambda z, s: right[4 + z : 5 + z] if s else own[z, 8:9])
    x_lo = column(lambda z, s: own[z, 7 + BX : 8 + BX] if s else left[4 + z : 5 + z])
    first = rows_of(centre) < NPL
    c2 = jnp.where(first, rims[0:1], rims[2:3])
    s2 = jnp.where(first, rims[1:2], rims[3:4])
    gx = 0.5 * (x_hi - x_lo)
    an = weigh(0.5 * (above - below), gx, 0.5 * (y_up(centre) - y_down(centre)), c2, s2)
    rim_flux = jnp.where(first, has_left, has_right) * (an * an * gx)
    for z in range(NPL):
        fx[z, 7:8] = rim_flux[z : z + 1]
        fx[z, 8 + BX : 9 + BX] = rim_flux[NPL + z : NPL + z + 1]

    def step(c, carry):
        r0 = pl.multiple_of(c * 8, 8)
        here, at, after = pl.ds(r0, 8), pl.ds(r0 + 8, 8), pl.ds(r0 + 16, 8)
        total = jnp.zeros((8, NY), F32)
        for z in range(NPL):
            p, f = own[z, at], fx[z, at]
            spread = (
                known[z, here]
                + 0.5 * (fz[z + 2, here] - fz[z, here])
                + 0.5 * (x_up(f, fx[z, after]) - x_down(f, fx[z, here]))
            )
            rise = scale[z, here] * spread
            fresh[z, here] = p + rise
            total = total + rise
        change[here] = total
        return carry

    lax.fori_loop(0, BX // 8, step, 0)
    spectral[...] = base[...] + dot(dot(sum_x[...], change[...]), mean_y[...])


def solute_kernel(state, own, left, right, za, zb, fresh, out, sown):
    n, w = lax.axis_index("narrow"), lax.axis_index("wide")
    even = lax.rem(n, 2) == 0
    has_left, has_right = flag(w > 0), flag(w < NWIDE - 1)
    has_low, has_high = flag(n > 0), flag(n < NNAR - 1)
    for z in range(NPL):
        sown[z, 8 : 8 + BX] = state[1, z]
        sown[z, 7:8] = left[8 + z : 9 + z] * has_left
        sown[z, 8 + BX : 9 + BX] = right[8 + z : 9 + z] * has_right

    def step(c, carry):
        r0 = pl.multiple_of(c * 8, 8)
        here, at, after = pl.ds(r0, 8), pl.ds(r0 + 8, 8), pl.ds(r0 + 16, 8)

        def outer(k_low, k_high, high):
            if high:
                return has_high * jnp.where(even, za[k_high, here], zb[k_high, here])
            return has_low * jnp.where(even, zb[k_low, here], za[k_low, here])

        ps = [outer(1, 0, False)] + [own[z, at] for z in range(NPL)] + [outer(1, 0, True)]
        ss = [outer(2, 2, False)] + [sown[z, at] for z in range(NPL)] + [outer(2, 2, True)]
        for z in range(NPL):
            p, s = ps[z + 1], ss[z + 1]
            q = 0.55 - 0.25 * p
            near = [
                (ps[z], ss[z]),
                (ps[z + 2], ss[z + 2]),
                (x_up(p, own[z, after]), x_up(s, sown[z, after])),
                (x_down(p, own[z, here]), x_down(s, sown[z, here])),
                (y_up(p), y_up(s)),
                (y_down(p), y_down(s)),
            ]
            total = jnp.zeros_like(p)
            for pn, sn in near:
                total = total + (q - 0.25 * pn) * (sn - s)
            grown = fresh[z, here]
            out[0, z, here] = grown
            out[1, z, here] = s + DT * total + (0.5 + 0.425 * s) * (grown - p)
        return carry

    lax.fori_loop(0, BX // 8, step, 0)


def window_kernel(before, here, after, out):
    w = lax.axis_index("wide")
    core, chip = lax.rem(w, 2), lax.div(w, 2)
    has_before, has_after = flag(chip > 0), flag(chip < NWIDE // 2 - 1)

    def put(first):
        view = [
            before[first:32] * has_before,
            here[...],
            after[0 : first - 8] * has_after,
        ]
        for m in range(NNAR):
            at = 0
            for part in view:
                out[m, at : at + part.shape[0]] = part
                at += part.shape[0]

    @pl.when(core == 0)
    def _():
        put(12)

    @pl.when(core == 1)
    def _():
        put(28)


def solve_kernel(planes, temp, inv, sz_rows, sy, out, modes, rows):
    n, w = lax.axis_index("narrow"), lax.axis_index("wide")
    has_left, has_right = flag(w > 0), flag(w < NWIDE - 1)
    values = [planes[m] for m in range(NNAR)]
    for k in range(NNAR):
        total = float(SZ[k, 0]) * values[0]
        for m in range(1, NNAR):
            total = total + float(SZ[k, m]) * values[m]
        modes[k * 56 : (k + 1) * 56] = total
    f = [modes[pl.ds(j, 8, stride=56), :] for j in range(56)]
    inv_of = [inv[i] for i in range(SUBX)]
    link = [KBAR * v for v in inv_of]

    def solve(order, keep):
        h = [inv_of[0] * f[order[0]]]
        for i in range(1, SUBX):
            h.append(inv_of[i] * f[order[i]] + link[i] * h[-1])
        x = h[-1]
        found = {order[-1]: x}
        for i in range(SUBX - 2, -1, -1):
            if order[i] not in keep:
                break
            x = h[i] + link[i] * x
            found[order[i]] = x
        return found

    mine = solve(list(range(16, 40)), set(range(20, 40)))
    lower = solve(list(range(0, 24)), set(range(20, 24)))
    upper = solve(list(range(55, 31, -1)), set(range(32, 36)))
    weight = sz_rows[n]
    for j in range(CX):
        x = mine[20 + j]
        if 20 + j in lower:
            x = x + has_left * lower[20 + j]
        if 20 + j in upper:
            x = x + has_right * upper[20 + j]
        rows[j : j + 1] = jnp.sum(x * weight, axis=0, keepdims=True)
    out[0] = temp[0] + dot(rows[...], sy[...])


def kernel(body, outs, scratch=(), cost=0):
    many = isinstance(outs, (list, tuple))

    def call(*args):
        return pl.pallas_call(
            body,
            out_shape=outs,
            in_specs=[VMEM] * len(args),
            out_specs=[VMEM] * len(outs) if many else VMEM,
            scratch_shapes=list(scratch),
            compiler_params=params(),
            cost_estimate=pl.CostEstimate(flops=cost, bytes_accessed=0, transcendentals=0),
            name=body.__name__,
        )(*args)

    return call


def on_device(state, ids, frozen, temp, angles):
    spread_y = jnp.asarray(SPREAD_Y, F32)
    sy = jnp.asarray(SY, F32)
    table = jnp.pad(angles, (0, CY - angles.shape[0])).reshape(1, CY)
    send_a, send_b, to_right, to_left, coarse = kernel(
        pack_kernel, [sds(3, BX, NY)] * 2 + [sds(16, NY)] * 2 + [sds(4, CX, CY)]
    )(state, ids, frozen, temp, table)
    za = lax.ppermute(send_a, "narrow", PAIR_A)
    zb = lax.ppermute(send_b, "narrow", PAIR_B)
    left = lax.ppermute(to_right, "wide", wide_ring(1))
    right = lax.ppermute(to_left, "wide", wide_ring(-1))
    corner_a, corner_b = kernel(corner_kernel, [sds(24, NY)] * 2)(coarse, left, right)
    ca = lax.ppermute(corner_a, "narrow", PAIR_A)
    cb = lax.ppermute(corner_b, "narrow", PAIR_B)
    own, fine, rims = kernel(
        prepare_kernel, [sds(NPL, BX + 16, NY), sds(3, BX, NY), sds(8, NY)]
    )(state, coarse, left, right, spread_y)
    sides, base = kernel(edge_kernel, [sds(4, BX, NY), sds(CX, CY)])(
        coarse, left, right, ca, cb, spread_y, sy
    )
    fresh, spectral = kernel(
        phase_kernel,
        [sds(NPL, BX, NY), sds(CX, CY)],
        [
            pltpu.VMEM((4, BX + 16, NY), F32),
            pltpu.VMEM((NPL, BX + 16, NY), F32),
            pltpu.VMEM((6, BX, NY), F32),
            pltpu.VMEM((NPL, BX, NY), F32),
            pltpu.VMEM((NPL, BX, NY), F32),
            pltpu.VMEM((BX, NY), F32),
        ],
    )(
        state, own, fine, rims, sides, left, right, za, zb, ca, cb, base,
        jnp.asarray(SUM_X, F32), jnp.asarray(MEAN_Y, F32),
    )
    partner = lax.ppermute(spectral, "wide", CORES)
    core = lax.rem(lax.axis_index("wide"), 2)
    here = jnp.where(
        core == 0,
        jnp.concatenate([spectral, partner], 0),
        jnp.concatenate([partner, spectral], 0),
    )
    before = lax.ppermute(here, "wide", wide_ring(2))
    after = lax.ppermute(here, "wide", wide_ring(-2))
    state_new = kernel(
        solute_kernel, sds(2, NPL, BX, NY), [pltpu.VMEM((NPL, BX + 16, NY), F32)]
    )(state, own, left, right, za, zb, fresh)
    windows = kernel(window_kernel, sds(NNAR, 56, CY))(before, here, after)
    planes = lax.all_to_all(windows, "narrow", 0, 0)
    adjusted = kernel(
        solve_kernel,
        sds(1, CX, CY),
        [pltpu.VMEM((NNAR * 56, CY), F32), pltpu.VMEM((CX, CY), F32)],
    )(planes, temp, jnp.asarray(INVERSE, F32), jnp.asarray(SZ_ROWS, F32), sy)
    return state_new, adjusted


def solution(mesh):
    return jax.shard_map(
        on_device,
        mesh=mesh,
        in_specs=(
            P(None, "narrow", "wide", None),
            P("narrow", "wide", None),
            P("narrow", "wide", None),
            P("narrow", "wide", None),
            P(),
        ),
        out_specs=(P(None, "narrow", "wide", None), P("narrow", "wide", None)),
        check_vma=False,
    )
```

```python
import functools

import jax
import jax.numpy as jnp
import numpy as np
from jax import lax
from jax.experimental import pallas as pl
from jax.experimental.pallas import tpu as pltpu
from jax.sharding import PartitionSpec as P

F32 = jnp.float32
HI = lax.Precision.HIGHEST
NNAR, NWIDE = 8, 32
NPL, BX, NY = 4, 64, 512
CORNERS, ROUGH, FACE = 128, 136, 152
CX, CY = 16, 128
SUBX = 24
SIGMA, KBAR = 0.05, 0.75
DT = 0.15
VMEM = pl.BlockSpec(memory_space=pltpu.VMEM)
HBM = pl.BlockSpec(memory_space=pltpu.HBM)


def sds(*shape):
    return jax.ShapeDtypeStruct(shape, F32)


def params(mib):
    return pltpu.CompilerParams(vmem_limit_bytes=mib * 1024 * 1024)


def sine(points):
    k = np.arange(1, points + 1)
    return np.sqrt(2.0 / (points + 1)) * np.sin(np.pi * np.outer(k, k) / (points + 1))


def level(points):
    return 2.0 - 2.0 * np.cos(np.pi * np.arange(1, points + 1) / (points + 1))


SZ, SY = sine(8), sine(CY)
SPREAD_Y = np.kron(np.eye(CY), np.ones((1, 4)))
SUM_X = np.kron(np.eye(CX), np.ones((1, 4)))
MEAN_Y = SPREAD_Y.T @ SY / 64.0
SZ_ROWS = np.repeat(SZ[:, :, None], CY, 2)


def elimination():
    diag = SIGMA + KBAR * (level(8)[:, None] + level(CY)[None, :] + 2.0)
    inv = [1.0 / diag]
    for _ in range(SUBX - 1):
        inv.append(1.0 / (diag - KBAR * KBAR * inv[-1]))
    return np.stack(inv)


INVERSE = elimination()


CONSTS = np.concatenate([SY, MEAN_Y, INVERSE.reshape(-1, CY), SZ_ROWS.reshape(-1, CY)]).astype(np.float32)
SY_AT, MEAN_AT, INV_AT, SZ_AT = slice(0, 128), slice(128, 640), 640, 640 + 8 * SUBX


def wide_ring(k):
    return [(i, (i + k) % NWIDE) for i in range(NWIDE)]


PAIR_A = [(i, i ^ 1) for i in range(NNAR)]
PAIR_B = [(i, (((i + 1) ^ 1) - 1) % NNAR) for i in range(NNAR)]
CORES = [(i, i ^ 1) for i in range(NWIDE)]
CHIPS = [(i, (((i + 1) ^ 1) - 1) % NWIDE) for i in range(NWIDE)]
NEXT_CHIPS = [(i, (i + (2 if i % 2 else -2)) % NWIDE) for i in range(NWIDE)]


def lanes(v):
    return lax.broadcasted_iota(jnp.int32, v.shape, v.ndim - 1)


def rows_of(v):
    return lax.broadcasted_iota(jnp.int32, v.shape, v.ndim - 2)


def y_up(v):
    n = v.shape[-1]
    return jnp.where(lanes(v) == n - 1, 0.0, pltpu.roll(v, n - 1, v.ndim - 1))


def y_down(v):
    return jnp.where(lanes(v) == 0, 0.0, pltpu.roll(v, 1, v.ndim - 1))


def x_up(v, after):
    return pltpu.roll(jnp.where(rows_of(v) == 0, after, v), 7, v.ndim - 2)


def x_down(v, before):
    return pltpu.roll(jnp.where(rows_of(v) == 7, before, v), 1, v.ndim - 2)


def inverse(v):
    guess = pl.reciprocal(v, approx=True)
    guess = guess * (2.0 - v * guess)
    return guess * (2.0 - v * guess)


def weigh(gz, gx, gy, c2, s2):
    q0, a, b = gz * gz, gx * gx, gy * gy
    r = a + b
    uv = s2 * (b - a) + c2 * (gx * gy)
    num = q0 * q0 + r * r - 2.0 * (uv * uv)
    over = inverse(q0 + r + 1.0)
    return 0.55 + 0.6 * (num * (over * over))


def flag(cond):
    return jnp.where(cond, 1.0, 0.0).astype(F32)


def spread_lanes():
    lane = lax.broadcasted_iota(jnp.int32, (CY, NY), 1)
    row = lax.broadcasted_iota(jnp.int32, (CY, NY), 0)
    return flag(lax.shift_right_logical(lane, 2) == row)


def sum_rows():
    lane = lax.broadcasted_iota(jnp.int32, (CX, BX), 1)
    row = lax.broadcasted_iota(jnp.int32, (CX, BX), 0)
    return flag(lax.shift_right_logical(lane, 2) == row)


def dot(a, b):
    return jnp.dot(a, b, precision=HI, preferred_element_type=F32)


def stage_kernel(
    state_in, ids_in, frozen_in, temp_in, angles_in,
    x_chip, x_core, state, coarse,
    ids, frozen, temp, angles, sems,
):
    copies = [
        pltpu.make_async_copy(src, dst, sems.at[i])
        for i, (src, dst) in enumerate(
            [
                (state_in.at[0], state.at[0]),
                (state_in.at[1], state.at[1]),
                (ids_in, ids),
                (frozen_in, frozen),
                (temp_in, temp),
                (angles_in, angles),
            ]
        )
    ]
    for copy in copies:
        copy.start()
    for copy in copies[2:]:
        copy.wait()
    table = jnp.concatenate([angles[...], angles[...]], 1)
    c = jnp.take_along_axis(jnp.broadcast_to(jnp.cos(table), (CX, CY)), ids[0], axis=1)
    s = jnp.take_along_axis(jnp.broadcast_to(jnp.sin(table), (CX, CY)), ids[0], axis=1)
    coarse[0] = c * c - s * s
    coarse[1] = c * s
    coarse[2] = temp[0]
    coarse[3] = -0.5 * frozen[0].astype(F32)
    for copy in copies[:2]:
        copy.wait()
    core0 = lax.rem(lax.axis_index("wide"), 2) == 0
    for ref, low in ((x_chip, core0), (x_core, jnp.logical_not(core0))):
        for z in range(NPL):
            for at, ch, first, last in ((0, 0, 0, BX - 1), (4, 0, 1, BX - 2), (8, 1, 0, BX - 1)):
                ref[at + z : at + z + 1] = jnp.where(
                    low, state[ch, z, first : first + 1], state[ch, z, last : last + 1]
                )
        for k in range(4):
            ref[12:13, k * CY : (k + 1) * CY] = jnp.where(
                low, coarse[k, 0:1], coarse[k, CX - 1 : CX]
            )
        ref[13:16] = jnp.zeros((3, NY), F32)


def x_sides(x_chip, x_core, rows):
    w = lax.axis_index("wide")
    core0 = lax.rem(w, 2) == 0
    left = jnp.where(core0, x_chip[rows], x_core[rows]) * flag(w > 0)
    right = jnp.where(core0, x_core[rows], x_chip[rows]) * flag(w < NWIDE - 1)
    return left, right


def face_kernel(state, coarse, x_chip, x_core, face_b, face_a):
    n = lax.axis_index("narrow")
    even = lax.rem(n, 2) == 0
    left, right = x_sides(x_chip, x_core, slice(0, 8))
    for ref, top in ((face_b, jnp.logical_not(even)), (face_a, even)):
        first = jnp.where(top, 2, 0)
        ref[0:BX] = state[0, first]
        ref[BX : 2 * BX] = state[0, first + 1]
        ref[CORNERS : CORNERS + 1] = jnp.where(top, left[3:4], left[0:1])
        ref[CORNERS + 1 : CORNERS + 2] = jnp.where(top, right[3:4], right[0:1])
        ref[CORNERS + 2 : CORNERS + 8] = jnp.zeros((6, NY), F32)
        for k in range(4):
            ref[ROUGH : ROUGH + CX, k * CY : (k + 1) * CY] = coarse[k]


def late_kernel(state, base, late_b, late_a):
    even = lax.rem(lax.axis_index("narrow"), 2) == 0
    for ref, top in ((late_b, jnp.logical_not(even)), (late_a, even)):
        ref[...] = state[1, jnp.where(top, 3, 0)]


def widen(ref, at, rough):
    for k in range(CX):
        ref[at, 4 * k : 4 * k + 4] = jnp.broadcast_to(rough[k : k + 1], (4, NY))


def spread_kernel(coarse, consts_in, fine, consts, sem):
    fetch = pltpu.make_async_copy(consts_in, consts, sem)
    fetch.start()
    spread_y = spread_lanes()
    for k in range(3):
        widen(fine, k, dot(coarse[k], spread_y))
    fetch.wait()


def prepare_kernel(
    state, coarse, fine, x_chip, x_core,
    own, rims, fx, fz, known, scale, gxy, base,
):
    left, right = x_sides(x_chip, x_core, slice(0, 4))
    for z in range(NPL):
        own[z, 8 : 8 + BX] = state[0, z]
        own[z, 7:8] = left[z : z + 1]
        own[z, 8 + BX : 9 + BX] = right[z : z + 1]
    left, right = x_sides(x_chip, x_core, slice(12, 13))
    rows = [side[:, k * CY : (k + 1) * CY] for side in (left, right) for k in (0, 1)]
    rims[...] = dot(jnp.concatenate(rows + rows, 0), spread_lanes())

    def chunk(c, carry):
        r0 = pl.multiple_of(c * 8, 8)
        here, at, after = pl.ds(r0, 8), pl.ds(r0 + 8, 8), pl.ds(r0 + 16, 8)
        for z in range(NPL):
            v = own[z, at]
            gx = 0.5 * (x_up(v, own[z, after]) - x_down(v, own[z, here]))
            gy = 0.5 * (y_up(v) - y_down(v))
            m = 1.0 - v * v
            drive = m * (v - 1.5 * (state[1, z, here] + fine[2, here]) * m)
            if z in (0, NPL - 1):
                known[z, here] = drive
                gxy[z // 2, 0, here] = gx
                gxy[z // 2, 1, here] = gy
                continue
            gz = 0.5 * (own[z + 1, at] - own[z - 1, at])
            an = weigh(gz, gx, gy, fine[0, here], fine[1, here])
            wt = an * an
            fz[z - 1, here] = wt * gz
            fx[z - 1, here] = wt * gx
            fy = wt * gy
            known[z, here] = 0.5 * (y_up(fy) - y_down(fy)) + drive
            scale[z - 1, here] = DT * inverse(wt)
        return carry

    lax.fori_loop(0, BX // 8, chunk, 0)

    t, e = coarse[2], coarse[3]
    row = rows_of(t)
    down, up = [], []
    for k, v in ((2, t), (3, e)):
        before, after = left[:, k * CY : (k + 1) * CY], right[:, k * CY : (k + 1) * CY]
        down.append(jnp.where(row == 0, before, pltpu.roll(v, 1, 0)))
        up.append(jnp.where(row == CX - 1, after, pltpu.roll(v, CX - 1, 0)))
    near = [tuple(down), tuple(up), (y_up(t), y_up(e)), (y_down(t), y_down(e))]
    total = jnp.zeros_like(t)
    for tn, en in near:
        total = total + (1.0 + 0.5 * (e + en)) * (tn - t)
    base[...] = total


def phase_kernel(
    coarse, own, fine, rims, fx12, fz12, known, scale12, gxy, x_chip, x_core, zb, za, base, consts,
    out, spectral,
    sides, halo, fx, fz03, fzout, bent, scale03, change, fresh, sems,
):
    n, w = lax.axis_index("narrow"), lax.axis_index("wide")
    even = lax.rem(n, 2) == 0
    has_left, has_right = flag(w > 0), flag(w < NWIDE - 1)
    has_low, has_high = flag(n > 0), flag(n < NNAR - 1)
    left, right = x_sides(x_chip, x_core, slice(4, 8))
    for face, at, there in (
        (zb, jnp.where(even, 0, 2), jnp.where(even, has_low, has_high)),
        (za, jnp.where(even, 2, 0), jnp.where(even, has_high, has_low)),
    ):
        for k in range(2):
            halo[at + k, 8 : 8 + BX] = face[k * BX : (k + 1) * BX] * there
            halo[at + k, 7:8] = face[CORNERS : CORNERS + 1] * there
            halo[at + k, 8 + BX : 9 + BX] = face[CORNERS + 1 : CORNERS + 2] * there
    low = jnp.where(even, zb[ROUGH:FACE], za[ROUGH:FACE])
    high = jnp.where(even, za[ROUGH:FACE], zb[ROUGH:FACE])
    outer = jnp.concatenate([v[:, k * CY : (k + 1) * CY] for v in (low, high) for k in (0, 1)], 0)
    outer = dot(outer, spread_lanes())
    for k in range(4):
        widen(sides, k, outer[k * CX : (k + 1) * CX])
    t, e = coarse[2], coarse[3]
    still = base[...]
    for v, there in ((low, has_low), (high, has_high)):
        tn, en = v[:, 2 * CY : 3 * CY] * there, v[:, 3 * CY :] * there
        still = still + (1.0 + 0.5 * (e + en)) * (tn - t)
    still = dot(still, consts[SY_AT])
    for z in (1, 2):
        fx[z, 8 : 8 + BX] = fx12[z - 1]
    planes = [(halo, 0), (halo, 1), (own, 0), (own, 1), (own, 2), (own, 3), (halo, 2), (halo, 3)]

    def get(k, rows):
        ref, z = planes[k]
        return ref[z, rows]

    def fluxes(c, carry):
        r0 = pl.multiple_of(c * 8, 8)
        here, at, after = pl.ds(r0, 8), pl.ds(r0 + 8, 8), pl.ds(r0 + 16, 8)
        for side, (zz, there) in enumerate(((0, has_low), (5, has_high))):
            v = get(zz + 1, at)
            gz = 0.5 * (get(zz + 2, at) - get(zz, at))
            gx = 0.5 * (x_up(v, get(zz + 1, after)) - x_down(v, get(zz + 1, here)))
            gy = 0.5 * (y_up(v) - y_down(v))
            an = weigh(gz, gx, gy, sides[2 * side, here], sides[2 * side + 1, here])
            fzout[side, here] = there * (an * an * gz)
        for side, z in enumerate((0, NPL - 1)):
            gz = 0.5 * (get(z + 3, at) - get(z + 1, at))
            gx, gy = gxy[side, 0, here], gxy[side, 1, here]
            an = weigh(gz, gx, gy, fine[0, here], fine[1, here])
            wt = an * an
            fz03[side, here] = wt * gz
            fx[z, at] = wt * gx
            fy = wt * gy
            bent[side, here] = known[z, here] + 0.5 * (y_up(fy) - y_down(fy))
            scale03[side, here] = DT * inverse(wt)
        return carry

    lax.fori_loop(0, BX // 8, fluxes, 0)

    def column(pick):
        return jnp.concatenate([pick(z, s) for s in (0, 1) for z in range(NPL)], 0)

    rim = (slice(7, 8), slice(8 + BX, 9 + BX))
    centre = column(lambda z, s: get(z + 2, rim[s]))
    below = column(lambda z, s: get(z + 1, rim[s]))
    above = column(lambda z, s: get(z + 3, rim[s]))
    x_hi = column(lambda z, s: right[z : z + 1] if s else own[z, 8:9])
    x_lo = column(lambda z, s: own[z, 7 + BX : 8 + BX] if s else left[z : z + 1])
    first = rows_of(centre) < NPL
    c2 = jnp.where(first, rims[0:1], rims[2:3])
    s2 = jnp.where(first, rims[1:2], rims[3:4])
    gx = 0.5 * (x_hi - x_lo)
    an = weigh(0.5 * (above - below), gx, 0.5 * (y_up(centre) - y_down(centre)), c2, s2)
    rim_flux = jnp.where(first, has_left, has_right) * (an * an * gx)
    for z in range(NPL):
        fx[z, 7:8] = rim_flux[z : z + 1]
        fx[z, 8 + BX : 9 + BX] = rim_flux[NPL + z : NPL + z + 1]

    flux_z = [(fzout, 0), (fz03, 0), (fz12, 0), (fz12, 1), (fz03, 1), (fzout, 1)]
    rest = [(bent, 0), (known, 1), (known, 2), (bent, 1)]
    scales = [(scale03, 0), (scale12, 0), (scale12, 1), (scale03, 1)]

    def step(c, carry):
        r0 = pl.multiple_of(c * 8, 8)
        here, at, after = pl.ds(r0, 8), pl.ds(r0 + 8, 8), pl.ds(r0 + 16, 8)

        def of(pair):
            return pair[0][pair[1], here]

        total = jnp.zeros((8, NY), F32)
        for z in range(NPL):
            p, f = own[z, at], fx[z, at]
            spread = (
                of(rest[z])
                + 0.5 * (of(flux_z[z + 2]) - of(flux_z[z]))
                + 0.5 * (x_up(f, fx[z, after]) - x_down(f, fx[z, here]))
            )
            rise = of(scales[z]) * spread
            fresh[z, here] = p + rise
            total = total + rise
        change[here] = total
        store(c).start()
        return carry

    def store(c):
        rows = pl.ds(pl.multiple_of(c * 8, 8), 8)
        return pltpu.make_async_copy(fresh.at[:, rows], out.at[0, :, rows], sems.at[c])

    lax.fori_loop(0, BX // 8, step, 0)
    spectral[...] = still + dot(dot(sum_rows(), change[...]), consts[MEAN_AT])
    for c in range(BX // 8):
        store(c).wait()


def solute_kernel(state, own, x_chip, x_core, zb, za, lb, la, done, out, sown, fresh, grown, sems):
    fetch = pltpu.make_async_copy(done.at[0], fresh, sems.at[0])
    fetch.start()
    n = lax.axis_index("narrow")
    even = lax.rem(n, 2) == 0
    left, right = x_sides(x_chip, x_core, slice(8, 12))
    has_low, has_high = flag(n > 0), flag(n < NNAR - 1)
    for z in range(NPL):
        sown[z, 8 : 8 + BX] = state[1, z]
        sown[z, 7:8] = left[z : z + 1]
        sown[z, 8 + BX : 9 + BX] = right[z : z + 1]
    fetch.wait()

    def step(c, carry):
        r0 = pl.multiple_of(c * 8, 8)
        here, at, after = pl.ds(r0, 8), pl.ds(r0 + 8, 8), pl.ds(r0 + 16, 8)

        beyond = pl.ds(pl.multiple_of(r0 + BX, 8), 8)
        ps = (
            [has_low * jnp.where(even, zb[beyond], za[beyond])]
            + [own[z, at] for z in range(NPL)]
            + [has_high * jnp.where(even, za[here], zb[here])]
        )
        ss = (
            [has_low * jnp.where(even, lb[here], la[here])]
            + [sown[z, at] for z in range(NPL)]
            + [has_high * jnp.where(even, la[here], lb[here])]
        )
        for z in range(NPL):
            p, s = ps[z + 1], ss[z + 1]
            q = 0.55 - 0.25 * p
            near = [
                (ps[z], ss[z]),
                (ps[z + 2], ss[z + 2]),
                (x_up(p, own[z, after]), x_up(s, sown[z, after])),
                (x_down(p, own[z, here]), x_down(s, sown[z, here])),
                (y_up(p), y_up(s)),
                (y_down(p), y_down(s)),
            ]
            total = jnp.zeros_like(p)
            for pn, sn in near:
                total = total + (q - 0.25 * pn) * (sn - s)
            grown[z, here] = s + DT * total + (0.5 + 0.425 * s) * (fresh[z, here] - p)
        store(c).start()
        return carry

    def store(c):
        rows = pl.ds(pl.multiple_of(c * 8, 8), 8)
        return pltpu.make_async_copy(grown.at[:, rows], out.at[1, :, rows], sems.at[1 + c])

    lax.fori_loop(0, BX // 8, step, 0)
    for c in range(BX // 8):
        store(c).wait()


def chip_kernel(mine, partner, lb, la, here, message, far):
    core = lax.rem(lax.axis_index("wide"), 2)
    first, second = pl.ds(pl.multiple_of(core * CX, 8), CX), pl.ds(pl.multiple_of((1 - core) * CX, 8), CX)
    here[first] = mine[...]
    here[second] = partner[...]
    message[0:CX] = mine[...]
    near = jnp.where(core == 0, partner[0:8], pltpu.roll(partner[8:16], 4, 0))
    message[CX : CX + 8] = near
    far[...] = jnp.where(core == 0, mine[0:8], pltpu.roll(mine[8:16], 4, 0))


def window_kernel(here, across, shared, out, view, sems):
    w = lax.axis_index("wide")
    core, chip = lax.rem(w, 2), lax.div(w, 2)
    has_before, has_after = flag(chip > 0), flag(chip < NWIDE // 2 - 1)

    @pl.when(core == 0)
    def _():
        view[0:4] = across[CX : CX + 4] * has_before
        view[4:20] = across[0:CX] * has_before
        view[20:52] = here[...]
        view[52:56] = shared[0:4] * has_after

    @pl.when(core == 1)
    def _():
        view[0:4] = shared[0:4] * has_before
        view[4:36] = here[...]
        view[36:56] = across[0:20] * has_after

    copies = [pltpu.make_async_copy(view, out.at[m], sems.at[m]) for m in range(NNAR)]
    for copy in copies:
        copy.start()
    for copy in copies:
        copy.wait()


def solve_kernel(planes, coarse, consts, out, modes, rows):
    n, w = lax.axis_index("narrow"), lax.axis_index("wide")
    has_left, has_right = flag(w > 0), flag(w < NWIDE - 1)
    values = [planes[m] for m in range(NNAR)]
    for k in range(NNAR):
        total = float(SZ[k, 0]) * values[0]
        for m in range(1, NNAR):
            total = total + float(SZ[k, m]) * values[m]
        modes[k * 56 : (k + 1) * 56] = total
    f = [modes[pl.ds(j, 8, stride=56), :] for j in range(56)]
    inv_of = [consts[INV_AT + 8 * i : INV_AT + 8 * i + 8] for i in range(SUBX)]
    link = [KBAR * v for v in inv_of]

    def solve(order, keep):
        h = [inv_of[0] * f[order[0]]]
        for i in range(1, SUBX):
            h.append(inv_of[i] * f[order[i]] + link[i] * h[-1])
        x = h[-1]
        found = {order[-1]: x}
        for i in range(SUBX - 2, -1, -1):
            if order[i] not in keep:
                break
            x = h[i] + link[i] * x
            found[order[i]] = x
        return found

    mine = solve(list(range(16, 40)), set(range(20, 40)))
    lower = solve(list(range(0, 24)), set(range(20, 24)))
    upper = solve(list(range(55, 31, -1)), set(range(32, 36)))
    weight = consts[pl.ds(pl.multiple_of(SZ_AT + 8 * n, 8), 8)]
    for j in range(CX):
        x = mine[20 + j]
        if 20 + j in lower:
            x = x + has_left * lower[20 + j]
        if 20 + j in upper:
            x = x + has_right * upper[20 + j]
        rows[j : j + 1] = jnp.sum(x * weight, axis=0, keepdims=True)
    out[0] = coarse[2] + dot(rows[...], consts[SY_AT])


def kernel(body, outs, scratch=(), far=(), far_outs=(), aliases=None, mib=16):
    many = isinstance(outs, (list, tuple))

    def call(*args):
        return pl.pallas_call(
            body,
            out_shape=outs,
            in_specs=[HBM if i in far else VMEM for i in range(len(args))],
            out_specs=[HBM if i in far_outs else VMEM for i in range(len(outs))] if many else (HBM if far_outs else VMEM),
            input_output_aliases=aliases or {},
            scratch_shapes=list(scratch),
            compiler_params=params(mib),
            name=body.__name__,
        )(*args)

    return call


def afar(v):
    return pltpu.with_memory_space_constraint(v, pltpu.HBM)


def on_device(state_in, ids, frozen, temp, angles):
    inputs = [afar(v) for v in (state_in, ids, frozen, temp, angles.reshape(1, -1))]
    to_chip, to_core, state, coarse = kernel(
        stage_kernel,
        [sds(16, NY)] * 2 + [sds(2, NPL, BX, NY), sds(4, CX, CY)],
        [
            pltpu.VMEM((1, CX, CY), jnp.int32),
            pltpu.VMEM((1, CX, CY), jnp.int32),
            pltpu.VMEM((1, CX, CY), F32),
            pltpu.VMEM((1, 64), F32),
            pltpu.SemaphoreType.DMA((6,)),
        ],
        far=range(5),
    )(*inputs)
    x_chip = lax.ppermute(to_chip, "wide", CHIPS)
    x_core = lax.ppermute(to_core, "wide", CORES)
    fine, consts = kernel(
        spread_kernel, [sds(3, BX, NY), sds(*CONSTS.shape)], [pltpu.SemaphoreType.DMA], far=(1,)
    )(coarse, afar(jnp.asarray(CONSTS)))
    face_b, face_a = kernel(face_kernel, [sds(FACE, NY)] * 2)(state, coarse, x_chip, x_core)
    zb = lax.ppermute(face_b, "narrow", PAIR_B)
    za = lax.ppermute(face_a, "narrow", PAIR_A)
    own, rims, fx12, fz12, known, scale12, gxy, base = kernel(
        prepare_kernel,
        [
            sds(NPL, BX + 16, NY), sds(8, NY), sds(2, BX, NY), sds(2, BX, NY),
            sds(NPL, BX, NY), sds(2, BX, NY), sds(2, 2, BX, NY), sds(CX, CY),
        ],
    )(state, coarse, fine, x_chip, x_core)
    late_b, late_a = kernel(late_kernel, [sds(BX, NY)] * 2)(state, base)
    lb = lax.ppermute(late_b, "narrow", PAIR_B)
    la = lax.ppermute(late_a, "narrow", PAIR_A)
    result, spectral = kernel(
        phase_kernel,
        [sds(2, NPL, BX, NY), sds(CX, CY)],
        [
            pltpu.VMEM((4, BX, NY), F32),
            pltpu.VMEM((4, BX + 16, NY), F32),
            pltpu.VMEM((NPL, BX + 16, NY), F32),
            pltpu.VMEM((2, BX, NY), F32),
            pltpu.VMEM((2, BX, NY), F32),
            pltpu.VMEM((2, BX, NY), F32),
            pltpu.VMEM((2, BX, NY), F32),
            pltpu.VMEM((BX, NY), F32),
            pltpu.VMEM((NPL, BX, NY), F32),
            pltpu.SemaphoreType.DMA((BX // 8,)),
        ],
        far_outs=(0,),
    )(coarse, own, fine, rims, fx12, fz12, known, scale12, gxy, x_chip, x_core, zb, za, base, consts)
    partner = lax.ppermute(spectral, "wide", CORES)
    here, message, far = kernel(
        chip_kernel, [sds(2 * CX, CY), sds(CX + 8, CY), sds(8, CY)]
    )(
        spectral, partner, lb, la
    )
    across = lax.ppermute(message, "wide", CHIPS)
    shared = lax.ppermute(far, "wide", NEXT_CHIPS)
    windows = kernel(
        window_kernel,
        sds(NNAR, 56, CY),
        [pltpu.VMEM((56, CY), F32), pltpu.SemaphoreType.DMA((NNAR,))],
        far_outs=(0,),
    )(here, across, shared)
    planes = lax.all_to_all(windows, "narrow", 0, 0)
    state_new = kernel(
        solute_kernel,
        sds(2, NPL, BX, NY),
        [
            pltpu.VMEM((NPL, BX + 16, NY), F32),
            pltpu.VMEM((NPL, BX, NY), F32),
            pltpu.VMEM((NPL, BX, NY), F32),
            pltpu.SemaphoreType.DMA((1 + BX // 8,)),
        ],
        far=(8,),
        far_outs=(0,),
        aliases={8: 0},
    )(state, own, x_chip, x_core, zb, za, lb, la, result)
    adjusted = kernel(
        solve_kernel,
        sds(1, CX, CY),
        [pltpu.VMEM((NNAR * 56, CY), F32), pltpu.VMEM((CX, CY), F32)],
    )(planes, coarse, consts)
    return state_new, adjusted


def solution(mesh):
    return jax.shard_map(
        on_device,
        mesh=mesh,
        in_specs=(
            P(None, "narrow", "wide", None),
            P("narrow", "wide", None),
            P("narrow", "wide", None),
            P("narrow", "wide", None),
            P(),
        ),
        out_specs=(P(None, "narrow", "wide", None), P("narrow", "wide", None)),
        check_vma=False,
    )
```

```python
import functools

import jax
import jax.numpy as jnp
import numpy as np
from jax import lax
from jax.experimental import pallas as pl
from jax.experimental.pallas import tpu as pltpu
from jax.sharding import PartitionSpec as P

F32 = jnp.float32
NNAR, NWIDE = 8, 32
NPL, BX, NY = 4, 64, 512
ROUGH, FACE, CORNERS, LATE = 128, 144, 64, 72
CX, CY = 16, 128
SUBX = 24
SIGMA, KBAR = 0.05, 0.75
DT = 0.15
VMEM = pl.BlockSpec(memory_space=pltpu.VMEM)
HBM = pl.BlockSpec(memory_space=pltpu.HBM)


def sds(*shape):
    return jax.ShapeDtypeStruct(shape, F32)


def params(mib):
    return pltpu.CompilerParams(vmem_limit_bytes=mib * 1024 * 1024)


def sine(points):
    k = np.arange(1, points + 1)
    return np.sqrt(2.0 / (points + 1)) * np.sin(np.pi * np.outer(k, k) / (points + 1))


def level(points):
    return 2.0 - 2.0 * np.cos(np.pi * np.arange(1, points + 1) / (points + 1))


SZ, SY = sine(8), sine(CY)
MEAN_Y = np.repeat(SY, 4, axis=0) / 64.0
SZ_ROWS = np.repeat(SZ[:, :, None], CY, 2)


def elimination():
    diag = SIGMA + KBAR * (level(8)[:, None] + level(CY)[None, :] + 2.0)
    inv = [1.0 / diag]
    for _ in range(SUBX - 1):
        inv.append(1.0 / (diag - KBAR * KBAR * inv[-1]))
    return np.stack(inv)


INVERSE = elimination()


CONSTS = np.concatenate([SY, MEAN_Y, INVERSE.reshape(-1, CY), SZ_ROWS.reshape(-1, CY)]).astype(np.float32)
SY_AT, MEAN_AT, INV_AT, SZ_AT = slice(0, 128), slice(128, 640), 640, 640 + 8 * SUBX


def wide_ring(k):
    return [(i, (i + k) % NWIDE) for i in range(NWIDE)]


PAIR_A = [(i, i ^ 1) for i in range(NNAR)]
PAIR_B = [(i, (((i + 1) ^ 1) - 1) % NNAR) for i in range(NNAR)]
CORES = [(i, i ^ 1) for i in range(NWIDE)]
CHIPS = [(i, (((i + 1) ^ 1) - 1) % NWIDE) for i in range(NWIDE)]
NEXT_CHIPS = [(i, (i + (2 if i % 2 else -2)) % NWIDE) for i in range(NWIDE)]


def lanes(v):
    return lax.broadcasted_iota(jnp.int32, v.shape, v.ndim - 1)


def rows_of(v):
    return lax.broadcasted_iota(jnp.int32, v.shape, len(v.shape) - 2)


def y_up(v):
    n = v.shape[-1]
    return jnp.where(lanes(v) == n - 1, 0.0, pltpu.roll(v, n - 1, v.ndim - 1))


def y_down(v):
    return jnp.where(lanes(v) == 0, 0.0, pltpu.roll(v, 1, v.ndim - 1))


def x_up(v, after):
    return pltpu.roll(jnp.where(rows_of(v) == 0, after, v), 7, v.ndim - 2)


def x_down(v, before):
    return pltpu.roll(jnp.where(rows_of(v) == 7, before, v), 1, v.ndim - 2)


def inverse(v):
    guess = pl.reciprocal(v, approx=True)
    return guess * (2.0 - v * guess)


def weigh(dz, dx, dy, c2, s2):
    q0, a, b = dz * dz, dx * dx, dy * dy
    r = a + b
    uv = s2 * (b - a) + c2 * (dx * dy)
    num = q0 * q0 + r * r - 2.0 * (uv * uv)
    over = inverse(q0 + r + 4.0)
    return 0.55 + 0.6 * (num * (over * over))


def flag(cond):
    return jnp.where(cond, 1.0, 0.0).astype(F32)


def spread(v):
    lane = lax.shift_right_logical(lanes(v), 2)
    return jnp.concatenate(
        [jnp.take_along_axis(v, lane + 32 * j, axis=1) for j in range(NY // CY)], 1
    )


def halves(v):
    high = v.astype(jnp.bfloat16)
    return high, (v - high.astype(F32)).astype(jnp.bfloat16)


def dot(a, b):
    (a1, a2), (b1, b2) = halves(a), halves(b)
    mul = functools.partial(jnp.dot, preferred_element_type=F32)
    return mul(a1, b1) + (mul(a1, b2) + mul(a2, b1))


def stage_kernel(
    state_in, ids_in, frozen_in, temp_in, angles_in,
    face_b, face_a, x_chip, x_core, state, coarse,
    ids, frozen, temp, angles, sems,
):
    copies = [
        pltpu.make_async_copy(src, dst, sems.at[i])
        for i, (src, dst) in enumerate(
            [
                (state_in.at[0], state.at[0]),
                (state_in.at[1], state.at[1]),
                (ids_in, ids),
                (frozen_in, frozen),
                (temp_in, temp),
                (angles_in, angles),
            ]
        )
    ]
    for copy in copies:
        copy.start()
    for copy in copies[2:]:
        copy.wait()
    table = jnp.concatenate([angles[...], angles[...]], 1)
    c = jnp.take_along_axis(jnp.broadcast_to(jnp.cos(table), (CX, CY)), ids[0], axis=1)
    s = jnp.take_along_axis(jnp.broadcast_to(jnp.sin(table), (CX, CY)), ids[0], axis=1)
    coarse[0] = c * c - s * s
    coarse[1] = c * s
    coarse[2] = temp[0]
    coarse[3] = -0.5 * frozen[0].astype(F32)
    for copy in copies[:2]:
        copy.wait()
    even = lax.rem(lax.axis_index("narrow"), 2) == 0
    for ref, top in ((face_b, jnp.logical_not(even)), (face_a, even)):
        first = jnp.where(top, 2, 0)
        ref[0:BX] = state[0, first]
        ref[BX : 2 * BX] = state[0, first + 1]
        for k in range(4):
            ref[ROUGH:FACE, k * CY : (k + 1) * CY] = coarse[k]
    core0 = lax.rem(lax.axis_index("wide"), 2) == 0
    for ref, low in ((x_chip, core0), (x_core, jnp.logical_not(core0))):
        for z in range(NPL):
            for at, ch, first, last in ((0, 0, 0, BX - 1), (4, 0, 1, BX - 2), (8, 1, 0, BX - 1)):
                ref[at + z : at + z + 1] = jnp.where(
                    low, state[ch, z, first : first + 1], state[ch, z, last : last + 1]
                )
        for k in range(4):
            ref[12:13, k * CY : (k + 1) * CY] = jnp.where(
                low, coarse[k, 0:1], coarse[k, CX - 1 : CX]
            )
        ref[13:16] = jnp.zeros((3, NY), F32)


def x_sides(x_chip, x_core, rows):
    w = lax.axis_index("wide")
    core0 = lax.rem(w, 2) == 0
    left = jnp.where(core0, x_chip[rows], x_core[rows]) * flag(w > 0)
    right = jnp.where(core0, x_core[rows], x_chip[rows]) * flag(w < NWIDE - 1)
    return left, right


def late_kernel(state, x_chip, x_core, own, late_b, late_a):
    even = lax.rem(lax.axis_index("narrow"), 2) == 0
    left, right = x_sides(x_chip, x_core, slice(0, 8))
    for ref, top in ((late_b, jnp.logical_not(even)), (late_a, even)):
        ref[0:BX] = state[1, jnp.where(top, 3, 0)]
        ref[CORNERS : CORNERS + 1] = jnp.where(top, left[3:4], left[0:1])
        ref[CORNERS + 1 : CORNERS + 2] = jnp.where(top, right[3:4], right[0:1])
        ref[CORNERS + 2 : LATE] = jnp.zeros((LATE - CORNERS - 2, NY), F32)


def widen(ref, at, rough):
    for k in range(CX):
        ref[at, 4 * k : 4 * k + 4] = jnp.broadcast_to(rough[k : k + 1], (4, NY))


def spread_kernel(coarse, fine):
    for k in range(3):
        widen(fine, k, spread(coarse[k]))


def local_terms(c, state, own, fine, fx, fz, known, scale, dxy):
    r0 = pl.multiple_of(c * 8, 8)
    here, at, after = pl.ds(r0, 8), pl.ds(r0 + 8, 8), pl.ds(r0 + 16, 8)
    for z in range(NPL):
        v = own[z, at]
        dx = x_up(v, own[z, after]) - x_down(v, own[z, here])
        dy = y_up(v) - y_down(v)
        m = 1.0 - v * v
        drive = m * (v - 1.5 * (state[1, z, here] + fine[2, here]) * m)
        if z in (0, NPL - 1):
            known[z, here] = drive
            dxy[z // 2, 0, here] = dx
            dxy[z // 2, 1, here] = dy
            continue
        dz = own[z + 1, at] - own[z - 1, at]
        an = weigh(dz, dx, dy, fine[0, here], fine[1, here])
        wt = an * an
        quarter = 0.25 * wt
        fz[z - 1, here] = quarter * dz
        fx[z - 1, here] = quarter * dx
        fy = quarter * dy
        known[z, here] = (y_up(fy) - y_down(fy)) + drive
        scale[z - 1, here] = DT * inverse(wt)


def inside_kernel(state, fine, own, fx, fz, known, scale, dxy):
    for z in range(NPL):
        own[z, 8 : 8 + BX] = state[0, z]

    def chunk(c, carry):
        local_terms(c, state, own, fine, fx, fz, known, scale, dxy)
        return carry

    lax.fori_loop(1, BX // 8 - 1, chunk, 0)


def edge_kernel(
    state, coarse, fine, x_chip, x_core, consts_in, own_in, fx_in, fz_in, known_in, scale_in, dxy_in,
    own, fx, fz, known, scale, dxy, rims, base, consts,
    sem,
):
    fetch = pltpu.make_async_copy(consts_in, consts, sem)
    fetch.start()
    left, right = x_sides(x_chip, x_core, slice(0, 4))
    for z in range(NPL):
        own[z, 7:8] = left[z : z + 1]
        own[z, 8 + BX : 9 + BX] = right[z : z + 1]
    left, right = x_sides(x_chip, x_core, slice(12, 13))
    rows = [side[:, k * CY : (k + 1) * CY] for side in (left, right) for k in (0, 1)]
    rims[...] = spread(jnp.concatenate(rows + rows, 0))
    for c in (0, BX // 8 - 1):
        local_terms(c, state, own, fine, fx, fz, known, scale, dxy)
    t, e = coarse[2], coarse[3]
    row = rows_of(t)
    down, up = [], []
    for k, v in ((2, t), (3, e)):
        before, after = left[:, k * CY : (k + 1) * CY], right[:, k * CY : (k + 1) * CY]
        down.append(jnp.where(row == 0, before, pltpu.roll(v, 1, 0)))
        up.append(jnp.where(row == CX - 1, after, pltpu.roll(v, CX - 1, 0)))
    near = [tuple(down), tuple(up), (y_up(t), y_up(e)), (y_down(t), y_down(e))]
    total = jnp.zeros_like(t)
    for tn, en in near:
        total = total + (1.0 + 0.5 * (e + en)) * (tn - t)
    base[...] = total
    fetch.wait()


def phase_kernel(
    coarse, own, fine, fx12, fz12, known, scale12, dxy, zb, za, base, consts,
    out, edges, spectral, lines,
    sides, halo, fx, fz03, fzout, bent, scale03, change, fresh, sems,
):
    n = lax.axis_index("narrow")
    even = lax.rem(n, 2) == 0
    has_low, has_high = flag(n > 0), flag(n < NNAR - 1)
    for face, at, there in (
        (zb, jnp.where(even, 0, 2), jnp.where(even, has_low, has_high)),
        (za, jnp.where(even, 2, 0), jnp.where(even, has_high, has_low)),
    ):
        for k in range(2):
            halo[at + k, 8 : 8 + BX] = face[k * BX : (k + 1) * BX] * there
    low = jnp.where(even, zb[ROUGH:FACE], za[ROUGH:FACE])
    high = jnp.where(even, za[ROUGH:FACE], zb[ROUGH:FACE])
    for k, v in enumerate((low, low, high, high)):
        wide = spread(v[:, (k % 2) * CY : (k % 2 + 1) * CY])
        widen(sides, k, wide)
        lines[8 + 4 * (k % 2) + 2 * (k // 2) : 9 + 4 * (k % 2) + 2 * (k // 2)] = wide[0:1]
        lines[9 + 4 * (k % 2) + 2 * (k // 2) : 10 + 4 * (k % 2) + 2 * (k // 2)] = wide[CX - 1 : CX]
    t, e = coarse[2], coarse[3]
    still = base[...]
    for v, there in ((low, has_low), (high, has_high)):
        tn, en = v[:, 2 * CY : 3 * CY] * there, v[:, 3 * CY :] * there
        still = still + (1.0 + 0.5 * (e + en)) * (tn - t)
    for z in range(NPL):
        fx[z, 7:8] = jnp.zeros((1, NY), F32)
        fx[z, 8 + BX : 9 + BX] = jnp.zeros((1, NY), F32)
    for z in (1, 2):
        fx[z, 8 : 8 + BX] = fx12[z - 1]
    planes = [(halo, 0), (halo, 1), (own, 0), (own, 1), (own, 2), (own, 3), (halo, 2), (halo, 3)]

    def get(k, rows):
        ref, z = planes[k]
        return ref[z, rows]

    def fluxes(c, carry):
        r0 = pl.multiple_of(c * 8, 8)
        here, at, after = pl.ds(r0, 8), pl.ds(r0 + 8, 8), pl.ds(r0 + 16, 8)
        for side, (zz, there) in enumerate(((0, has_low), (5, has_high))):
            v = get(zz + 1, at)
            dz = get(zz + 2, at) - get(zz, at)
            dx = x_up(v, get(zz + 1, after)) - x_down(v, get(zz + 1, here))
            dy = y_up(v) - y_down(v)
            an = weigh(dz, dx, dy, sides[2 * side, here], sides[2 * side + 1, here])
            fzout[side, here] = (0.25 * there) * (an * an * dz)
        for side, z in enumerate((0, NPL - 1)):
            dz = get(z + 3, at) - get(z + 1, at)
            dx, dy = dxy[side, 0, here], dxy[side, 1, here]
            an = weigh(dz, dx, dy, fine[0, here], fine[1, here])
            wt = an * an
            quarter = 0.25 * wt
            fz03[side, here] = quarter * dz
            fx[z, at] = quarter * dx
            fy = quarter * dy
            bent[side, here] = known[z, here] + (y_up(fy) - y_down(fy))
            scale03[side, here] = DT * inverse(wt)
        return carry

    lax.fori_loop(0, BX // 8, fluxes, 0)

    for side in range(2):
        for row in (0, BX - 1):
            fzout[side, row : row + 1] = jnp.zeros((1, NY), F32)
    flux_z = [(fzout, 0), (fz03, 0), (fz12, 0), (fz12, 1), (fz03, 1), (fzout, 1)]
    rest = [(bent, 0), (known, 1), (known, 2), (bent, 1)]
    scales = [(scale03, 0), (scale12, 0), (scale12, 1), (scale03, 1)]

    def store(c):
        rows = pl.ds(8 * c, 8)
        return pltpu.make_async_copy(fresh.at[:, rows], out.at[0, :, rows], sems.at[c])

    for c in range(BX // 8):
        here, at, after = pl.ds(8 * c, 8), pl.ds(8 * c + 8, 8), pl.ds(8 * c + 16, 8)
        total = jnp.zeros((8, NY), F32)
        for z in range(NPL):
            p, f = own[z, at], fx[z, at]
            spread_z = flux_z[z + 2][0][flux_z[z + 2][1], here] - flux_z[z][0][flux_z[z][1], here]
            spread_x = x_up(f, fx[z, after]) - x_down(f, fx[z, here])
            factor = scales[z][0][scales[z][1], here]
            rise = factor * (rest[z][0][rest[z][1], here] + spread_z + spread_x)
            total = total + rise
            if c in (0, BX // 8 - 1):
                edges[z, 0 if c == 0 else 1] = p + rise
                row, line = (0, z) if c == 0 else (7, NPL + z)
                lines[line : line + 1] = factor[row : row + 1]
            else:
                fresh[z, here] = p + rise
        total = total + pltpu.roll(total, 1, 0)
        total = total + pltpu.roll(total, 2, 0)
        change[2 * c : 2 * c + 1] = total[3:4]
        change[2 * c + 1 : 2 * c + 2] = total[7:8]
        if 0 < c < BX // 8 - 1:
            store(c).start()
    spectral[...] = dot(still, consts[SY_AT]) + dot(change[...], consts[MEAN_AT])
    for c in range(1, BX // 8 - 1):
        store(c).wait()


def rim_kernel(
    own, rims, x_chip, x_core, zb, za, lb, la, edges, spectral_in, lines, consts,
    tiles, spectral, far,
):
    n, w = lax.axis_index("narrow"), lax.axis_index("wide")
    even = lax.rem(n, 2) == 0
    has_left, has_right = flag(w > 0), flag(w < NWIDE - 1)
    has_low, has_high = flag(n > 0), flag(n < NNAR - 1)
    inner = x_sides(x_chip, x_core, slice(4, 8))

    def beyond(b, a, rows, high):
        if high:
            return jnp.where(even, a[rows], b[rows]) * has_high
        return jnp.where(even, b[rows], a[rows]) * has_low

    def corner(high, s):
        return beyond(lb, la, slice(CORNERS + s, CORNERS + s + 1), high)

    def outer(high, plane, x):
        return beyond(zb, za, slice(plane * BX + x, plane * BX + x + 1), high)

    rim = (7, 8 + BX)
    values = [[], [], [], [], []]
    for s in range(2):
        for z in range(NPL):
            at = slice(rim[s], rim[s] + 1)
            here = own[z, at]
            below = own[z - 1, at] if z > 0 else corner(False, s)
            above = own[z + 1, at] if z < NPL - 1 else corner(True, s)
            side = inner[s][z : z + 1]
            x_lo, x_hi = (own[z, 7 + BX : 8 + BX], side) if s else (side, own[z, 8:9])
            for rows, v in zip(values, (here, below, above, x_lo, x_hi)):
                rows.append(v)
    for high in (False, True):
        for s in range(2):
            x, near = (BX - 1, BX - 2) if s else (0, 1)
            mine = own[NPL - 1 if high else 0, 8 + x : 9 + x]
            here, behind = outer(high, 0 if high else 1, x), outer(high, 1 if high else 0, x)
            beside, past = outer(high, 0 if high else 1, near), corner(high, s)
            below, above = (mine, behind) if high else (behind, mine)
            x_lo, x_hi = (beside, past) if s else (past, beside)
            for rows, v in zip(values, (here, below, above, x_lo, x_hi)):
                rows.append(v)
    here, below, above, x_lo, x_hi = (
        jnp.concatenate(rows + [jnp.zeros((4, NY), F32)], 0) for rows in values
    )
    c2, s2 = (
        jnp.concatenate(
            [jnp.broadcast_to(rims[k : k + 1], (NPL, NY)), jnp.broadcast_to(rims[k + 2 : k + 3], (NPL, NY)),
             lines[8 + 4 * k : 12 + 4 * k], jnp.zeros((4, NY), F32)], 0,
        )
        for k in (0, 1)
    )
    dz, dx, dy = above - below, x_hi - x_lo, y_up(here) - y_down(here)
    an = weigh(dz, dx, dy, c2, s2)
    quarter = 0.25 * (an * an)
    row = rows_of(here[0:8])
    x_part = quarter[0:8] * dx[0:8] * jnp.where(row < NPL, -has_left, has_right)
    z_flux = quarter[8:16] * dz[8:16]
    z_part = jnp.zeros((8, NY), F32)
    for high in (False, True):
        for s in range(2):
            line = z_flux[2 * high + s : 2 * high + s + 1]
            line = line * has_high if high else -has_low * line
            z_part = jnp.where(row == NPL * s + (NPL - 1 if high else 0), line, z_part)
    rise = lines[0:8] * (x_part + z_part)
    for c in range(2):
        for z in range(NPL):
            add = rise[NPL * c + z : NPL * c + z + 1]
            tiles[z, c] = edges[z, c] + jnp.where(row == 7 * c, add, 0.0)
    sums = [jnp.sum(rise[NPL * c : NPL * (c + 1)], axis=0, keepdims=True) for c in range(2)]
    more = dot(jnp.concatenate(sums + [jnp.zeros((14, NY), F32)], 0), consts[MEAN_AT])
    first = rows_of(spectral_in)
    moved = spectral_in[...] + jnp.where(
        first == 0, more[0:1], jnp.where(first == CX - 1, more[1:2], 0.0)
    )
    spectral[...] = moved
    core0 = lax.rem(w, 2) == 0
    far[...] = jnp.where(core0, moved[0:8], pltpu.roll(moved[8:16], 4, 0))


def solute_kernel(state, own, x_chip, x_core, zb, za, lb, la, tiles, done, out, sown, fresh, grown, sems):
    within = pl.ds(8, BX - 16)
    fetch = pltpu.make_async_copy(done.at[0, :, within], fresh.at[:, within], sems.at[0])
    fetch.start()
    ends = [
        pltpu.make_async_copy(tiles.at[:, c], out.at[0, :, pl.ds((BX - 8) * c, 8)], sems.at[9 + c])
        for c in range(2)
    ]
    for copy in ends:
        copy.start()
    for c in range(2):
        fresh[:, (BX - 8) * c : (BX - 8) * c + 8] = tiles[:, c]
    n = lax.axis_index("narrow")
    even = lax.rem(n, 2) == 0
    left, right = x_sides(x_chip, x_core, slice(8, 12))
    has_low, has_high = flag(n > 0), flag(n < NNAR - 1)
    for z in range(NPL):
        sown[z, 8 : 8 + BX] = state[1, z]
        sown[z, 7:8] = left[z : z + 1]
        sown[z, 8 + BX : 9 + BX] = right[z : z + 1]
    fetch.wait()

    def step(c, carry):
        r0 = pl.multiple_of(c * 8, 8)
        here, at, after = pl.ds(r0, 8), pl.ds(r0 + 8, 8), pl.ds(r0 + 16, 8)

        beyond = pl.ds(pl.multiple_of(r0 + BX, 8), 8)
        ps = (
            [has_low * jnp.where(even, zb[beyond], za[beyond])]
            + [own[z, at] for z in range(NPL)]
            + [has_high * jnp.where(even, za[here], zb[here])]
        )
        ss = (
            [has_low * jnp.where(even, lb[here], la[here])]
            + [sown[z, at] for z in range(NPL)]
            + [has_high * jnp.where(even, la[here], lb[here])]
        )
        for z in range(NPL):
            p, s = ps[z + 1], ss[z + 1]
            q = 0.55 - 0.25 * p
            near = [
                (ps[z], ss[z]),
                (ps[z + 2], ss[z + 2]),
                (x_up(p, own[z, after]), x_up(s, sown[z, after])),
                (x_down(p, own[z, here]), x_down(s, sown[z, here])),
                (y_up(p), y_up(s)),
                (y_down(p), y_down(s)),
            ]
            total = jnp.zeros_like(p)
            for pn, sn in near:
                total = total + (q - 0.25 * pn) * (sn - s)
            grown[z, here] = s + DT * total + (0.5 + 0.425 * s) * (fresh[z, here] - p)
        store(c).start()
        return carry

    def store(c):
        rows = pl.ds(pl.multiple_of(c * 8, 8), 8)
        return pltpu.make_async_copy(grown.at[:, rows], out.at[1, :, rows], sems.at[1 + c])

    lax.fori_loop(0, BX // 8, step, 0)
    for c in range(BX // 8):
        store(c).wait()
    for copy in ends:
        copy.wait()


def chip_kernel(mine, partner, here, message):
    core = lax.rem(lax.axis_index("wide"), 2)
    first, second = pl.ds(pl.multiple_of(core * CX, 8), CX), pl.ds(pl.multiple_of((1 - core) * CX, 8), CX)
    here[first] = mine[...]
    here[second] = partner[...]
    message[0:CX] = mine[...]
    near = jnp.where(core == 0, partner[0:8], pltpu.roll(partner[8:16], 4, 0))
    message[CX : CX + 8] = near
def window_kernel(here, across, shared, view):
    w = lax.axis_index("wide")
    core, chip = lax.rem(w, 2), lax.div(w, 2)
    has_before, has_after = flag(chip > 0), flag(chip < NWIDE // 2 - 1)

    @pl.when(core == 0)
    def _():
        view[0:4] = across[CX : CX + 4] * has_before
        view[4:20] = across[0:CX] * has_before
        view[20:52] = here[...]
        view[52:56] = shared[0:4] * has_after

    @pl.when(core == 1)
    def _():
        view[0:4] = shared[0:4] * has_before
        view[4:36] = here[...]
        view[36:56] = across[0:20] * has_after


def solve_kernel(planes, coarse, consts, out, modes, rows):
    n, w = lax.axis_index("narrow"), lax.axis_index("wide")
    has_left, has_right = flag(w > 0), flag(w < NWIDE - 1)
    half = NNAR // 2
    folded = [
        [planes[m] + planes[NNAR - 1 - m] for m in range(half)],
        [planes[m] - planes[NNAR - 1 - m] for m in range(half)],
    ]
    for k in range(NNAR):
        total = float(SZ[k, 0]) * folded[k % 2][0]
        for m in range(1, half):
            total = total + float(SZ[k, m]) * folded[k % 2][m]
        modes[k * 56 : (k + 1) * 56] = total
    f = [modes[pl.ds(j, 8, stride=56), :] for j in range(56)]
    inv_of = [consts[INV_AT + 8 * i : INV_AT + 8 * i + 8] for i in range(SUBX)]
    link = [KBAR * v for v in inv_of]

    def solve(order, keep):
        h = [inv_of[0] * f[order[0]]]
        for i in range(1, SUBX):
            h.append(inv_of[i] * f[order[i]] + link[i] * h[-1])
        x = h[-1]
        found = {order[-1]: x}
        for i in range(SUBX - 2, -1, -1):
            if order[i] not in keep:
                break
            x = h[i] + link[i] * x
            found[order[i]] = x
        return found

    mine = solve(list(range(16, 40)), set(range(20, 40)))
    lower = solve(list(range(0, 24)), set(range(20, 24)))
    upper = solve(list(range(55, 31, -1)), set(range(32, 36)))
    weight = consts[pl.ds(pl.multiple_of(SZ_AT + 8 * n, 8), 8)]
    for j in range(CX):
        x = mine[20 + j]
        if 20 + j in lower:
            x = x + has_left * lower[20 + j]
        if 20 + j in upper:
            x = x + has_right * upper[20 + j]
        rows[j : j + 1] = jnp.sum(x * weight, axis=0, keepdims=True)
    out[0] = coarse[2] + dot(rows[...], consts[SY_AT])


def kernel(body, outs, scratch=(), far=(), far_outs=(), aliases=None, mib=16):
    many = isinstance(outs, (list, tuple))

    def call(*args):
        return pl.pallas_call(
            body,
            out_shape=outs,
            in_specs=[HBM if i in far else VMEM for i in range(len(args))],
            out_specs=[HBM if i in far_outs else VMEM for i in range(len(outs))] if many else (HBM if far_outs else VMEM),
            input_output_aliases=aliases or {},
            scratch_shapes=list(scratch),
            compiler_params=params(mib),
            name=body.__name__,
        )(*args)

    return call


def afar(v):
    return pltpu.with_memory_space_constraint(v, pltpu.HBM)


def on_device(state_in, ids, frozen, temp, angles):
    inputs = [afar(v) for v in (state_in, ids, frozen, temp, angles.reshape(1, -1))]
    face_b, face_a, to_chip, to_core, state, coarse = kernel(
        stage_kernel,
        [sds(FACE, NY)] * 2 + [sds(16, NY)] * 2 + [sds(2, NPL, BX, NY), sds(4, CX, CY)],
        [
            pltpu.VMEM((1, CX, CY), jnp.int32),
            pltpu.VMEM((1, CX, CY), jnp.int32),
            pltpu.VMEM((1, CX, CY), F32),
            pltpu.VMEM((1, 64), F32),
            pltpu.SemaphoreType.DMA((6,)),
        ],
        far=range(5),
    )(*inputs)
    zb = lax.ppermute(face_b, "narrow", PAIR_B)
    za = lax.ppermute(face_a, "narrow", PAIR_A)
    x_chip = lax.ppermute(to_chip, "wide", CHIPS)
    x_core = lax.ppermute(to_core, "wide", CORES)
    fine = kernel(spread_kernel, sds(3, BX, NY))(coarse)
    shapes = [
        sds(NPL, BX + 16, NY), sds(2, BX, NY), sds(2, BX, NY), sds(NPL, BX, NY), sds(2, BX, NY),
        sds(2, 2, BX, NY),
    ]
    inside = kernel(inside_kernel, shapes)(state, fine)
    late_b, late_a = kernel(late_kernel, [sds(LATE, NY)] * 2)(state, x_chip, x_core, inside[0])
    lb = lax.ppermute(late_b, "narrow", PAIR_B)
    la = lax.ppermute(late_a, "narrow", PAIR_A)
    own, fx12, fz12, known, scale12, dxy, rims, base, consts = kernel(
        edge_kernel,
        shapes + [sds(8, NY), sds(CX, CY), sds(*CONSTS.shape)],
        [pltpu.SemaphoreType.DMA],
        far=(5,),
        aliases={6 + i: i for i in range(6)},
    )(state, coarse, fine, x_chip, x_core, afar(jnp.asarray(CONSTS)), *inside)
    result, edges, spectral, lines = kernel(
        phase_kernel,
        [sds(2, NPL, BX, NY), sds(NPL, 2, 8, NY), sds(CX, CY), sds(16, NY)],
        [
            pltpu.VMEM((4, BX, NY), F32),
            pltpu.VMEM((4, BX + 16, NY), F32),
            pltpu.VMEM((NPL, BX + 16, NY), F32),
            pltpu.VMEM((2, BX, NY), F32),
            pltpu.VMEM((2, BX, NY), F32),
            pltpu.VMEM((2, BX, NY), F32),
            pltpu.VMEM((2, BX, NY), F32),
            pltpu.VMEM((CX, NY), F32),
            pltpu.VMEM((NPL, BX, NY), F32),
            pltpu.SemaphoreType.DMA((BX // 8,)),
        ],
        far_outs=(0,),
    )(coarse, own, fine, fx12, fz12, known, scale12, dxy, zb, za, base, consts)
    tiles, spectral, far = kernel(
        rim_kernel, [sds(NPL, 2, 8, NY), sds(CX, CY), sds(8, CY)]
    )(own, rims, x_chip, x_core, zb, za, lb, la, edges, spectral, lines, consts)
    partner = lax.ppermute(spectral, "wide", CORES)
    shared = lax.ppermute(far, "wide", NEXT_CHIPS)
    here, message = kernel(chip_kernel, [sds(2 * CX, CY), sds(CX + 8, CY)])(spectral, partner)
    across = lax.ppermute(message, "wide", CHIPS)
    view = kernel(window_kernel, sds(56, CY))(here, across, shared)
    planes = lax.all_to_all(jnp.broadcast_to(view[None], (NNAR, 56, CY)), "narrow", 0, 0)
    state_new = kernel(
        solute_kernel,
        sds(2, NPL, BX, NY),
        [
            pltpu.VMEM((NPL, BX + 16, NY), F32),
            pltpu.VMEM((NPL, BX, NY), F32),
            pltpu.VMEM((NPL, BX, NY), F32),
            pltpu.SemaphoreType.DMA((3 + BX // 8,)),
        ],
        far=(9,),
        far_outs=(0,),
        aliases={9: 0},
    )(state, own, x_chip, x_core, zb, za, lb, la, tiles, result)
    adjusted = kernel(
        solve_kernel,
        sds(1, CX, CY),
        [pltpu.VMEM((NNAR * 56, CY), F32), pltpu.VMEM((CX, CY), F32)],
    )(planes, coarse, consts)
    return state_new, adjusted


def solution(mesh):
    return jax.shard_map(
        on_device,
        mesh=mesh,
        in_specs=(
            P(None, "narrow", "wide", None),
            P("narrow", "wide", None),
            P("narrow", "wide", None),
            P("narrow", "wide", None),
            P(),
        ),
        out_specs=(P(None, "narrow", "wide", None), P("narrow", "wide", None)),
        check_vma=False,
    )
```

```python
import functools

import jax
import jax.numpy as jnp
import numpy as np
from jax import lax
from jax.experimental import pallas as pl
from jax.experimental.pallas import tpu as pltpu
from jax.sharding import PartitionSpec as P

F32 = jnp.float32
NNAR, NWIDE = 8, 32
NPL, BX, NY = 4, 64, 512
ROUGH, FACE, CORNERS, LATE = 128, 144, 64, 72
CX, CY = 16, 128
SUBX = 24
SIGMA, KBAR = 0.05, 0.75
DT = 0.15
VMEM = pl.BlockSpec(memory_space=pltpu.VMEM)
HBM = pl.BlockSpec(memory_space=pltpu.HBM)


def sds(*shape):
    return jax.ShapeDtypeStruct(shape, F32)


def params(mib):
    return pltpu.CompilerParams(vmem_limit_bytes=mib * 1024 * 1024)


def sine(points):
    k = np.arange(1, points + 1)
    return np.sqrt(2.0 / (points + 1)) * np.sin(np.pi * np.outer(k, k) / (points + 1))


def level(points):
    return 2.0 - 2.0 * np.cos(np.pi * np.arange(1, points + 1) / (points + 1))


SZ, SY = sine(8), sine(CY)
MEAN_Y = np.repeat(SY, 4, axis=0) / 64.0
SZ_ROWS = np.repeat(SZ[:, :, None], CY, 2)


def elimination():
    diag = SIGMA + KBAR * (level(8)[:, None] + level(CY)[None, :] + 2.0)
    inv = [1.0 / diag]
    for _ in range(SUBX - 1):
        inv.append(1.0 / (diag - KBAR * KBAR * inv[-1]))
    return np.stack(inv)


INVERSE = elimination()


LINK = KBAR * INVERSE
PASS = np.prod(LINK[4:20], axis=0)
MEET = 1.0 / (1.0 - LINK[11] ** 2)

CONSTS = np.concatenate(
    [SY, MEAN_Y, INVERSE.reshape(-1, CY), SZ_ROWS.reshape(-1, CY), PASS, MEET]
).astype(np.float32)
SY_AT, MEAN_AT, INV_AT, SZ_AT = slice(0, 128), slice(128, 640), 640, 640 + 8 * SUBX
PASS_AT = slice(SZ_AT + 64, SZ_AT + 72)
MEET_AT = slice(SZ_AT + 72, SZ_AT + 80)


def flat(n, w):
    return n * NWIDE + w


def everywhere(step):
    return [(flat(n, w), flat(*step(n, w))) for n in range(NNAR) for w in range(NWIDE)]


def swap_b(n, w):
    return (n, w ^ 1) if n in (0, NNAR - 1) else (((n + 1) ^ 1) - 1, w)


def swap_chips(n, w):
    return (n ^ 1, w) if w in (0, NWIDE - 1) else (n, ((w + 1) ^ 1) - 1)


def inward(n, w):
    to = w + 2 if w % 2 else w - 2
    return n, to if 0 <= to < NWIDE else w ^ 1


BOTH = ("narrow", "wide")
PAIR_A = [(i, i ^ 1) for i in range(NNAR)]
CORES = [(i, i ^ 1) for i in range(NWIDE)]
PAIR_B, CHIPS = everywhere(swap_b), everywhere(swap_chips)
INWARD = everywhere(inward)


def lanes(v):
    return lax.broadcasted_iota(jnp.int32, v.shape, v.ndim - 1)


def rows_of(v):
    return lax.broadcasted_iota(jnp.int32, v.shape, len(v.shape) - 2)


def y_up(v):
    n = v.shape[-1]
    return jnp.where(lanes(v) == n - 1, 0.0, pltpu.roll(v, n - 1, v.ndim - 1))


def y_down(v):
    return jnp.where(lanes(v) == 0, 0.0, pltpu.roll(v, 1, v.ndim - 1))


def x_up(v, after):
    return pltpu.roll(jnp.where(rows_of(v) == 0, after, v), 7, v.ndim - 2)


def x_down(v, before):
    return pltpu.roll(jnp.where(rows_of(v) == 7, before, v), 1, v.ndim - 2)


def inverse(v):
    guess = pl.reciprocal(v, approx=True)
    return guess * (2.0 - v * guess)


def weigh(dz, dx, dy, c2, s2):
    q0, a, b = dz * dz, dx * dx, dy * dy
    r = a + b
    uv = s2 * (b - a) + c2 * (dx * dy)
    num = q0 * q0 + r * r - 2.0 * (uv * uv)
    over = inverse(q0 + r + 4.0)
    return 0.55 + 0.6 * (num * (over * over))


def flag(cond):
    return jnp.where(cond, 1.0, 0.0).astype(F32)


def spread(v):
    lane = lax.shift_right_logical(lanes(v), 2)
    return jnp.concatenate(
        [jnp.take_along_axis(v, lane + 32 * j, axis=1) for j in range(NY // CY)], 1
    )


def halves(v):
    high = v.astype(jnp.bfloat16)
    return high, (v - high.astype(F32)).astype(jnp.bfloat16)


def dot(a, b):
    (a1, a2), (b1, b2) = halves(a), halves(b)
    mul = functools.partial(jnp.dot, preferred_element_type=F32)
    return mul(a1, b1) + (mul(a1, b2) + mul(a2, b1))


def stage_kernel(
    state_in, ids_in, frozen_in, temp_in, angles_in,
    face_b, face_a, x_chip, x_core, state, coarse,
    ids, frozen, temp, angles, sems,
):
    copies = [
        pltpu.make_async_copy(src, dst, sems.at[i])
        for i, (src, dst) in enumerate(
            [
                (state_in.at[0], state.at[0]),
                (state_in.at[1], state.at[1]),
                (ids_in, ids),
                (frozen_in, frozen),
                (temp_in, temp),
                (angles_in, angles),
            ]
        )
    ]
    for copy in copies:
        copy.start()
    for copy in copies[2:]:
        copy.wait()
    table = jnp.concatenate([angles[...], angles[...]], 1)
    c = jnp.take_along_axis(jnp.broadcast_to(jnp.cos(table), (CX, CY)), ids[0], axis=1)
    s = jnp.take_along_axis(jnp.broadcast_to(jnp.sin(table), (CX, CY)), ids[0], axis=1)
    coarse[0] = c * c - s * s
    coarse[1] = c * s
    coarse[2] = temp[0]
    coarse[3] = -0.5 * frozen[0].astype(F32)
    for copy in copies[:2]:
        copy.wait()
    even = lax.rem(lax.axis_index("narrow"), 2) == 0
    for ref, top in ((face_b, jnp.logical_not(even)), (face_a, even)):
        first = jnp.where(top, 2, 0)
        ref[0:BX] = state[0, first]
        ref[BX : 2 * BX] = state[0, first + 1]
        for k in range(4):
            ref[ROUGH:FACE, k * CY : (k + 1) * CY] = coarse[k]
    core0 = lax.rem(lax.axis_index("wide"), 2) == 0
    for ref, low in ((x_chip, core0), (x_core, jnp.logical_not(core0))):
        for z in range(NPL):
            for at, ch, first, last in ((0, 0, 0, BX - 1), (4, 0, 1, BX - 2), (8, 1, 0, BX - 1)):
                ref[at + z : at + z + 1] = jnp.where(
                    low, state[ch, z, first : first + 1], state[ch, z, last : last + 1]
                )
        for k in range(4):
            ref[12:13, k * CY : (k + 1) * CY] = jnp.where(
                low, coarse[k, 0:1], coarse[k, CX - 1 : CX]
            )
        ref[13:16] = jnp.zeros((3, NY), F32)


def x_sides(x_chip, x_core, rows):
    w = lax.axis_index("wide")
    core0 = lax.rem(w, 2) == 0
    left = jnp.where(core0, x_chip[rows], x_core[rows]) * flag(w > 0)
    right = jnp.where(core0, x_core[rows], x_chip[rows]) * flag(w < NWIDE - 1)
    return left, right


def late_kernel(state, x_chip, x_core, own, late_b, late_a):
    even = lax.rem(lax.axis_index("narrow"), 2) == 0
    left, right = x_sides(x_chip, x_core, slice(0, 8))
    for ref, top in ((late_b, jnp.logical_not(even)), (late_a, even)):
        ref[0:BX] = state[1, jnp.where(top, 3, 0)]
        ref[CORNERS : CORNERS + 1] = jnp.where(top, left[3:4], left[0:1])
        ref[CORNERS + 1 : CORNERS + 2] = jnp.where(top, right[3:4], right[0:1])
        ref[CORNERS + 2 : LATE] = jnp.zeros((LATE - CORNERS - 2, NY), F32)


def widen(ref, at, rough):
    for k in range(CX):
        ref[at, 4 * k : 4 * k + 4] = jnp.broadcast_to(rough[k : k + 1], (4, NY))


def spread_kernel(coarse, fine):
    for k in range(3):
        widen(fine, k, spread(coarse[k]))


def local_terms(c, state, own, fine, fx, fz, known, scale, dxy):
    r0 = 8 * c
    here, at, after = pl.ds(r0, 8), pl.ds(r0 + 8, 8), pl.ds(r0 + 16, 8)
    for z in range(NPL):
        v = own[z, at]
        dx = x_up(v, own[z, after]) - x_down(v, own[z, here])
        dy = y_up(v) - y_down(v)
        m = 1.0 - v * v
        drive = m * (v - 1.5 * (state[1, z, here] + fine[2, here]) * m)
        if z in (0, NPL - 1):
            known[z, here] = drive
            dxy[z // 2, 0, here] = dx
            dxy[z // 2, 1, here] = dy
            continue
        dz = own[z + 1, at] - own[z - 1, at]
        an = weigh(dz, dx, dy, fine[0, here], fine[1, here])
        wt = an * an
        quarter = 0.25 * wt
        fz[z - 1, here] = quarter * dz
        fx[z - 1, here] = quarter * dx
        fy = quarter * dy
        known[z, here] = (y_up(fy) - y_down(fy)) + drive
        scale[z - 1, here] = DT * inverse(wt)


def inside_kernel(state, fine, consts_in, own, fx, fz, known, scale, dxy, consts, sem):
    fetch = pltpu.make_async_copy(consts_in, consts, sem)
    fetch.start()
    for z in range(NPL):
        own[z, 8 : 8 + BX] = state[0, z]

    def chunk(c, carry):
        local_terms(c, state, own, fine, fx, fz, known, scale, dxy)
        return carry

    for c in range(1, BX // 8 - 1):
        chunk(c, 0)
    fetch.wait()


def edge_kernel(
    state, coarse, fine, x_chip, x_core, own_in, fx_in, fz_in, known_in, scale_in, dxy_in,
    own, fx, fz, known, scale, dxy, rims, base,
):
    left, right = x_sides(x_chip, x_core, slice(0, 4))
    for z in range(NPL):
        own[z, 7:8] = left[z : z + 1]
        own[z, 8 + BX : 9 + BX] = right[z : z + 1]
    left, right = x_sides(x_chip, x_core, slice(12, 13))
    rows = [side[:, k * CY : (k + 1) * CY] for side in (left, right) for k in (0, 1)]
    rims[...] = spread(jnp.concatenate(rows + rows, 0))
    for c in (0, BX // 8 - 1):
        local_terms(c, state, own, fine, fx, fz, known, scale, dxy)
    t, e = coarse[2], coarse[3]
    row = rows_of(t)
    down, up = [], []
    for k, v in ((2, t), (3, e)):
        before, after = left[:, k * CY : (k + 1) * CY], right[:, k * CY : (k + 1) * CY]
        down.append(jnp.where(row == 0, before, pltpu.roll(v, 1, 0)))
        up.append(jnp.where(row == CX - 1, after, pltpu.roll(v, CX - 1, 0)))
    near = [tuple(down), tuple(up), (y_up(t), y_up(e)), (y_down(t), y_down(e))]
    total = jnp.zeros_like(t)
    for tn, en in near:
        total = total + (1.0 + 0.5 * (e + en)) * (tn - t)
    base[...] = total


def phase_kernel(
    coarse, own, fine, fx12, fz12, known, scale12, dxy, zb, za, base, consts,
    out, edges, spectral, lines,
    sides, halo, fx, fz03, fzout, bent, scale03, change, fresh, sems,
):
    n = lax.axis_index("narrow")
    even = lax.rem(n, 2) == 0
    has_low, has_high = flag(n > 0), flag(n < NNAR - 1)
    for face, at, there in (
        (zb, jnp.where(even, 0, 2), jnp.where(even, has_low, has_high)),
        (za, jnp.where(even, 2, 0), jnp.where(even, has_high, has_low)),
    ):
        for k in range(2):
            halo[at + k, 8 : 8 + BX] = face[k * BX : (k + 1) * BX] * there
    low = jnp.where(even, zb[ROUGH:FACE], za[ROUGH:FACE])
    high = jnp.where(even, za[ROUGH:FACE], zb[ROUGH:FACE])
    for k, v in enumerate((low, low, high, high)):
        wide = spread(v[:, (k % 2) * CY : (k % 2 + 1) * CY])
        widen(sides, k, wide)
        lines[8 + 4 * (k % 2) + 2 * (k // 2) : 9 + 4 * (k % 2) + 2 * (k // 2)] = wide[0:1]
        lines[9 + 4 * (k % 2) + 2 * (k // 2) : 10 + 4 * (k % 2) + 2 * (k // 2)] = wide[CX - 1 : CX]
    t, e = coarse[2], coarse[3]
    still = base[...]
    for v, there in ((low, has_low), (high, has_high)):
        tn, en = v[:, 2 * CY : 3 * CY] * there, v[:, 3 * CY :] * there
        still = still + (1.0 + 0.5 * (e + en)) * (tn - t)
    for z in range(NPL):
        fx[z, 7:8] = jnp.zeros((1, NY), F32)
        fx[z, 8 + BX : 9 + BX] = jnp.zeros((1, NY), F32)
    for z in (1, 2):
        fx[z, 8 : 8 + BX] = fx12[z - 1]
    planes = [(halo, 0), (halo, 1), (own, 0), (own, 1), (own, 2), (own, 3), (halo, 2), (halo, 3)]

    def get(k, rows):
        ref, z = planes[k]
        return ref[z, rows]

    def fluxes(c, carry):
        r0 = 8 * c
        here, at, after = pl.ds(r0, 8), pl.ds(r0 + 8, 8), pl.ds(r0 + 16, 8)
        for side, (zz, there) in enumerate(((0, has_low), (5, has_high))):
            v = get(zz + 1, at)
            dz = get(zz + 2, at) - get(zz, at)
            dx = x_up(v, get(zz + 1, after)) - x_down(v, get(zz + 1, here))
            dy = y_up(v) - y_down(v)
            an = weigh(dz, dx, dy, sides[2 * side, here], sides[2 * side + 1, here])
            fzout[side, here] = (0.25 * there) * (an * an * dz)
        for side, z in enumerate((0, NPL - 1)):
            dz = get(z + 3, at) - get(z + 1, at)
            dx, dy = dxy[side, 0, here], dxy[side, 1, here]
            an = weigh(dz, dx, dy, fine[0, here], fine[1, here])
            wt = an * an
            quarter = 0.25 * wt
            fz03[side, here] = quarter * dz
            fx[z, at] = quarter * dx
            fy = quarter * dy
            bent[side, here] = known[z, here] + (y_up(fy) - y_down(fy))
            scale03[side, here] = DT * inverse(wt)
        return carry

    for c in range(BX // 8):
        fluxes(c, 0)

    for side in range(2):
        for row in (0, BX - 1):
            fzout[side, row : row + 1] = jnp.zeros((1, NY), F32)
    flux_z = [(fzout, 0), (fz03, 0), (fz12, 0), (fz12, 1), (fz03, 1), (fzout, 1)]
    rest = [(bent, 0), (known, 1), (known, 2), (bent, 1)]
    scales = [(scale03, 0), (scale12, 0), (scale12, 1), (scale03, 1)]

    def store(c):
        rows = pl.ds(8 * c, 8)
        return pltpu.make_async_copy(fresh.at[:, rows], out.at[0, :, rows], sems.at[c])

    for c in range(BX // 8):
        here, at, after = pl.ds(8 * c, 8), pl.ds(8 * c + 8, 8), pl.ds(8 * c + 16, 8)
        total = jnp.zeros((8, NY), F32)
        for z in range(NPL):
            p, f = own[z, at], fx[z, at]
            spread_z = flux_z[z + 2][0][flux_z[z + 2][1], here] - flux_z[z][0][flux_z[z][1], here]
            spread_x = x_up(f, fx[z, after]) - x_down(f, fx[z, here])
            factor = scales[z][0][scales[z][1], here]
            rise = factor * (rest[z][0][rest[z][1], here] + spread_z + spread_x)
            total = total + rise
            if c in (0, BX // 8 - 1):
                edges[z, 0 if c == 0 else 1] = p + rise
                row, line = (0, z) if c == 0 else (7, NPL + z)
                lines[line : line + 1] = factor[row : row + 1]
            else:
                fresh[z, here] = p + rise
        total = total + pltpu.roll(total, 1, 0)
        total = total + pltpu.roll(total, 2, 0)
        change[2 * c : 2 * c + 1] = total[3:4]
        change[2 * c + 1 : 2 * c + 2] = total[7:8]
        if 0 < c < BX // 8 - 1:
            store(c).start()
    spectral[...] = dot(still, consts[SY_AT]) + dot(change[...], consts[MEAN_AT])
    for c in range(1, BX // 8 - 1):
        store(c).wait()


def rim_kernel(
    own, rims, x_chip, x_core, zb, za, lb, la, edges, spectral_in, lines, consts,
    tiles, spectral,
):
    n, w = lax.axis_index("narrow"), lax.axis_index("wide")
    even = lax.rem(n, 2) == 0
    has_left, has_right = flag(w > 0), flag(w < NWIDE - 1)
    has_low, has_high = flag(n > 0), flag(n < NNAR - 1)
    inner = x_sides(x_chip, x_core, slice(4, 8))

    def beyond(b, a, rows, high):
        if high:
            return jnp.where(even, a[rows], b[rows]) * has_high
        return jnp.where(even, b[rows], a[rows]) * has_low

    def corner(high, s):
        return beyond(lb, la, slice(CORNERS + s, CORNERS + s + 1), high)

    def outer(high, plane, x):
        return beyond(zb, za, slice(plane * BX + x, plane * BX + x + 1), high)

    rim = (7, 8 + BX)
    values = [[], [], [], [], []]
    for s in range(2):
        for z in range(NPL):
            at = slice(rim[s], rim[s] + 1)
            here = own[z, at]
            below = own[z - 1, at] if z > 0 else corner(False, s)
            above = own[z + 1, at] if z < NPL - 1 else corner(True, s)
            side = inner[s][z : z + 1]
            x_lo, x_hi = (own[z, 7 + BX : 8 + BX], side) if s else (side, own[z, 8:9])
            for rows, v in zip(values, (here, below, above, x_lo, x_hi)):
                rows.append(v)
    for high in (False, True):
        for s in range(2):
            x, near = (BX - 1, BX - 2) if s else (0, 1)
            mine = own[NPL - 1 if high else 0, 8 + x : 9 + x]
            here, behind = outer(high, 0 if high else 1, x), outer(high, 1 if high else 0, x)
            beside, past = outer(high, 0 if high else 1, near), corner(high, s)
            below, above = (mine, behind) if high else (behind, mine)
            x_lo, x_hi = (beside, past) if s else (past, beside)
            for rows, v in zip(values, (here, below, above, x_lo, x_hi)):
                rows.append(v)
    here, below, above, x_lo, x_hi = (
        jnp.concatenate(rows + [jnp.zeros((4, NY), F32)], 0) for rows in values
    )
    c2, s2 = (
        jnp.concatenate(
            [jnp.broadcast_to(rims[k : k + 1], (NPL, NY)), jnp.broadcast_to(rims[k + 2 : k + 3], (NPL, NY)),
             lines[8 + 4 * k : 12 + 4 * k], jnp.zeros((4, NY), F32)], 0,
        )
        for k in (0, 1)
    )
    dz, dx, dy = above - below, x_hi - x_lo, y_up(here) - y_down(here)
    an = weigh(dz, dx, dy, c2, s2)
    quarter = 0.25 * (an * an)
    row = rows_of(here[0:8])
    x_part = quarter[0:8] * dx[0:8] * jnp.where(row < NPL, -has_left, has_right)
    z_flux = quarter[8:16] * dz[8:16]
    z_part = jnp.zeros((8, NY), F32)
    for high in (False, True):
        for s in range(2):
            line = z_flux[2 * high + s : 2 * high + s + 1]
            line = line * has_high if high else -has_low * line
            z_part = jnp.where(row == NPL * s + (NPL - 1 if high else 0), line, z_part)
    rise = lines[0:8] * (x_part + z_part)
    for c in range(2):
        for z in range(NPL):
            add = rise[NPL * c + z : NPL * c + z + 1]
            tiles[z, c] = edges[z, c] + jnp.where(row == 7 * c, add, 0.0)
    sums = [jnp.sum(rise[NPL * c : NPL * (c + 1)], axis=0, keepdims=True) for c in range(2)]
    more = dot(jnp.concatenate(sums + [jnp.zeros((14, NY), F32)], 0), consts[MEAN_AT])
    first = rows_of(spectral_in)
    moved = spectral_in[...] + jnp.where(
        first == 0, more[0:1], jnp.where(first == CX - 1, more[1:2], 0.0)
    )
    spectral[...] = moved


def solute_kernel(state, own, x_chip, x_core, zb, za, lb, la, tiles, done, out, sown, fresh, grown, sems):
    within = pl.ds(8, BX - 16)
    fetch = pltpu.make_async_copy(done.at[0, :, within], fresh.at[:, within], sems.at[0])
    fetch.start()
    ends = [
        pltpu.make_async_copy(tiles.at[:, c], out.at[0, :, pl.ds((BX - 8) * c, 8)], sems.at[9 + c])
        for c in range(2)
    ]
    for copy in ends:
        copy.start()
    for c in range(2):
        fresh[:, (BX - 8) * c : (BX - 8) * c + 8] = tiles[:, c]
    n = lax.axis_index("narrow")
    even = lax.rem(n, 2) == 0
    left, right = x_sides(x_chip, x_core, slice(8, 12))
    has_low, has_high = flag(n > 0), flag(n < NNAR - 1)
    for z in range(NPL):
        sown[z, 8 : 8 + BX] = state[1, z]
        sown[z, 7:8] = left[z : z + 1]
        sown[z, 8 + BX : 9 + BX] = right[z : z + 1]
    fetch.wait()

    def step(c):
        r0 = 8 * c
        here, at, after = pl.ds(r0, 8), pl.ds(r0 + 8, 8), pl.ds(r0 + 16, 8)

        beyond = pl.ds(r0 + BX, 8)
        ps = (
            [has_low * jnp.where(even, zb[beyond], za[beyond])]
            + [own[z, at] for z in range(NPL)]
            + [has_high * jnp.where(even, za[here], zb[here])]
        )
        ss = (
            [has_low * jnp.where(even, lb[here], la[here])]
            + [sown[z, at] for z in range(NPL)]
            + [has_high * jnp.where(even, la[here], lb[here])]
        )
        for z in range(NPL):
            p, s = ps[z + 1], ss[z + 1]
            q = 0.55 - 0.25 * p
            near = [
                (ps[z], ss[z]),
                (ps[z + 2], ss[z + 2]),
                (x_up(p, own[z, after]), x_up(s, sown[z, after])),
                (x_down(p, own[z, here]), x_down(s, sown[z, here])),
                (y_up(p), y_up(s)),
                (y_down(p), y_down(s)),
            ]
            total = jnp.zeros_like(p)
            for pn, sn in near:
                total = total + (q - 0.25 * pn) * (sn - s)
            grown[z, here] = s + DT * total + (0.5 + 0.425 * s) * (fresh[z, here] - p)
        store(c).start()

    def store(c):
        rows = pl.ds(8 * c, 8)
        return pltpu.make_async_copy(grown.at[:, rows], out.at[1, :, rows], sems.at[1 + c])

    for c in range(BX // 8):
        step(c)
    for c in range(BX // 8):
        store(c).wait()
    for copy in ends:
        copy.wait()


def eliminate(state, f, consts, first):
    states = []
    for i, v in enumerate(f):
        inv = consts[INV_AT + 8 * (first + i) : INV_AT + 8 * (first + i) + 8]
        state = inv * v if state is None else inv * v + (KBAR * inv) * state
        states.append(state)
    return states


def back(x, states, consts, first):
    values = []
    for i in range(len(states) - 1, -1, -1):
        inv = consts[INV_AT + 8 * (first + i) : INV_AT + 8 * (first + i) + 8]
        x = states[i] + (KBAR * inv) * x
        values.append(x)
    return values[::-1]


def mode_kernel(planes, consts, f, to_chip, to_core, to_next, modes):
    half = NNAR // 2
    folded = [
        [planes[m] + planes[NNAR - 1 - m] for m in range(half)],
        [planes[m] - planes[NNAR - 1 - m] for m in range(half)],
    ]
    for k in range(NNAR):
        total = float(SZ[k, 0]) * folded[k % 2][0]
        for m in range(1, half):
            total = total + float(SZ[k, m]) * folded[k % 2][m]
        modes[k * CX : (k + 1) * CX] = total
    values = [modes[pl.ds(j, 8, stride=CX), :] for j in range(CX)]
    for j in range(CX):
        f[j] = values[j]
    mirrored = values[::-1]
    right_margin = eliminate(None, values[12:], consts, 0)[-1]
    left_margin = eliminate(None, mirrored[12:], consts, 0)[-1]
    right_core = eliminate(None, values, consts, 4)[-1]
    left_core = eliminate(None, mirrored, consts, 4)[-1]
    core0 = lax.rem(lax.axis_index("wide"), 2) == 0
    to_core[0:8] = jnp.where(core0, right_margin, left_margin)
    to_core[8:16] = jnp.where(core0, right_core, left_core)
    to_chip[0:8] = jnp.where(core0, left_margin, right_margin)
    to_chip[8:16] = jnp.where(core0, left_core, right_core)
    to_next[...] = to_chip[0:8]


def pass_kernel(to_chip, by_core, consts, message):
    message[0:8] = to_chip[0:8]
    message[8:16] = to_chip[8:16] + consts[PASS_AT] * by_core[0:8]


def solve_kernel(f, by_chip, by_core, by_next, coarse, consts, out, rows):
    n, w = lax.axis_index("narrow"), lax.axis_index("wide")
    core0 = lax.rem(w, 2) == 0
    has_left, has_right = flag(w > 0), flag(w < NWIDE - 1)
    beyond = consts[PASS_AT] * by_next[...] * jnp.where(core0, flag(w < NWIDE - 2), flag(w > 1))
    other = jnp.concatenate([by_core[0:8], by_core[8:16] + beyond], 0)
    left = jnp.where(core0, by_chip[...], other) * has_left
    right = jnp.where(core0, other, by_chip[...]) * has_right
    values = [f[j] for j in range(CX)]
    mirrored = values[::-1]
    half = CX // 2

    low = eliminate(left[0:8], values[:half], consts, 4)
    high = eliminate(right[0:8], mirrored[:half], consts, 4)
    link = KBAR * consts[INV_AT + 8 * 11 : INV_AT + 8 * 12]
    x_low = consts[MEET_AT] * (low[-1] + link * high[-1])
    x_high = consts[MEET_AT] * (high[-1] + link * low[-1])
    x = back(x_low, low[:-1], consts, 4) + [x_low]
    x += (back(x_high, high[:-1], consts, 4) + [x_high])[::-1]

    for here, near, there in (
        (range(4), left, has_left),
        (range(CX - 1, CX - 5, -1), right, has_right),
    ):
        states = eliminate(near[8:16], [values[j] for j in here], consts, 20)
        found = back(states[-1], states[:-1], consts, 20) + [states[-1]]
        for j, v in zip(here, found):
            x[j] = x[j] + there * v

    weight = consts[pl.ds(pl.multiple_of(SZ_AT + 8 * n, 8), 8)]
    for j in range(CX):
        rows[j : j + 1] = jnp.sum(x[j] * weight, axis=0, keepdims=True)
    out[0] = coarse[2] + dot(rows[...], consts[SY_AT])


def kernel(body, outs, scratch=(), far=(), far_outs=(), aliases=None, mib=16):
    many = isinstance(outs, (list, tuple))

    def call(*args):
        return pl.pallas_call(
            body,
            out_shape=outs,
            in_specs=[HBM if i in far else VMEM for i in range(len(args))],
            out_specs=[HBM if i in far_outs else VMEM for i in range(len(outs))] if many else (HBM if far_outs else VMEM),
            input_output_aliases=aliases or {},
            scratch_shapes=list(scratch),
            compiler_params=params(mib),
            name=body.__name__,
        )(*args)

    return call


def afar(v):
    return pltpu.with_memory_space_constraint(v, pltpu.HBM)


def on_device(state_in, ids, frozen, temp, angles):
    inputs = [afar(v) for v in (state_in, ids, frozen, temp, angles.reshape(1, -1))]
    face_b, face_a, to_chip, to_core, state, coarse = kernel(
        stage_kernel,
        [sds(FACE, NY)] * 2 + [sds(16, NY)] * 2 + [sds(2, NPL, BX, NY), sds(4, CX, CY)],
        [
            pltpu.VMEM((1, CX, CY), jnp.int32),
            pltpu.VMEM((1, CX, CY), jnp.int32),
            pltpu.VMEM((1, CX, CY), F32),
            pltpu.VMEM((1, 64), F32),
            pltpu.SemaphoreType.DMA((6,)),
        ],
        far=range(5),
    )(*inputs)
    zb = lax.ppermute(face_b, BOTH, PAIR_B)
    za = lax.ppermute(face_a, "narrow", PAIR_A)
    x_chip = lax.ppermute(to_chip, BOTH, CHIPS)
    x_core = lax.ppermute(to_core, "wide", CORES)
    fine = kernel(spread_kernel, sds(3, BX, NY))(coarse)
    shapes = [
        sds(NPL, BX + 16, NY), sds(2, BX, NY), sds(2, BX, NY), sds(NPL, BX, NY), sds(2, BX, NY),
        sds(2, 2, BX, NY),
    ]
    *inside, consts = kernel(
        inside_kernel, shapes + [sds(*CONSTS.shape)], [pltpu.SemaphoreType.DMA], far=(2,)
    )(state, fine, afar(jnp.asarray(CONSTS)))
    late_b, late_a = kernel(late_kernel, [sds(LATE, NY)] * 2)(state, x_chip, x_core, inside[0])
    lb = lax.ppermute(late_b, BOTH, PAIR_B)
    la = lax.ppermute(late_a, "narrow", PAIR_A)
    own, fx12, fz12, known, scale12, dxy, rims, base = kernel(
        edge_kernel,
        shapes + [sds(8, NY), sds(CX, CY)],
        aliases={5 + i: i for i in range(6)},
    )(state, coarse, fine, x_chip, x_core, *inside)
    result, edges, spectral, lines = kernel(
        phase_kernel,
        [sds(2, NPL, BX, NY), sds(NPL, 2, 8, NY), sds(CX, CY), sds(16, NY)],
        [
            pltpu.VMEM((4, BX, NY), F32),
            pltpu.VMEM((4, BX + 16, NY), F32),
            pltpu.VMEM((NPL, BX + 16, NY), F32),
            pltpu.VMEM((2, BX, NY), F32),
            pltpu.VMEM((2, BX, NY), F32),
            pltpu.VMEM((2, BX, NY), F32),
            pltpu.VMEM((2, BX, NY), F32),
            pltpu.VMEM((CX, NY), F32),
            pltpu.VMEM((NPL, BX, NY), F32),
            pltpu.SemaphoreType.DMA((BX // 8,)),
        ],
        far_outs=(0,),
    )(coarse, own, fine, fx12, fz12, known, scale12, dxy, zb, za, base, consts)
    tiles, spectral = kernel(rim_kernel, [sds(NPL, 2, 8, NY), sds(CX, CY)])(
        own, rims, x_chip, x_core, zb, za, lb, la, edges, spectral, lines, consts
    )
    planes = lax.all_to_all(jnp.broadcast_to(spectral[None], (NNAR, CX, CY)), "narrow", 0, 0)
    state_new = kernel(
        solute_kernel,
        sds(2, NPL, BX, NY),
        [
            pltpu.VMEM((NPL, BX + 16, NY), F32),
            pltpu.VMEM((NPL, BX, NY), F32),
            pltpu.VMEM((NPL, BX, NY), F32),
            pltpu.SemaphoreType.DMA((3 + BX // 8,)),
        ],
        far=(9,),
        far_outs=(0,),
        aliases={9: 0},
    )(state, own, x_chip, x_core, zb, za, lb, la, tiles, result)
    f, to_chip, to_core, to_next = kernel(
        mode_kernel,
        [sds(CX, 8, CY), sds(16, CY), sds(16, CY), sds(8, CY)],
        [pltpu.VMEM((NNAR * CX, CY), F32)],
    )(planes, consts)
    by_core = lax.ppermute(to_core, "wide", CORES)
    by_next = lax.ppermute(to_next, BOTH, INWARD)
    by_chip = lax.ppermute(kernel(pass_kernel, sds(16, CY))(to_chip, by_core, consts), BOTH, CHIPS)
    adjusted = kernel(solve_kernel, sds(1, CX, CY), [pltpu.VMEM((CX, CY), F32)])(
        f, by_chip, by_core, by_next, coarse, consts
    )
    return state_new, adjusted


def solution(mesh):
    return jax.shard_map(
        on_device,
        mesh=mesh,
        in_specs=(
            P(None, "narrow", "wide", None),
            P("narrow", "wide", None),
            P("narrow", "wide", None),
            P("narrow", "wide", None),
            P(),
        ),
        out_specs=(P(None, "narrow", "wide", None), P("narrow", "wide", None)),
        check_vma=False,
    )
```

```python
import functools

import jax
import jax.numpy as jnp
import numpy as np
from jax import lax
from jax.experimental import pallas as pl
from jax.experimental.pallas import tpu as pltpu
from jax.sharding import PartitionSpec as P

F32 = jnp.float32
NNAR, NWIDE = 8, 32
NPL, BX, NY = 4, 64, 512
SPLIT = 24
ROUGH, EARLY, FACE = 128, 144, 144 + SPLIT
CORNERS, LATE = 64 - SPLIT, 72 - SPLIT
CX, CY = 16, 128
SUBX = 24
SIGMA, KBAR = 0.05, 0.75
DT = 0.15
VMEM = pl.BlockSpec(memory_space=pltpu.VMEM)
HBM = pl.BlockSpec(memory_space=pltpu.HBM)


def sds(*shape):
    return jax.ShapeDtypeStruct(shape, F32)


def params(mib):
    return pltpu.CompilerParams(vmem_limit_bytes=mib * 1024 * 1024)


def sine(points):
    k = np.arange(1, points + 1)
    return np.sqrt(2.0 / (points + 1)) * np.sin(np.pi * np.outer(k, k) / (points + 1))


def level(points):
    return 2.0 - 2.0 * np.cos(np.pi * np.arange(1, points + 1) / (points + 1))


SZ, SY = sine(8), sine(CY)
MEAN_Y = np.repeat(SY, 4, axis=0) / 64.0
SZ_ROWS = np.repeat(SZ[:, :, None], CY, 2)


def elimination():
    diag = SIGMA + KBAR * (level(8)[:, None] + level(CY)[None, :] + 2.0)
    inv = [1.0 / diag]
    for _ in range(SUBX - 1):
        inv.append(1.0 / (diag - KBAR * KBAR * inv[-1]))
    return np.stack(inv)


INVERSE = elimination()


LINK = KBAR * INVERSE
PASS = np.prod(LINK[4:20], axis=0)
MEET = 1.0 / (1.0 - LINK[11] ** 2)

CONSTS = np.concatenate(
    [SY, MEAN_Y, INVERSE.reshape(-1, CY), SZ_ROWS.reshape(-1, CY), PASS, MEET]
).astype(np.float32)
SY_AT, MEAN_AT, INV_AT, SZ_AT = slice(0, 128), slice(128, 640), 640, 640 + 8 * SUBX
PASS_AT = slice(SZ_AT + 64, SZ_AT + 72)
MEET_AT = slice(SZ_AT + 72, SZ_AT + 80)


def flat(n, w):
    return n * NWIDE + w


def everywhere(step):
    return [(flat(n, w), flat(*step(n, w))) for n in range(NNAR) for w in range(NWIDE)]


def swap_b(n, w):
    return (n, w ^ 1) if n in (0, NNAR - 1) else (((n + 1) ^ 1) - 1, w)


def swap_chips(n, w):
    if w in (0, NWIDE - 1):
        return (n ^ 4, w) if n % 4 in (1, 2) else (n, NWIDE - 1 - w)
    return n, ((w + 1) ^ 1) - 1


def inward(n, w):
    to = w + 2 if w % 2 else w - 2
    return n, to if 0 <= to < NWIDE else w ^ 1


BOTH = ("narrow", "wide")
PAIR_A = [(i, i ^ 1) for i in range(NNAR)]
CORES = [(i, i ^ 1) for i in range(NWIDE)]
PAIR_B, CHIPS = everywhere(swap_b), everywhere(swap_chips)
INWARD = everywhere(inward)


def lanes(v):
    return lax.broadcasted_iota(jnp.int32, v.shape, v.ndim - 1)


def rows_of(v):
    return lax.broadcasted_iota(jnp.int32, v.shape, len(v.shape) - 2)


def y_up(v):
    n = v.shape[-1]
    return jnp.where(lanes(v) == n - 1, 0.0, pltpu.roll(v, n - 1, v.ndim - 1))


def y_down(v):
    return jnp.where(lanes(v) == 0, 0.0, pltpu.roll(v, 1, v.ndim - 1))


def x_up(v, after):
    return pltpu.roll(jnp.where(rows_of(v) == 0, after, v), 7, v.ndim - 2)


def x_down(v, before):
    return pltpu.roll(jnp.where(rows_of(v) == 7, before, v), 1, v.ndim - 2)


def inverse(v):
    guess = pl.reciprocal(v, approx=True)
    return guess * (2.0 - v * guess)


def weigh(dz, dx, dy, c2, s2):
    q0, a, b = dz * dz, dx * dx, dy * dy
    r = a + b
    uv = s2 * (b - a) + c2 * (dx * dy)
    num = q0 * q0 + r * r - 2.0 * (uv * uv)
    over = inverse(q0 + r + 4.0)
    return 0.55 + 0.6 * (num * (over * over))


def flag(cond):
    return jnp.where(cond, 1.0, 0.0).astype(F32)


def spread(v):
    lane = lax.shift_right_logical(lanes(v), 2)
    return jnp.concatenate(
        [jnp.take_along_axis(v, lane + 32 * j, axis=1) for j in range(NY // CY)], 1
    )


def halves(v):
    high = v.astype(jnp.bfloat16)
    return high, (v - high.astype(F32)).astype(jnp.bfloat16)


def dot(a, b):
    (a1, a2), (b1, b2) = halves(a), halves(b)
    mul = functools.partial(jnp.dot, preferred_element_type=F32)
    return mul(a1, b1) + (mul(a1, b2) + mul(a2, b1))


def stage_kernel(
    state_in, ids_in, frozen_in, temp_in, angles_in,
    face_b, face_a, x_chip, x_core, state, coarse,
    ids, frozen, temp, angles, sems,
):
    copies = [
        pltpu.make_async_copy(src, dst, sems.at[i])
        for i, (src, dst) in enumerate(
            [
                (state_in.at[0], state.at[0]),
                (state_in.at[1], state.at[1]),
                (ids_in, ids),
                (frozen_in, frozen),
                (temp_in, temp),
                (angles_in, angles),
            ]
        )
    ]
    for copy in copies:
        copy.start()
    for copy in copies[2:]:
        copy.wait()
    table = jnp.concatenate([angles[...], angles[...]], 1)
    c = jnp.take_along_axis(jnp.broadcast_to(jnp.cos(table), (CX, CY)), ids[0], axis=1)
    s = jnp.take_along_axis(jnp.broadcast_to(jnp.sin(table), (CX, CY)), ids[0], axis=1)
    coarse[0] = c * c - s * s
    coarse[1] = c * s
    coarse[2] = temp[0]
    coarse[3] = -0.5 * frozen[0].astype(F32)
    even = lax.rem(lax.axis_index("narrow"), 2) == 0
    for ref in (face_b, face_a):
        for k in range(4):
            ref[ROUGH:EARLY, k * CY : (k + 1) * CY] = coarse[k]
    copies[0].wait()
    for ref, top in ((face_b, jnp.logical_not(even)), (face_a, even)):
        first = jnp.where(top, 2, 0)
        ref[0:BX] = state[0, first]
        ref[BX : 2 * BX] = state[0, first + 1]
    copies[1].wait()
    for ref, top in ((face_b, jnp.logical_not(even)), (face_a, even)):
        ref[EARLY:FACE] = state[1, jnp.where(top, 3, 0), 0:SPLIT]
    core0 = lax.rem(lax.axis_index("wide"), 2) == 0
    for ref, low in ((x_chip, core0), (x_core, jnp.logical_not(core0))):
        for z in range(NPL):
            for at, ch, first, last in ((0, 0, 0, BX - 1), (4, 0, 1, BX - 2), (8, 1, 0, BX - 1)):
                ref[at + z : at + z + 1] = jnp.where(
                    low, state[ch, z, first : first + 1], state[ch, z, last : last + 1]
                )
        for k in range(4):
            ref[12:13, k * CY : (k + 1) * CY] = jnp.where(
                low, coarse[k, 0:1], coarse[k, CX - 1 : CX]
            )
        ref[13:16] = jnp.zeros((3, NY), F32)


def x_sides(x_chip, x_core, rows):
    w = lax.axis_index("wide")
    core0 = lax.rem(w, 2) == 0
    left = jnp.where(core0, x_chip[rows], x_core[rows]) * flag(w > 0)
    right = jnp.where(core0, x_core[rows], x_chip[rows]) * flag(w < NWIDE - 1)
    return left, right


def late_kernel(state, x_chip, x_core, own, late_b, late_a):
    even = lax.rem(lax.axis_index("narrow"), 2) == 0
    left, right = x_sides(x_chip, x_core, slice(0, 8))
    for ref, top in ((late_b, jnp.logical_not(even)), (late_a, even)):
        ref[0:CORNERS] = state[1, jnp.where(top, 3, 0), SPLIT:BX]
        ref[CORNERS : CORNERS + 1] = jnp.where(top, left[3:4], left[0:1])
        ref[CORNERS + 1 : CORNERS + 2] = jnp.where(top, right[3:4], right[0:1])
        ref[CORNERS + 2 : LATE] = jnp.zeros((LATE - CORNERS - 2, NY), F32)


def widen(ref, at, rough):
    for k in range(CX):
        ref[at, 4 * k : 4 * k + 4] = jnp.broadcast_to(rough[k : k + 1], (4, NY))


def spread_kernel(coarse, fine):
    for k in range(3):
        widen(fine, k, spread(coarse[k]))


def local_terms(c, state, own, fine, fx, fz, known, scale, dxy):
    r0 = 8 * c
    here, at, after = pl.ds(r0, 8), pl.ds(r0 + 8, 8), pl.ds(r0 + 16, 8)
    for z in range(NPL):
        v = own[z, at]
        dx = x_up(v, own[z, after]) - x_down(v, own[z, here])
        dy = y_up(v) - y_down(v)
        m = 1.0 - v * v
        drive = m * (v - 1.5 * (state[1, z, here] + fine[2, here]) * m)
        if z in (0, NPL - 1):
            known[z, here] = drive
            dxy[z // 2, 0, here] = dx
            dxy[z // 2, 1, here] = dy
            continue
        dz = own[z + 1, at] - own[z - 1, at]
        an = weigh(dz, dx, dy, fine[0, here], fine[1, here])
        wt = an * an
        quarter = 0.25 * wt
        fz[z - 1, here] = quarter * dz
        fx[z - 1, here] = quarter * dx
        fy = quarter * dy
        known[z, here] = (y_up(fy) - y_down(fy)) + drive
        scale[z - 1, here] = DT * inverse(wt)


def inside_kernel(state, fine, consts_in, own, fx, fz, known, scale, dxy, consts, sem):
    fetch = pltpu.make_async_copy(consts_in, consts, sem)
    fetch.start()
    for z in range(NPL):
        own[z, 8 : 8 + BX] = state[0, z]

    def chunk(c, carry):
        local_terms(c, state, own, fine, fx, fz, known, scale, dxy)
        return carry

    for c in range(1, BX // 8 - 1):
        chunk(c, 0)
    fetch.wait()


def edge_kernel(
    state, coarse, fine, x_chip, x_core, own_in, fx_in, fz_in, known_in, scale_in, dxy_in,
    own, fx, fz, known, scale, dxy, rims, base,
):
    left, right = x_sides(x_chip, x_core, slice(0, 4))
    for z in range(NPL):
        own[z, 7:8] = left[z : z + 1]
        own[z, 8 + BX : 9 + BX] = right[z : z + 1]
    left, right = x_sides(x_chip, x_core, slice(12, 13))
    rows = [side[:, k * CY : (k + 1) * CY] for side in (left, right) for k in (0, 1)]
    rims[...] = spread(jnp.concatenate(rows + rows, 0))
    for c in (0, BX // 8 - 1):
        local_terms(c, state, own, fine, fx, fz, known, scale, dxy)
    t, e = coarse[2], coarse[3]
    row = rows_of(t)
    down, up = [], []
    for k, v in ((2, t), (3, e)):
        before, after = left[:, k * CY : (k + 1) * CY], right[:, k * CY : (k + 1) * CY]
        down.append(jnp.where(row == 0, before, pltpu.roll(v, 1, 0)))
        up.append(jnp.where(row == CX - 1, after, pltpu.roll(v, CX - 1, 0)))
    near = [tuple(down), tuple(up), (y_up(t), y_up(e)), (y_down(t), y_down(e))]
    total = jnp.zeros_like(t)
    for tn, en in near:
        total = total + (1.0 + 0.5 * (e + en)) * (tn - t)
    base[...] = total


def phase_kernel(
    coarse, own, fine, fx12, fz12, known, scale12, dxy, zb, za, base, consts,
    fresh, spectral, lines,
    sides, halo, fx, fz03, fzout, bent, scale03, change,
):
    n = lax.axis_index("narrow")
    even = lax.rem(n, 2) == 0
    has_low, has_high = flag(n > 0), flag(n < NNAR - 1)
    for face, at, there in (
        (zb, jnp.where(even, 0, 2), jnp.where(even, has_low, has_high)),
        (za, jnp.where(even, 2, 0), jnp.where(even, has_high, has_low)),
    ):
        for k in range(2):
            halo[at + k, 8 : 8 + BX] = face[k * BX : (k + 1) * BX] * there
    low = jnp.where(even, zb[ROUGH:EARLY], za[ROUGH:EARLY])
    high = jnp.where(even, za[ROUGH:EARLY], zb[ROUGH:EARLY])
    for k, v in enumerate((low, low, high, high)):
        wide = spread(v[:, (k % 2) * CY : (k % 2 + 1) * CY])
        widen(sides, k, wide)
        lines[8 + 4 * (k % 2) + 2 * (k // 2) : 9 + 4 * (k % 2) + 2 * (k // 2)] = wide[0:1]
        lines[9 + 4 * (k % 2) + 2 * (k // 2) : 10 + 4 * (k % 2) + 2 * (k // 2)] = wide[CX - 1 : CX]
    t, e = coarse[2], coarse[3]
    still = base[...]
    for v, there in ((low, has_low), (high, has_high)):
        tn, en = v[:, 2 * CY : 3 * CY] * there, v[:, 3 * CY :] * there
        still = still + (1.0 + 0.5 * (e + en)) * (tn - t)
    for z in range(NPL):
        fx[z, 7:8] = jnp.zeros((1, NY), F32)
        fx[z, 8 + BX : 9 + BX] = jnp.zeros((1, NY), F32)
    for z in (1, 2):
        fx[z, 8 : 8 + BX] = fx12[z - 1]
    planes = [(halo, 0), (halo, 1), (own, 0), (own, 1), (own, 2), (own, 3), (halo, 2), (halo, 3)]

    def get(k, rows):
        ref, z = planes[k]
        return ref[z, rows]

    def fluxes(c, carry):
        r0 = 8 * c
        here, at, after = pl.ds(r0, 8), pl.ds(r0 + 8, 8), pl.ds(r0 + 16, 8)
        for side, (zz, there) in enumerate(((0, has_low), (5, has_high))):
            v = get(zz + 1, at)
            dz = get(zz + 2, at) - get(zz, at)
            dx = x_up(v, get(zz + 1, after)) - x_down(v, get(zz + 1, here))
            dy = y_up(v) - y_down(v)
            an = weigh(dz, dx, dy, sides[2 * side, here], sides[2 * side + 1, here])
            fzout[side, here] = (0.25 * there) * (an * an * dz)
        for side, z in enumerate((0, NPL - 1)):
            dz = get(z + 3, at) - get(z + 1, at)
            dx, dy = dxy[side, 0, here], dxy[side, 1, here]
            an = weigh(dz, dx, dy, fine[0, here], fine[1, here])
            wt = an * an
            quarter = 0.25 * wt
            fz03[side, here] = quarter * dz
            fx[z, at] = quarter * dx
            fy = quarter * dy
            bent[side, here] = known[z, here] + (y_up(fy) - y_down(fy))
            scale03[side, here] = DT * inverse(wt)
        return carry

    for c in range(BX // 8):
        fluxes(c, 0)

    for side in range(2):
        for row in (0, BX - 1):
            fzout[side, row : row + 1] = jnp.zeros((1, NY), F32)
    flux_z = [(fzout, 0), (fz03, 0), (fz12, 0), (fz12, 1), (fz03, 1), (fzout, 1)]
    rest = [(bent, 0), (known, 1), (known, 2), (bent, 1)]
    scales = [(scale03, 0), (scale12, 0), (scale12, 1), (scale03, 1)]

    for c in range(BX // 8):
        here, at, after = pl.ds(8 * c, 8), pl.ds(8 * c + 8, 8), pl.ds(8 * c + 16, 8)
        total = jnp.zeros((8, NY), F32)
        for z in range(NPL):
            p, f = own[z, at], fx[z, at]
            spread_z = flux_z[z + 2][0][flux_z[z + 2][1], here] - flux_z[z][0][flux_z[z][1], here]
            spread_x = x_up(f, fx[z, after]) - x_down(f, fx[z, here])
            factor = scales[z][0][scales[z][1], here]
            rise = factor * (rest[z][0][rest[z][1], here] + spread_z + spread_x)
            total = total + rise
            if c in (0, BX // 8 - 1):
                row, line = (0, z) if c == 0 else (7, NPL + z)
                lines[line : line + 1] = factor[row : row + 1]
            fresh[z, here] = p + rise
        total = total + pltpu.roll(total, 1, 0)
        total = total + pltpu.roll(total, 2, 0)
        change[2 * c : 2 * c + 1] = total[3:4]
        change[2 * c + 1 : 2 * c + 2] = total[7:8]
    spectral[...] = dot(still, consts[SY_AT]) + dot(change[...], consts[MEAN_AT])


def rim_kernel(
    own, rims, x_chip, x_core, zb, za, lb, la, spectral_in, lines, consts, fresh_in,
    fresh, spectral,
):
    n, w = lax.axis_index("narrow"), lax.axis_index("wide")
    even = lax.rem(n, 2) == 0
    has_left, has_right = flag(w > 0), flag(w < NWIDE - 1)
    has_low, has_high = flag(n > 0), flag(n < NNAR - 1)
    inner = x_sides(x_chip, x_core, slice(4, 8))

    def beyond(b, a, rows, high):
        if high:
            return jnp.where(even, a[rows], b[rows]) * has_high
        return jnp.where(even, b[rows], a[rows]) * has_low

    def corner(high, s):
        return beyond(lb, la, slice(CORNERS + s, CORNERS + s + 1), high)

    def outer(high, plane, x):
        return beyond(zb, za, slice(plane * BX + x, plane * BX + x + 1), high)

    rim = (7, 8 + BX)
    values = [[], [], [], [], []]
    for s in range(2):
        for z in range(NPL):
            at = slice(rim[s], rim[s] + 1)
            here = own[z, at]
            below = own[z - 1, at] if z > 0 else corner(False, s)
            above = own[z + 1, at] if z < NPL - 1 else corner(True, s)
            side = inner[s][z : z + 1]
            x_lo, x_hi = (own[z, 7 + BX : 8 + BX], side) if s else (side, own[z, 8:9])
            for rows, v in zip(values, (here, below, above, x_lo, x_hi)):
                rows.append(v)
    for high in (False, True):
        for s in range(2):
            x, near = (BX - 1, BX - 2) if s else (0, 1)
            mine = own[NPL - 1 if high else 0, 8 + x : 9 + x]
            here, behind = outer(high, 0 if high else 1, x), outer(high, 1 if high else 0, x)
            beside, past = outer(high, 0 if high else 1, near), corner(high, s)
            below, above = (mine, behind) if high else (behind, mine)
            x_lo, x_hi = (beside, past) if s else (past, beside)
            for rows, v in zip(values, (here, below, above, x_lo, x_hi)):
                rows.append(v)
    here, below, above, x_lo, x_hi = (
        jnp.concatenate(rows + [jnp.zeros((4, NY), F32)], 0) for rows in values
    )
    c2, s2 = (
        jnp.concatenate(
            [jnp.broadcast_to(rims[k : k + 1], (NPL, NY)), jnp.broadcast_to(rims[k + 2 : k + 3], (NPL, NY)),
             lines[8 + 4 * k : 12 + 4 * k], jnp.zeros((4, NY), F32)], 0,
        )
        for k in (0, 1)
    )
    dz, dx, dy = above - below, x_hi - x_lo, y_up(here) - y_down(here)
    an = weigh(dz, dx, dy, c2, s2)
    quarter = 0.25 * (an * an)
    row = rows_of(here[0:8])
    x_part = quarter[0:8] * dx[0:8] * jnp.where(row < NPL, -has_left, has_right)
    z_flux = quarter[8:16] * dz[8:16]
    z_part = jnp.zeros((8, NY), F32)
    for high in (False, True):
        for s in range(2):
            line = z_flux[2 * high + s : 2 * high + s + 1]
            line = line * has_high if high else -has_low * line
            z_part = jnp.where(row == NPL * s + (NPL - 1 if high else 0), line, z_part)
    rise = lines[0:8] * (x_part + z_part)
    for c in range(2):
        for z in range(NPL):
            add = rise[NPL * c + z : NPL * c + z + 1]
            at = (BX - 1) * c
            fresh[z, at : at + 1] = fresh_in[z, at : at + 1] + add
    sums = [jnp.sum(rise[NPL * c : NPL * (c + 1)], axis=0, keepdims=True) for c in range(2)]
    more = dot(jnp.concatenate(sums + [jnp.zeros((14, NY), F32)], 0), consts[MEAN_AT])
    first = rows_of(spectral_in)
    moved = spectral_in[...] + jnp.where(
        first == 0, more[0:1], jnp.where(first == CX - 1, more[1:2], 0.0)
    )
    spectral[...] = moved


def solute_kernel(state, own, x_chip, x_core, zb, za, lb, la, fresh, out, sown, grown, sems):
    phase_out = [
        pltpu.make_async_copy(fresh.at[z], out.at[0, z], sems.at[8 + z]) for z in range(NPL)
    ]
    for copy in phase_out:
        copy.start()
    n = lax.axis_index("narrow")
    even = lax.rem(n, 2) == 0
    left, right = x_sides(x_chip, x_core, slice(8, 12))
    has_low, has_high = flag(n > 0), flag(n < NNAR - 1)
    for z in range(NPL):
        sown[z, 8 : 8 + BX] = state[1, z]
        sown[z, 7:8] = left[z : z + 1]
        sown[z, 8 + BX : 9 + BX] = right[z : z + 1]

    def step(c):
        r0 = 8 * c
        here, at, after = pl.ds(r0, 8), pl.ds(r0 + 8, 8), pl.ds(r0 + 16, 8)

        beyond = pl.ds(r0 + BX, 8)
        ps = (
            [has_low * jnp.where(even, zb[beyond], za[beyond])]
            + [own[z, at] for z in range(NPL)]
            + [has_high * jnp.where(even, za[here], zb[here])]
        )
        if r0 < SPLIT:
            (b, a), there = (zb, za), pl.ds(EARLY + r0, 8)
        else:
            (b, a), there = (lb, la), pl.ds(r0 - SPLIT, 8)
        ss = (
            [has_low * jnp.where(even, b[there], a[there])]
            + [sown[z, at] for z in range(NPL)]
            + [has_high * jnp.where(even, a[there], b[there])]
        )
        for z in range(NPL):
            p, s = ps[z + 1], ss[z + 1]
            q = 0.55 - 0.25 * p
            near = [
                (ps[z], ss[z]),
                (ps[z + 2], ss[z + 2]),
                (x_up(p, own[z, after]), x_up(s, sown[z, after])),
                (x_down(p, own[z, here]), x_down(s, sown[z, here])),
                (y_up(p), y_up(s)),
                (y_down(p), y_down(s)),
            ]
            total = jnp.zeros_like(p)
            for pn, sn in near:
                total = total + (q - 0.25 * pn) * (sn - s)
            grown[z, here] = s + DT * total + (0.5 + 0.425 * s) * (fresh[z, here] - p)
        store(c).start()

    def store(c):
        rows = pl.ds(8 * c, 8)
        return pltpu.make_async_copy(grown.at[:, rows], out.at[1, :, rows], sems.at[c])

    for c in range(BX // 8):
        step(c)
    for c in range(BX // 8):
        store(c).wait()
    for copy in phase_out:
        copy.wait()


def eliminate(state, f, consts, first):
    states = []
    for i, v in enumerate(f):
        inv = consts[INV_AT + 8 * (first + i) : INV_AT + 8 * (first + i) + 8]
        state = inv * v if state is None else inv * v + (KBAR * inv) * state
        states.append(state)
    return states


def back(x, states, consts, first):
    values = []
    for i in range(len(states) - 1, -1, -1):
        inv = consts[INV_AT + 8 * (first + i) : INV_AT + 8 * (first + i) + 8]
        x = states[i] + (KBAR * inv) * x
        values.append(x)
    return values[::-1]


def mode_kernel(planes, consts, f, to_chip, to_core, to_next, modes):
    half = NNAR // 2
    folded = [
        [planes[m] + planes[NNAR - 1 - m] for m in range(half)],
        [planes[m] - planes[NNAR - 1 - m] for m in range(half)],
    ]
    for k in range(NNAR):
        total = float(SZ[k, 0]) * folded[k % 2][0]
        for m in range(1, half):
            total = total + float(SZ[k, m]) * folded[k % 2][m]
        modes[k * CX : (k + 1) * CX] = total
    values = [modes[pl.ds(j, 8, stride=CX), :] for j in range(CX)]
    for j in range(CX):
        f[j] = values[j]
    mirrored = values[::-1]
    right_margin = eliminate(None, values[12:], consts, 0)[-1]
    left_margin = eliminate(None, mirrored[12:], consts, 0)[-1]
    right_core = eliminate(None, values, consts, 4)[-1]
    left_core = eliminate(None, mirrored, consts, 4)[-1]
    core0 = lax.rem(lax.axis_index("wide"), 2) == 0
    to_core[0:8] = jnp.where(core0, right_margin, left_margin)
    to_core[8:16] = jnp.where(core0, right_core, left_core)
    to_chip[0:8] = jnp.where(core0, left_margin, right_margin)
    to_chip[8:16] = jnp.where(core0, left_core, right_core)
    to_next[0:8] = to_chip[0:8]
    to_next[8:24] = jnp.zeros((16, CY), F32)


def pass_kernel(to_chip, by_core, consts, message):
    message[0:8] = to_chip[0:8]
    message[8:16] = to_chip[8:16] + consts[PASS_AT] * by_core[0:8]


def solve_kernel(f, by_chip, by_core, by_next, coarse, consts, out, rows):
    n, w = lax.axis_index("narrow"), lax.axis_index("wide")
    core0 = lax.rem(w, 2) == 0
    has_left, has_right = flag(w > 0), flag(w < NWIDE - 1)
    beyond = consts[PASS_AT] * by_next[0:8] * jnp.where(core0, flag(w < NWIDE - 2), flag(w > 1))
    other = jnp.concatenate([by_core[0:8], by_core[8:16] + beyond], 0)
    left = jnp.where(core0, by_chip[...], other) * has_left
    right = jnp.where(core0, other, by_chip[...]) * has_right
    values = [f[j] for j in range(CX)]
    mirrored = values[::-1]
    half = CX // 2

    low = eliminate(left[0:8], values[:half], consts, 4)
    high = eliminate(right[0:8], mirrored[:half], consts, 4)
    link = KBAR * consts[INV_AT + 8 * 11 : INV_AT + 8 * 12]
    x_low = consts[MEET_AT] * (low[-1] + link * high[-1])
    x_high = consts[MEET_AT] * (high[-1] + link * low[-1])
    x = back(x_low, low[:-1], consts, 4) + [x_low]
    x += (back(x_high, high[:-1], consts, 4) + [x_high])[::-1]

    for here, near, there in (
        (range(4), left, has_left),
        (range(CX - 1, CX - 5, -1), right, has_right),
    ):
        states = eliminate(near[8:16], [values[j] for j in here], consts, 20)
        found = back(states[-1], states[:-1], consts, 20) + [states[-1]]
        for j, v in zip(here, found):
            x[j] = x[j] + there * v

    weight = consts[pl.ds(pl.multiple_of(SZ_AT + 8 * n, 8), 8)]
    for j in range(CX):
        rows[j : j + 1] = jnp.sum(x[j] * weight, axis=0, keepdims=True)
    out[0] = coarse[2] + dot(rows[...], consts[SY_AT])


def kernel(body, outs, scratch=(), far=(), far_outs=(), aliases=None, mib=16):
    many = isinstance(outs, (list, tuple))

    def call(*args):
        return pl.pallas_call(
            body,
            out_shape=outs,
            in_specs=[HBM if i in far else VMEM for i in range(len(args))],
            out_specs=[HBM if i in far_outs else VMEM for i in range(len(outs))] if many else (HBM if far_outs else VMEM),
            input_output_aliases=aliases or {},
            scratch_shapes=list(scratch),
            compiler_params=params(mib),
            name=body.__name__,
        )(*args)

    return call


def afar(v):
    return pltpu.with_memory_space_constraint(v, pltpu.HBM)


def on_device(state_in, ids, frozen, temp, angles):
    inputs = [afar(v) for v in (state_in, ids, frozen, temp, angles.reshape(1, -1))]
    face_b, face_a, to_chip, to_core, state, coarse = kernel(
        stage_kernel,
        [sds(FACE, NY)] * 2 + [sds(16, NY)] * 2 + [sds(2, NPL, BX, NY), sds(4, CX, CY)],
        [
            pltpu.VMEM((1, CX, CY), jnp.int32),
            pltpu.VMEM((1, CX, CY), jnp.int32),
            pltpu.VMEM((1, CX, CY), F32),
            pltpu.VMEM((1, 64), F32),
            pltpu.SemaphoreType.DMA((6,)),
        ],
        far=range(5),
    )(*inputs)
    zb = lax.ppermute(face_b, BOTH, PAIR_B)
    za = lax.ppermute(face_a, "narrow", PAIR_A)
    x_chip = lax.ppermute(to_chip, BOTH, CHIPS)
    x_core = lax.ppermute(to_core, "wide", CORES)
    fine = kernel(spread_kernel, sds(3, BX, NY))(coarse)
    shapes = [
        sds(NPL, BX + 16, NY), sds(2, BX, NY), sds(2, BX, NY), sds(NPL, BX, NY), sds(2, BX, NY),
        sds(2, 2, BX, NY),
    ]
    *inside, consts = kernel(
        inside_kernel, shapes + [sds(*CONSTS.shape)], [pltpu.SemaphoreType.DMA], far=(2,)
    )(state, fine, afar(jnp.asarray(CONSTS)))
    late_b, late_a = kernel(late_kernel, [sds(LATE, NY)] * 2)(state, x_chip, x_core, inside[0])
    lb = lax.ppermute(late_b, BOTH, PAIR_B)
    la = lax.ppermute(late_a, "narrow", PAIR_A)
    own, fx12, fz12, known, scale12, dxy, rims, base = kernel(
        edge_kernel,
        shapes + [sds(8, NY), sds(CX, CY)],
        aliases={5 + i: i for i in range(6)},
    )(state, coarse, fine, x_chip, x_core, *inside)
    fresh, spectral, lines = kernel(
        phase_kernel,
        [sds(NPL, BX, NY), sds(CX, CY), sds(16, NY)],
        [
            pltpu.VMEM((4, BX, NY), F32),
            pltpu.VMEM((4, BX + 16, NY), F32),
            pltpu.VMEM((NPL, BX + 16, NY), F32),
            pltpu.VMEM((2, BX, NY), F32),
            pltpu.VMEM((2, BX, NY), F32),
            pltpu.VMEM((2, BX, NY), F32),
            pltpu.VMEM((2, BX, NY), F32),
            pltpu.VMEM((CX, NY), F32),
        ],
    )(coarse, own, fine, fx12, fz12, known, scale12, dxy, zb, za, base, consts)
    fresh, spectral = kernel(
        rim_kernel, [sds(NPL, BX, NY), sds(CX, CY)], aliases={11: 0}
    )(own, rims, x_chip, x_core, zb, za, lb, la, spectral, lines, consts, fresh)
    planes = lax.all_to_all(jnp.broadcast_to(spectral[None], (NNAR, CX, CY)), "narrow", 0, 0)
    state_new = kernel(
        solute_kernel,
        sds(2, NPL, BX, NY),
        [
            pltpu.VMEM((NPL, BX + 16, NY), F32),
            pltpu.VMEM((NPL, BX, NY), F32),
            pltpu.SemaphoreType.DMA((BX // 8 + NPL,)),
        ],
        far_outs=(0,),
    )(state, own, x_chip, x_core, zb, za, lb, la, fresh)
    f, to_chip, to_core, to_next = kernel(
        mode_kernel,
        [sds(CX, 8, CY), sds(16, CY), sds(16, CY), sds(24, CY)],
        [pltpu.VMEM((NNAR * CX, CY), F32)],
    )(planes, consts)
    by_core = lax.ppermute(to_core, "wide", CORES)
    by_next = lax.ppermute(to_next, BOTH, INWARD)
    by_chip = lax.ppermute(kernel(pass_kernel, sds(16, CY))(to_chip, by_core, consts), BOTH, CHIPS)
    adjusted = kernel(solve_kernel, sds(1, CX, CY), [pltpu.VMEM((CX, CY), F32)])(
        f, by_chip, by_core, by_next, coarse, consts
    )
    return state_new, adjusted


def solution(mesh):
    return jax.shard_map(
        on_device,
        mesh=mesh,
        in_specs=(
            P(None, "narrow", "wide", None),
            P("narrow", "wide", None),
            P("narrow", "wide", None),
            P("narrow", "wide", None),
            P(),
        ),
        out_specs=(P(None, "narrow", "wide", None), P("narrow", "wide", None)),
        check_vma=False,
    )
```

```python
import functools

import jax
import jax.numpy as jnp
import numpy as np
from jax import lax
from jax.experimental import pallas as pl
from jax.experimental.pallas import tpu as pltpu
from jax.sharding import PartitionSpec as P

F32 = jnp.float32
NNAR, NWIDE = 8, 32
NPL, BX, NY = 4, 64, 512
SPLIT = 24
ROUGH, EARLY, FACE = 128, 144, 144 + SPLIT
CORNERS, LATE = 64 - SPLIT, 72 - SPLIT
CX, CY = 16, 128
SUBX = 24
SIGMA, KBAR = 0.05, 0.75
DT = 0.15
VMEM = pl.BlockSpec(memory_space=pltpu.VMEM)
HBM = pl.BlockSpec(memory_space=pltpu.HBM)


def sds(*shape):
    return jax.ShapeDtypeStruct(shape, F32)


def params(mib):
    return pltpu.CompilerParams(vmem_limit_bytes=mib * 1024 * 1024)


def sine(points):
    k = np.arange(1, points + 1)
    return np.sqrt(2.0 / (points + 1)) * np.sin(np.pi * np.outer(k, k) / (points + 1))


def level(points):
    return 2.0 - 2.0 * np.cos(np.pi * np.arange(1, points + 1) / (points + 1))


SZ, SY = sine(8), sine(CY)
MEAN_Y = np.repeat(SY, 4, axis=0) / 64.0
SZ_ROWS = np.repeat(SZ[:, :, None], CY, 2)


def elimination():
    diag = SIGMA + KBAR * (level(8)[:, None] + level(CY)[None, :] + 2.0)
    inv = [1.0 / diag]
    for _ in range(SUBX - 1):
        inv.append(1.0 / (diag - KBAR * KBAR * inv[-1]))
    return np.stack(inv)


INVERSE = elimination()


LINK = KBAR * INVERSE
PASS = np.prod(LINK[4:20], axis=0)
MEET = 1.0 / (1.0 - LINK[11] ** 2)

CONSTS = np.concatenate(
    [SY, MEAN_Y, INVERSE.reshape(-1, CY), SZ_ROWS.reshape(-1, CY), PASS, MEET]
).astype(np.float32)
SY_AT, MEAN_AT, INV_AT, SZ_AT = slice(0, 128), slice(128, 640), 640, 640 + 8 * SUBX
PASS_AT = slice(SZ_AT + 64, SZ_AT + 72)
MEET_AT = slice(SZ_AT + 72, SZ_AT + 80)


def flat(n, w):
    return n * NWIDE + w


def everywhere(step):
    return [(flat(n, w), flat(*step(n, w))) for n in range(NNAR) for w in range(NWIDE)]


def swap_b(n, w):
    return (n, w ^ 1) if n in (0, NNAR - 1) else (((n + 1) ^ 1) - 1, w)


def swap_chips(n, w):
    if w in (0, NWIDE - 1):
        return (n ^ 4, w) if n % 4 in (1, 2) else (n, NWIDE - 1 - w)
    return n, ((w + 1) ^ 1) - 1


def swap_chips_last(n, w):
    return (n ^ 1, w) if w in (0, NWIDE - 1) else (n, ((w + 1) ^ 1) - 1)


def inward(n, w):
    to = w + 2 if w % 2 else w - 2
    return n, to if 0 <= to < NWIDE else w ^ 1


BOTH = ("narrow", "wide")
PAIR_A = [(i, i ^ 1) for i in range(NNAR)]
CORES = [(i, i ^ 1) for i in range(NWIDE)]
PAIR_B, CHIPS = everywhere(swap_b), everywhere(swap_chips)
INWARD, CHIPS_LAST = everywhere(inward), everywhere(swap_chips_last)


def lanes(v):
    return lax.broadcasted_iota(jnp.int32, v.shape, v.ndim - 1)


def rows_of(v):
    return lax.broadcasted_iota(jnp.int32, v.shape, len(v.shape) - 2)


def y_up(v):
    n = v.shape[-1]
    return jnp.where(lanes(v) == n - 1, 0.0, pltpu.roll(v, n - 1, v.ndim - 1))


def y_down(v):
    return jnp.where(lanes(v) == 0, 0.0, pltpu.roll(v, 1, v.ndim - 1))


def x_up(v, after):
    return pltpu.roll(jnp.where(rows_of(v) == 0, after, v), 7, v.ndim - 2)


def x_down(v, before):
    return pltpu.roll(jnp.where(rows_of(v) == 7, before, v), 1, v.ndim - 2)


def inverse(v):
    guess = pl.reciprocal(v, approx=True)
    return guess * (2.0 - v * guess)


def weigh(dz, dx, dy, c2, s2):
    q0, a, b = dz * dz, dx * dx, dy * dy
    r = a + b
    uv = s2 * (b - a) + c2 * (dx * dy)
    num = q0 * q0 + r * r - 2.0 * (uv * uv)
    over = inverse(q0 + r + 4.0)
    return 0.55 + 0.6 * (num * (over * over))


def flag(cond):
    return jnp.where(cond, 1.0, 0.0).astype(F32)


def spread(v):
    lane = lax.shift_right_logical(lanes(v), 2)
    return jnp.concatenate(
        [jnp.take_along_axis(v, lane + 32 * j, axis=1) for j in range(NY // CY)], 1
    )


def halves(v):
    high = v.astype(jnp.bfloat16)
    return high, (v - high.astype(F32)).astype(jnp.bfloat16)


def dot(a, b):
    (a1, a2), (b1, b2) = halves(a), halves(b)
    mul = functools.partial(jnp.dot, preferred_element_type=F32)
    return mul(a1, b1) + (mul(a1, b2) + mul(a2, b1))


def stage_kernel(
    state_in, ids_in, frozen_in, temp_in, angles_in,
    face_b, face_a, x_chip, x_core, state, coarse,
    ids, frozen, temp, angles, sems,
):
    copies = [
        pltpu.make_async_copy(src, dst, sems.at[i])
        for i, (src, dst) in enumerate(
            [
                (state_in.at[0], state.at[0]),
                (state_in.at[1], state.at[1]),
                (ids_in, ids),
                (frozen_in, frozen),
                (temp_in, temp),
                (angles_in, angles),
            ]
        )
    ]
    for copy in copies:
        copy.start()
    for copy in copies[2:]:
        copy.wait()
    table = jnp.concatenate([angles[...], angles[...]], 1)
    c = jnp.take_along_axis(jnp.broadcast_to(jnp.cos(table), (CX, CY)), ids[0], axis=1)
    s = jnp.take_along_axis(jnp.broadcast_to(jnp.sin(table), (CX, CY)), ids[0], axis=1)
    coarse[0] = c * c - s * s
    coarse[1] = c * s
    coarse[2] = temp[0]
    coarse[3] = -0.5 * frozen[0].astype(F32)
    even = lax.rem(lax.axis_index("narrow"), 2) == 0
    for ref in (face_b, face_a):
        for k in range(4):
            ref[ROUGH:EARLY, k * CY : (k + 1) * CY] = coarse[k]
    copies[0].wait()
    for ref, top in ((face_b, jnp.logical_not(even)), (face_a, even)):
        first = jnp.where(top, 2, 0)
        ref[0:BX] = state[0, first]
        ref[BX : 2 * BX] = state[0, first + 1]
    copies[1].wait()
    for ref, top in ((face_b, jnp.logical_not(even)), (face_a, even)):
        ref[EARLY:FACE] = state[1, jnp.where(top, 3, 0), 0:SPLIT]
    core0 = lax.rem(lax.axis_index("wide"), 2) == 0
    for ref, low in ((x_chip, core0), (x_core, jnp.logical_not(core0))):
        for z in range(NPL):
            for at, ch, first, last in ((0, 0, 0, BX - 1), (4, 0, 1, BX - 2), (8, 1, 0, BX - 1)):
                ref[at + z : at + z + 1] = jnp.where(
                    low, state[ch, z, first : first + 1], state[ch, z, last : last + 1]
                )
        for k in range(4):
            ref[12:13, k * CY : (k + 1) * CY] = jnp.where(
                low, coarse[k, 0:1], coarse[k, CX - 1 : CX]
            )
        ref[13:16] = jnp.zeros((3, NY), F32)


def x_sides(x_chip, x_core, rows):
    w = lax.axis_index("wide")
    core0 = lax.rem(w, 2) == 0
    left = jnp.where(core0, x_chip[rows], x_core[rows]) * flag(w > 0)
    right = jnp.where(core0, x_core[rows], x_chip[rows]) * flag(w < NWIDE - 1)
    return left, right


def late_kernel(state, x_chip, x_core, own, late_b, late_a):
    even = lax.rem(lax.axis_index("narrow"), 2) == 0
    left, right = x_sides(x_chip, x_core, slice(0, 8))
    for ref, top in ((late_b, jnp.logical_not(even)), (late_a, even)):
        ref[0:CORNERS] = state[1, jnp.where(top, 3, 0), SPLIT:BX]
        ref[CORNERS : CORNERS + 1] = jnp.where(top, left[3:4], left[0:1])
        ref[CORNERS + 1 : CORNERS + 2] = jnp.where(top, right[3:4], right[0:1])
        ref[CORNERS + 2 : LATE] = jnp.zeros((LATE - CORNERS - 2, NY), F32)


def widen(ref, at, rough):
    for k in range(CX):
        ref[at, 4 * k : 4 * k + 4] = jnp.broadcast_to(rough[k : k + 1], (4, NY))


def spread_kernel(coarse, fine):
    for k in range(3):
        widen(fine, k, spread(coarse[k]))


def local_terms(c, state, own, fine, fx, fz, known, scale, dxy):
    r0 = 8 * c
    here, at, after = pl.ds(r0, 8), pl.ds(r0 + 8, 8), pl.ds(r0 + 16, 8)
    for z in range(NPL):
        v = own[z, at]
        dx = x_up(v, own[z, after]) - x_down(v, own[z, here])
        dy = y_up(v) - y_down(v)
        m = 1.0 - v * v
        drive = m * (v - 1.5 * (state[1, z, here] + fine[2, here]) * m)
        if z in (0, NPL - 1):
            known[z, here] = drive
            dxy[z // 2, 0, here] = dx
            dxy[z // 2, 1, here] = dy
            continue
        dz = own[z + 1, at] - own[z - 1, at]
        an = weigh(dz, dx, dy, fine[0, here], fine[1, here])
        wt = an * an
        quarter = 0.25 * wt
        fz[z - 1, here] = quarter * dz
        fx[z - 1, here] = quarter * dx
        fy = quarter * dy
        known[z, here] = (y_up(fy) - y_down(fy)) + drive
        scale[z - 1, here] = DT * inverse(wt)


def inside_kernel(state, fine, consts_in, own, fx, fz, known, scale, dxy, consts, sem):
    fetch = pltpu.make_async_copy(consts_in, consts, sem)
    fetch.start()
    for z in range(NPL):
        own[z, 8 : 8 + BX] = state[0, z]

    def chunk(c, carry):
        local_terms(c, state, own, fine, fx, fz, known, scale, dxy)
        return carry

    for c in range(1, BX // 8 - 1):
        chunk(c, 0)
    fetch.wait()


def edge_kernel(
    state, coarse, fine, x_chip, x_core, own_in, fx_in, fz_in, known_in, scale_in, dxy_in,
    own, fx, fz, known, scale, dxy, rims, base,
):
    left, right = x_sides(x_chip, x_core, slice(0, 4))
    for z in range(NPL):
        own[z, 7:8] = left[z : z + 1]
        own[z, 8 + BX : 9 + BX] = right[z : z + 1]
    left, right = x_sides(x_chip, x_core, slice(12, 13))
    rows = [side[:, k * CY : (k + 1) * CY] for side in (left, right) for k in (0, 1)]
    rims[...] = spread(jnp.concatenate(rows + rows, 0))
    for c in (0, BX // 8 - 1):
        local_terms(c, state, own, fine, fx, fz, known, scale, dxy)
    t, e = coarse[2], coarse[3]
    row = rows_of(t)
    down, up = [], []
    for k, v in ((2, t), (3, e)):
        before, after = left[:, k * CY : (k + 1) * CY], right[:, k * CY : (k + 1) * CY]
        down.append(jnp.where(row == 0, before, pltpu.roll(v, 1, 0)))
        up.append(jnp.where(row == CX - 1, after, pltpu.roll(v, CX - 1, 0)))
    near = [tuple(down), tuple(up), (y_up(t), y_up(e)), (y_down(t), y_down(e))]
    total = jnp.zeros_like(t)
    for tn, en in near:
        total = total + (1.0 + 0.5 * (e + en)) * (tn - t)
    base[...] = total


def phase_kernel(
    coarse, own, fine, fx12, fz12, known, scale12, dxy, zb, za, base, consts,
    fresh, spectral, lines,
    sides, halo, fx, fz03, fzout, bent, scale03, change,
):
    n = lax.axis_index("narrow")
    even = lax.rem(n, 2) == 0
    has_low, has_high = flag(n > 0), flag(n < NNAR - 1)
    for face, at, there in (
        (zb, jnp.where(even, 0, 2), jnp.where(even, has_low, has_high)),
        (za, jnp.where(even, 2, 0), jnp.where(even, has_high, has_low)),
    ):
        for k in range(2):
            halo[at + k, 8 : 8 + BX] = face[k * BX : (k + 1) * BX] * there
    low = jnp.where(even, zb[ROUGH:EARLY], za[ROUGH:EARLY])
    high = jnp.where(even, za[ROUGH:EARLY], zb[ROUGH:EARLY])
    for k, v in enumerate((low, low, high, high)):
        wide = spread(v[:, (k % 2) * CY : (k % 2 + 1) * CY])
        widen(sides, k, wide)
        lines[8 + 4 * (k % 2) + 2 * (k // 2) : 9 + 4 * (k % 2) + 2 * (k // 2)] = wide[0:1]
        lines[9 + 4 * (k % 2) + 2 * (k // 2) : 10 + 4 * (k % 2) + 2 * (k // 2)] = wide[CX - 1 : CX]
    t, e = coarse[2], coarse[3]
    still = base[...]
    for v, there in ((low, has_low), (high, has_high)):
        tn, en = v[:, 2 * CY : 3 * CY] * there, v[:, 3 * CY :] * there
        still = still + (1.0 + 0.5 * (e + en)) * (tn - t)
    for z in range(NPL):
        fx[z, 7:8] = jnp.zeros((1, NY), F32)
        fx[z, 8 + BX : 9 + BX] = jnp.zeros((1, NY), F32)
    for z in (1, 2):
        fx[z, 8 : 8 + BX] = fx12[z - 1]
    planes = [(halo, 0), (halo, 1), (own, 0), (own, 1), (own, 2), (own, 3), (halo, 2), (halo, 3)]

    def get(k, rows):
        ref, z = planes[k]
        return ref[z, rows]

    def fluxes(c, carry):
        r0 = 8 * c
        here, at, after = pl.ds(r0, 8), pl.ds(r0 + 8, 8), pl.ds(r0 + 16, 8)
        for side, (zz, there) in enumerate(((0, has_low), (5, has_high))):
            v = get(zz + 1, at)
            dz = get(zz + 2, at) - get(zz, at)
            dx = x_up(v, get(zz + 1, after)) - x_down(v, get(zz + 1, here))
            dy = y_up(v) - y_down(v)
            an = weigh(dz, dx, dy, sides[2 * side, here], sides[2 * side + 1, here])
            fzout[side, here] = (0.25 * there) * (an * an * dz)
        for side, z in enumerate((0, NPL - 1)):
            dz = get(z + 3, at) - get(z + 1, at)
            dx, dy = dxy[side, 0, here], dxy[side, 1, here]
            an = weigh(dz, dx, dy, fine[0, here], fine[1, here])
            wt = an * an
            quarter = 0.25 * wt
            fz03[side, here] = quarter * dz
            fx[z, at] = quarter * dx
            fy = quarter * dy
            bent[side, here] = known[z, here] + (y_up(fy) - y_down(fy))
            scale03[side, here] = DT * inverse(wt)
        return carry

    for c in range(BX // 8):
        fluxes(c, 0)

    for side in range(2):
        for row in (0, BX - 1):
            fzout[side, row : row + 1] = jnp.zeros((1, NY), F32)
    flux_z = [(fzout, 0), (fz03, 0), (fz12, 0), (fz12, 1), (fz03, 1), (fzout, 1)]
    rest = [(bent, 0), (known, 1), (known, 2), (bent, 1)]
    scales = [(scale03, 0), (scale12, 0), (scale12, 1), (scale03, 1)]

    for c in range(BX // 8):
        here, at, after = pl.ds(8 * c, 8), pl.ds(8 * c + 8, 8), pl.ds(8 * c + 16, 8)
        total = jnp.zeros((8, NY), F32)
        for z in range(NPL):
            p, f = own[z, at], fx[z, at]
            spread_z = flux_z[z + 2][0][flux_z[z + 2][1], here] - flux_z[z][0][flux_z[z][1], here]
            spread_x = x_up(f, fx[z, after]) - x_down(f, fx[z, here])
            factor = scales[z][0][scales[z][1], here]
            rise = factor * (rest[z][0][rest[z][1], here] + spread_z + spread_x)
            total = total + rise
            if c in (0, BX // 8 - 1):
                row, line = (0, z) if c == 0 else (7, NPL + z)
                lines[line : line + 1] = factor[row : row + 1]
            fresh[z, here] = p + rise
        total = total + pltpu.roll(total, 1, 0)
        total = total + pltpu.roll(total, 2, 0)
        change[2 * c : 2 * c + 1] = total[3:4]
        change[2 * c + 1 : 2 * c + 2] = total[7:8]
    spectral[...] = dot(still, consts[SY_AT]) + dot(change[...], consts[MEAN_AT])


def rim_kernel(
    own, rims, x_chip, x_core, zb, za, lb, la, spectral_in, lines, consts, fresh_in,
    fresh, spectral,
):
    n, w = lax.axis_index("narrow"), lax.axis_index("wide")
    even = lax.rem(n, 2) == 0
    has_left, has_right = flag(w > 0), flag(w < NWIDE - 1)
    has_low, has_high = flag(n > 0), flag(n < NNAR - 1)
    inner = x_sides(x_chip, x_core, slice(4, 8))

    def beyond(b, a, rows, high):
        if high:
            return jnp.where(even, a[rows], b[rows]) * has_high
        return jnp.where(even, b[rows], a[rows]) * has_low

    def corner(high, s):
        return beyond(lb, la, slice(CORNERS + s, CORNERS + s + 1), high)

    def outer(high, plane, x):
        return beyond(zb, za, slice(plane * BX + x, plane * BX + x + 1), high)

    rim = (7, 8 + BX)
    values = [[], [], [], [], []]
    for s in range(2):
        for z in range(NPL):
            at = slice(rim[s], rim[s] + 1)
            here = own[z, at]
            below = own[z - 1, at] if z > 0 else corner(False, s)
            above = own[z + 1, at] if z < NPL - 1 else corner(True, s)
            side = inner[s][z : z + 1]
            x_lo, x_hi = (own[z, 7 + BX : 8 + BX], side) if s else (side, own[z, 8:9])
            for rows, v in zip(values, (here, below, above, x_lo, x_hi)):
                rows.append(v)
    for high in (False, True):
        for s in range(2):
            x, near = (BX - 1, BX - 2) if s else (0, 1)
            mine = own[NPL - 1 if high else 0, 8 + x : 9 + x]
            here, behind = outer(high, 0 if high else 1, x), outer(high, 1 if high else 0, x)
            beside, past = outer(high, 0 if high else 1, near), corner(high, s)
            below, above = (mine, behind) if high else (behind, mine)
            x_lo, x_hi = (beside, past) if s else (past, beside)
            for rows, v in zip(values, (here, below, above, x_lo, x_hi)):
                rows.append(v)
    here, below, above, x_lo, x_hi = (
        jnp.concatenate(rows + [jnp.zeros((4, NY), F32)], 0) for rows in values
    )
    c2, s2 = (
        jnp.concatenate(
            [jnp.broadcast_to(rims[k : k + 1], (NPL, NY)), jnp.broadcast_to(rims[k + 2 : k + 3], (NPL, NY)),
             lines[8 + 4 * k : 12 + 4 * k], jnp.zeros((4, NY), F32)], 0,
        )
        for k in (0, 1)
    )
    dz, dx, dy = above - below, x_hi - x_lo, y_up(here) - y_down(here)
    an = weigh(dz, dx, dy, c2, s2)
    quarter = 0.25 * (an * an)
    row = rows_of(here[0:8])
    x_part = quarter[0:8] * dx[0:8] * jnp.where(row < NPL, -has_left, has_right)
    z_flux = quarter[8:16] * dz[8:16]
    z_part = jnp.zeros((8, NY), F32)
    for high in (False, True):
        for s in range(2):
            line = z_flux[2 * high + s : 2 * high + s + 1]
            line = line * has_high if high else -has_low * line
            z_part = jnp.where(row == NPL * s + (NPL - 1 if high else 0), line, z_part)
    rise = lines[0:8] * (x_part + z_part)
    for c in range(2):
        for z in range(NPL):
            add = rise[NPL * c + z : NPL * c + z + 1]
            at = (BX - 1) * c
            fresh[z, at : at + 1] = fresh_in[z, at : at + 1] + add
    sums = [jnp.sum(rise[NPL * c : NPL * (c + 1)], axis=0, keepdims=True) for c in range(2)]
    more = dot(jnp.concatenate(sums + [jnp.zeros((14, NY), F32)], 0), consts[MEAN_AT])
    first = rows_of(spectral_in)
    moved = spectral_in[...] + jnp.where(
        first == 0, more[0:1], jnp.where(first == CX - 1, more[1:2], 0.0)
    )
    spectral[...] = moved


def solute_kernel(state, own, x_chip, x_core, zb, za, lb, la, fresh, out, sown, grown, sems):
    phase_out = [
        pltpu.make_async_copy(fresh.at[z], out.at[0, z], sems.at[8 + z]) for z in range(NPL)
    ]
    for copy in phase_out:
        copy.start()
    n = lax.axis_index("narrow")
    even = lax.rem(n, 2) == 0
    left, right = x_sides(x_chip, x_core, slice(8, 12))
    has_low, has_high = flag(n > 0), flag(n < NNAR - 1)
    for z in range(NPL):
        sown[z, 8 : 8 + BX] = state[1, z]
        sown[z, 7:8] = left[z : z + 1]
        sown[z, 8 + BX : 9 + BX] = right[z : z + 1]

    def step(c):
        r0 = 8 * c
        here, at, after = pl.ds(r0, 8), pl.ds(r0 + 8, 8), pl.ds(r0 + 16, 8)

        beyond = pl.ds(r0 + BX, 8)
        ps = (
            [has_low * jnp.where(even, zb[beyond], za[beyond])]
            + [own[z, at] for z in range(NPL)]
            + [has_high * jnp.where(even, za[here], zb[here])]
        )
        if r0 < SPLIT:
            (b, a), there = (zb, za), pl.ds(EARLY + r0, 8)
        else:
            (b, a), there = (lb, la), pl.ds(r0 - SPLIT, 8)
        ss = (
            [has_low * jnp.where(even, b[there], a[there])]
            + [sown[z, at] for z in range(NPL)]
            + [has_high * jnp.where(even, a[there], b[there])]
        )
        for z in range(NPL):
            p, s = ps[z + 1], ss[z + 1]
            q = 0.55 - 0.25 * p
            near = [
                (ps[z], ss[z]),
                (ps[z + 2], ss[z + 2]),
                (x_up(p, own[z, after]), x_up(s, sown[z, after])),
                (x_down(p, own[z, here]), x_down(s, sown[z, here])),
                (y_up(p), y_up(s)),
                (y_down(p), y_down(s)),
            ]
            total = jnp.zeros_like(p)
            for pn, sn in near:
                total = total + (q - 0.25 * pn) * (sn - s)
            grown[z, here] = s + DT * total + (0.5 + 0.425 * s) * (fresh[z, here] - p)
        store(c).start()

    def store(c):
        rows = pl.ds(8 * c, 8)
        return pltpu.make_async_copy(grown.at[:, rows], out.at[1, :, rows], sems.at[c])

    for c in range(BX // 8):
        step(c)
    for c in range(BX // 8):
        store(c).wait()
    for copy in phase_out:
        copy.wait()


def eliminate(state, f, consts, first):
    states = []
    for i, v in enumerate(f):
        inv = consts[INV_AT + 8 * (first + i) : INV_AT + 8 * (first + i) + 8]
        state = inv * v if state is None else inv * v + (KBAR * inv) * state
        states.append(state)
    return states


def back(x, states, consts, first):
    values = []
    for i in range(len(states) - 1, -1, -1):
        inv = consts[INV_AT + 8 * (first + i) : INV_AT + 8 * (first + i) + 8]
        x = states[i] + (KBAR * inv) * x
        values.append(x)
    return values[::-1]


def mode_kernel(planes, consts, f, to_chip, to_core, to_next, modes):
    half = NNAR // 2
    folded = [
        [planes[m] + planes[NNAR - 1 - m] for m in range(half)],
        [planes[m] - planes[NNAR - 1 - m] for m in range(half)],
    ]
    for k in range(NNAR):
        total = float(SZ[k, 0]) * folded[k % 2][0]
        for m in range(1, half):
            total = total + float(SZ[k, m]) * folded[k % 2][m]
        modes[k * CX : (k + 1) * CX] = total
    values = [modes[pl.ds(j, 8, stride=CX), :] for j in range(CX)]
    for j in range(CX):
        f[j] = values[j]
    mirrored = values[::-1]
    right_margin = eliminate(None, values[12:], consts, 0)[-1]
    left_margin = eliminate(None, mirrored[12:], consts, 0)[-1]
    right_core = eliminate(None, values, consts, 4)[-1]
    left_core = eliminate(None, mirrored, consts, 4)[-1]
    core0 = lax.rem(lax.axis_index("wide"), 2) == 0
    to_core[0:8] = jnp.where(core0, right_margin, left_margin)
    to_core[8:16] = jnp.where(core0, right_core, left_core)
    to_chip[0:8] = jnp.where(core0, left_margin, right_margin)
    to_chip[8:16] = jnp.where(core0, left_core, right_core)
    to_next[...] = to_chip[0:8]


def pass_kernel(to_chip, by_core, consts, message):
    message[0:8] = to_chip[0:8]
    message[8:16] = to_chip[8:16] + consts[PASS_AT] * by_core[0:8]


def solve_kernel(f, by_chip, by_core, by_next, coarse, consts, out, rows):
    n, w = lax.axis_index("narrow"), lax.axis_index("wide")
    core0 = lax.rem(w, 2) == 0
    has_left, has_right = flag(w > 0), flag(w < NWIDE - 1)
    beyond = consts[PASS_AT] * by_next[...] * jnp.where(core0, flag(w < NWIDE - 2), flag(w > 1))
    other = jnp.concatenate([by_core[0:8], by_core[8:16] + beyond], 0)
    left = jnp.where(core0, by_chip[...], other) * has_left
    right = jnp.where(core0, other, by_chip[...]) * has_right
    values = [f[j] for j in range(CX)]
    mirrored = values[::-1]
    half = CX // 2

    low = eliminate(left[0:8], values[:half], consts, 4)
    high = eliminate(right[0:8], mirrored[:half], consts, 4)
    link = KBAR * consts[INV_AT + 8 * 11 : INV_AT + 8 * 12]
    x_low = consts[MEET_AT] * (low[-1] + link * high[-1])
    x_high = consts[MEET_AT] * (high[-1] + link * low[-1])
    x = back(x_low, low[:-1], consts, 4) + [x_low]
    x += (back(x_high, high[:-1], consts, 4) + [x_high])[::-1]

    for here, near, there in (
        (range(4), left, has_left),
        (range(CX - 1, CX - 5, -1), right, has_right),
    ):
        states = eliminate(near[8:16], [values[j] for j in here], consts, 20)
        found = back(states[-1], states[:-1], consts, 20) + [states[-1]]
        for j, v in zip(here, found):
            x[j] = x[j] + there * v

    weight = consts[pl.ds(pl.multiple_of(SZ_AT + 8 * n, 8), 8)]
    for j in range(CX):
        rows[j : j + 1] = jnp.sum(x[j] * weight, axis=0, keepdims=True)
    out[0] = coarse[2] + dot(rows[...], consts[SY_AT])


def kernel(body, outs, scratch=(), far=(), far_outs=(), aliases=None, mib=16):
    many = isinstance(outs, (list, tuple))

    def call(*args):
        return pl.pallas_call(
            body,
            out_shape=outs,
            in_specs=[HBM if i in far else VMEM for i in range(len(args))],
            out_specs=[HBM if i in far_outs else VMEM for i in range(len(outs))] if many else (HBM if far_outs else VMEM),
            input_output_aliases=aliases or {},
            scratch_shapes=list(scratch),
            compiler_params=params(mib),
            name=body.__name__,
        )(*args)

    return call


def afar(v):
    return pltpu.with_memory_space_constraint(v, pltpu.HBM)


def on_device(state_in, ids, frozen, temp, angles):
    inputs = [afar(v) for v in (state_in, ids, frozen, temp, angles.reshape(1, -1))]
    face_b, face_a, to_chip, to_core, state, coarse = kernel(
        stage_kernel,
        [sds(FACE, NY)] * 2 + [sds(16, NY)] * 2 + [sds(2, NPL, BX, NY), sds(4, CX, CY)],
        [
            pltpu.VMEM((1, CX, CY), jnp.int32),
            pltpu.VMEM((1, CX, CY), jnp.int32),
            pltpu.VMEM((1, CX, CY), F32),
            pltpu.VMEM((1, 64), F32),
            pltpu.SemaphoreType.DMA((6,)),
        ],
        far=range(5),
    )(*inputs)
    zb = lax.ppermute(face_b, BOTH, PAIR_B)
    za = lax.ppermute(face_a, "narrow", PAIR_A)
    x_chip = lax.ppermute(to_chip, BOTH, CHIPS)
    x_core = lax.ppermute(to_core, "wide", CORES)
    fine = kernel(spread_kernel, sds(3, BX, NY))(coarse)
    shapes = [
        sds(NPL, BX + 16, NY), sds(2, BX, NY), sds(2, BX, NY), sds(NPL, BX, NY), sds(2, BX, NY),
        sds(2, 2, BX, NY),
    ]
    *inside, consts = kernel(
        inside_kernel, shapes + [sds(*CONSTS.shape)], [pltpu.SemaphoreType.DMA], far=(2,)
    )(state, fine, afar(jnp.asarray(CONSTS)))
    late_b, late_a = kernel(late_kernel, [sds(LATE, NY)] * 2)(state, x_chip, x_core, inside[0])
    lb = lax.ppermute(late_b, BOTH, PAIR_B)
    la = lax.ppermute(late_a, "narrow", PAIR_A)
    own, fx12, fz12, known, scale12, dxy, rims, base = kernel(
        edge_kernel,
        shapes + [sds(8, NY), sds(CX, CY)],
        aliases={5 + i: i for i in range(6)},
    )(state, coarse, fine, x_chip, x_core, *inside)
    fresh, spectral, lines = kernel(
        phase_kernel,
        [sds(NPL, BX, NY), sds(CX, CY), sds(16, NY)],
        [
            pltpu.VMEM((4, BX, NY), F32),
            pltpu.VMEM((4, BX + 16, NY), F32),
            pltpu.VMEM((NPL, BX + 16, NY), F32),
            pltpu.VMEM((2, BX, NY), F32),
            pltpu.VMEM((2, BX, NY), F32),
            pltpu.VMEM((2, BX, NY), F32),
            pltpu.VMEM((2, BX, NY), F32),
            pltpu.VMEM((CX, NY), F32),
        ],
    )(coarse, own, fine, fx12, fz12, known, scale12, dxy, zb, za, base, consts)
    fresh, spectral = kernel(
        rim_kernel, [sds(NPL, BX, NY), sds(CX, CY)], aliases={11: 0}
    )(own, rims, x_chip, x_core, zb, za, lb, la, spectral, lines, consts, fresh)
    planes = lax.all_to_all(jnp.broadcast_to(spectral[None], (NNAR, CX, CY)), "narrow", 0, 0)
    state_new = kernel(
        solute_kernel,
        sds(2, NPL, BX, NY),
        [
            pltpu.VMEM((NPL, BX + 16, NY), F32),
            pltpu.VMEM((NPL, BX, NY), F32),
            pltpu.SemaphoreType.DMA((BX // 8 + NPL,)),
        ],
        far_outs=(0,),
    )(state, own, x_chip, x_core, zb, za, lb, la, fresh)
    f, to_chip, to_core, to_next = kernel(
        mode_kernel,
        [sds(CX, 8, CY), sds(16, CY), sds(16, CY), sds(8, CY)],
        [pltpu.VMEM((NNAR * CX, CY), F32)],
    )(planes, consts)
    by_core = lax.ppermute(to_core, "wide", CORES)
    by_next = lax.ppermute(to_next, BOTH, INWARD)
    by_chip = lax.ppermute(kernel(pass_kernel, sds(16, CY))(to_chip, by_core, consts), BOTH, CHIPS_LAST)
    adjusted = kernel(solve_kernel, sds(1, CX, CY), [pltpu.VMEM((CX, CY), F32)])(
        f, by_chip, by_core, by_next, coarse, consts
    )
    return state_new, adjusted


def solution(mesh):
    return jax.shard_map(
        on_device,
        mesh=mesh,
        in_specs=(
            P(None, "narrow", "wide", None),
            P("narrow", "wide", None),
            P("narrow", "wide", None),
            P("narrow", "wide", None),
            P(),
        ),
        out_specs=(P(None, "narrow", "wide", None), P("narrow", "wide", None)),
        check_vma=False,
    )
```

```python
import functools

import jax
import jax.numpy as jnp
import numpy as np
from jax import lax
from jax.experimental import pallas as pl
from jax.experimental.pallas import tpu as pltpu
from jax.sharding import PartitionSpec as P

F32 = jnp.float32
NNAR, NWIDE = 8, 32
NPL, BX, NY = 4, 64, 512
SPLIT = 24
ROUGH, EARLY, FACE = 128, 144, 144 + SPLIT
CORNERS, LATE = 64 - SPLIT, 72 - SPLIT
CX, CY = 16, 128
SUBX = 24
SIGMA, KBAR = 0.05, 0.75
DT = 0.15
VMEM = pl.BlockSpec(memory_space=pltpu.VMEM)
HBM = pl.BlockSpec(memory_space=pltpu.HBM)


def sds(*shape):
    return jax.ShapeDtypeStruct(shape, F32)


def params(mib):
    return pltpu.CompilerParams(vmem_limit_bytes=mib * 1024 * 1024)


def sine(points):
    k = np.arange(1, points + 1)
    return np.sqrt(2.0 / (points + 1)) * np.sin(np.pi * np.outer(k, k) / (points + 1))


def level(points):
    return 2.0 - 2.0 * np.cos(np.pi * np.arange(1, points + 1) / (points + 1))


SZ, SY = sine(8), sine(CY)
MEAN_Y = np.repeat(SY, 4, axis=0) / 64.0
SZ_ROWS = np.repeat(SZ[:, :, None], CY, 2)


def elimination():
    diag = SIGMA + KBAR * (level(8)[:, None] + level(CY)[None, :] + 2.0)
    inv = [1.0 / diag]
    for _ in range(SUBX - 1):
        inv.append(1.0 / (diag - KBAR * KBAR * inv[-1]))
    return np.stack(inv)


INVERSE = elimination()


LINK = KBAR * INVERSE
PASS = np.prod(LINK[4:20], axis=0)
MEET = 1.0 / (1.0 - LINK[11] ** 2)

CONSTS = np.concatenate(
    [SY, MEAN_Y, INVERSE.reshape(-1, CY), SZ_ROWS.reshape(-1, CY), PASS, MEET]
).astype(np.float32)
SY_AT, MEAN_AT, INV_AT, SZ_AT = slice(0, 128), slice(128, 640), 640, 640 + 8 * SUBX
PASS_AT = slice(SZ_AT + 64, SZ_AT + 72)
MEET_AT = slice(SZ_AT + 72, SZ_AT + 80)


def flat(n, w):
    return n * NWIDE + w


def everywhere(step):
    return [(flat(n, w), flat(*step(n, w))) for n in range(NNAR) for w in range(NWIDE)]


def swap_b(n, w):
    return (n, w ^ 1) if n in (0, NNAR - 1) else (((n + 1) ^ 1) - 1, w)


def swap_chips(n, w):
    if w in (0, NWIDE - 1):
        return (n ^ 4, w) if n % 4 in (1, 2) else (n, NWIDE - 1 - w)
    return n, ((w + 1) ^ 1) - 1


def swap_chips_last(n, w):
    return (n ^ 1, w) if w in (0, NWIDE - 1) else (n, ((w + 1) ^ 1) - 1)


def inward(n, w):
    to = w + 2 if w % 2 else w - 2
    return n, to if 0 <= to < NWIDE else w ^ 1


BOTH = ("narrow", "wide")
PAIR_A = [(i, i ^ 1) for i in range(NNAR)]
CORES = [(i, i ^ 1) for i in range(NWIDE)]
PAIR_B, CHIPS = everywhere(swap_b), everywhere(swap_chips)
INWARD, CHIPS_LAST = everywhere(inward), everywhere(swap_chips_last)


def lanes(v):
    return lax.broadcasted_iota(jnp.int32, v.shape, v.ndim - 1)


def rows_of(v):
    return lax.broadcasted_iota(jnp.int32, v.shape, len(v.shape) - 2)


def y_up(v):
    n = v.shape[-1]
    return jnp.where(lanes(v) == n - 1, 0.0, pltpu.roll(v, n - 1, v.ndim - 1))


def y_down(v):
    return jnp.where(lanes(v) == 0, 0.0, pltpu.roll(v, 1, v.ndim - 1))


def x_up(v, after):
    return pltpu.roll(jnp.where(rows_of(v) == 0, after, v), 7, v.ndim - 2)


def x_down(v, before):
    return pltpu.roll(jnp.where(rows_of(v) == 7, before, v), 1, v.ndim - 2)


def inverse(v):
    guess = pl.reciprocal(v, approx=True)
    return guess * (2.0 - v * guess)


def weigh(dz, dx, dy, c2, s2):
    q0, a, b = dz * dz, dx * dx, dy * dy
    r = a + b
    uv = s2 * (b - a) + c2 * (dx * dy)
    num = q0 * q0 + r * r - 2.0 * (uv * uv)
    over = inverse(q0 + r + 4.0)
    return 0.55 + 0.6 * (num * (over * over))


def flag(cond):
    return jnp.where(cond, 1.0, 0.0).astype(F32)


def spread(v):
    lane = lax.shift_right_logical(lanes(v), 2)
    return jnp.concatenate(
        [jnp.take_along_axis(v, lane + 32 * j, axis=1) for j in range(NY // CY)], 1
    )


def halves(v):
    high = v.astype(jnp.bfloat16)
    return high, (v - high.astype(F32)).astype(jnp.bfloat16)


def dot(a, b):
    (a1, a2), (b1, b2) = halves(a), halves(b)
    mul = functools.partial(jnp.dot, preferred_element_type=F32)
    return mul(a1, b1) + (mul(a1, b2) + mul(a2, b1))


def stage_kernel(
    state_in, ids_in, frozen_in, temp_in, angles_in,
    face_b, face_a, state, coarse,
    ids, frozen, temp, angles, sems,
):
    copies = [
        pltpu.make_async_copy(src, dst, sems.at[i])
        for i, (src, dst) in enumerate(
            [
                (state_in.at[0], state.at[0]),
                (state_in.at[1], state.at[1]),
                (ids_in, ids),
                (frozen_in, frozen),
                (temp_in, temp),
                (angles_in, angles),
            ]
        )
    ]
    for copy in copies[2:] + copies[:2]:
        copy.start()
    for copy in copies[2:]:
        copy.wait()
    table = jnp.concatenate([angles[...], angles[...]], 1)
    c = jnp.take_along_axis(jnp.broadcast_to(jnp.cos(table), (CX, CY)), ids[0], axis=1)
    s = jnp.take_along_axis(jnp.broadcast_to(jnp.sin(table), (CX, CY)), ids[0], axis=1)
    coarse[0] = c * c - s * s
    coarse[1] = c * s
    coarse[2] = temp[0]
    coarse[3] = -0.5 * frozen[0].astype(F32)
    even = lax.rem(lax.axis_index("narrow"), 2) == 0
    for ref in (face_b, face_a):
        for k in range(4):
            ref[ROUGH:EARLY, k * CY : (k + 1) * CY] = coarse[k]
    copies[0].wait()
    for ref, top in ((face_b, jnp.logical_not(even)), (face_a, even)):
        first = jnp.where(top, 2, 0)
        ref[0:BX] = state[0, first]
        ref[BX : 2 * BX] = state[0, first + 1]
    copies[1].wait()
    for ref, top in ((face_b, jnp.logical_not(even)), (face_a, even)):
        ref[EARLY:FACE] = state[1, jnp.where(top, 3, 0), 0:SPLIT]


def column_kernel(state, coarse, x_chip, x_core):
    core0 = lax.rem(lax.axis_index("wide"), 2) == 0
    for ref, low in ((x_chip, core0), (x_core, jnp.logical_not(core0))):
        for z in range(NPL):
            for at, ch, first, last in ((0, 0, 0, BX - 1), (4, 0, 1, BX - 2), (8, 1, 0, BX - 1)):
                ref[at + z : at + z + 1] = jnp.where(
                    low, state[ch, z, first : first + 1], state[ch, z, last : last + 1]
                )
        for k in range(4):
            ref[12:13, k * CY : (k + 1) * CY] = jnp.where(
                low, coarse[k, 0:1], coarse[k, CX - 1 : CX]
            )
        ref[13:16] = jnp.zeros((3, NY), F32)


def x_sides(x_chip, x_core, rows):
    w = lax.axis_index("wide")
    core0 = lax.rem(w, 2) == 0
    left = jnp.where(core0, x_chip[rows], x_core[rows]) * flag(w > 0)
    right = jnp.where(core0, x_core[rows], x_chip[rows]) * flag(w < NWIDE - 1)
    return left, right


def late_kernel(state, x_chip, x_core, own, late_b, late_a):
    even = lax.rem(lax.axis_index("narrow"), 2) == 0
    left, right = x_sides(x_chip, x_core, slice(0, 8))
    for ref, top in ((late_b, jnp.logical_not(even)), (late_a, even)):
        ref[0:CORNERS] = state[1, jnp.where(top, 3, 0), SPLIT:BX]
        ref[CORNERS : CORNERS + 1] = jnp.where(top, left[3:4], left[0:1])
        ref[CORNERS + 1 : CORNERS + 2] = jnp.where(top, right[3:4], right[0:1])
        ref[CORNERS + 2 : LATE] = jnp.zeros((LATE - CORNERS - 2, NY), F32)


def widen(ref, at, rough):
    for k in range(CX):
        ref[at, 4 * k : 4 * k + 4] = jnp.broadcast_to(rough[k : k + 1], (4, NY))


def spread_kernel(coarse, fine):
    for k in range(3):
        widen(fine, k, spread(coarse[k]))


def local_terms(c, state, own, fine, fx, fz, known, scale, dxy):
    r0 = 8 * c
    here, at, after = pl.ds(r0, 8), pl.ds(r0 + 8, 8), pl.ds(r0 + 16, 8)
    for z in range(NPL):
        v = own[z, at]
        dx = x_up(v, own[z, after]) - x_down(v, own[z, here])
        dy = y_up(v) - y_down(v)
        m = 1.0 - v * v
        drive = m * (v - 1.5 * (state[1, z, here] + fine[2, here]) * m)
        if z in (0, NPL - 1):
            known[z, here] = drive
            dxy[z // 2, 0, here] = dx
            dxy[z // 2, 1, here] = dy
            continue
        dz = own[z + 1, at] - own[z - 1, at]
        an = weigh(dz, dx, dy, fine[0, here], fine[1, here])
        wt = an * an
        quarter = 0.25 * wt
        fz[z - 1, here] = quarter * dz
        fx[z - 1, here] = quarter * dx
        fy = quarter * dy
        known[z, here] = (y_up(fy) - y_down(fy)) + drive
        scale[z - 1, here] = DT * inverse(wt)


def inside_kernel(state, fine, consts_in, own, fx, fz, known, scale, dxy, consts, sem):
    fetch = pltpu.make_async_copy(consts_in, consts, sem)
    fetch.start()
    for z in range(NPL):
        own[z, 8 : 8 + BX] = state[0, z]

    def chunk(c, carry):
        local_terms(c, state, own, fine, fx, fz, known, scale, dxy)
        return carry

    for c in range(1, BX // 8 - 1):
        chunk(c, 0)
    fetch.wait()


def edge_kernel(
    state, coarse, fine, x_chip, x_core, own_in, fx_in, fz_in, known_in, scale_in, dxy_in,
    own, fx, fz, known, scale, dxy, rims, base,
):
    left, right = x_sides(x_chip, x_core, slice(0, 4))
    for z in range(NPL):
        own[z, 7:8] = left[z : z + 1]
        own[z, 8 + BX : 9 + BX] = right[z : z + 1]
    left, right = x_sides(x_chip, x_core, slice(12, 13))
    rows = [side[:, k * CY : (k + 1) * CY] for side in (left, right) for k in (0, 1)]
    rims[...] = spread(jnp.concatenate(rows + rows, 0))
    for c in (0, BX // 8 - 1):
        local_terms(c, state, own, fine, fx, fz, known, scale, dxy)
    t, e = coarse[2], coarse[3]
    row = rows_of(t)
    down, up = [], []
    for k, v in ((2, t), (3, e)):
        before, after = left[:, k * CY : (k + 1) * CY], right[:, k * CY : (k + 1) * CY]
        down.append(jnp.where(row == 0, before, pltpu.roll(v, 1, 0)))
        up.append(jnp.where(row == CX - 1, after, pltpu.roll(v, CX - 1, 0)))
    near = [tuple(down), tuple(up), (y_up(t), y_up(e)), (y_down(t), y_down(e))]
    total = jnp.zeros_like(t)
    for tn, en in near:
        total = total + (1.0 + 0.5 * (e + en)) * (tn - t)
    base[...] = total


def phase_kernel(
    coarse, own, fine, fx12, fz12, known, scale12, dxy, zb, za, base, consts,
    fresh, spectral, lines,
    sides, halo, fx, fz03, fzout, bent, scale03, change,
):
    n = lax.axis_index("narrow")
    even = lax.rem(n, 2) == 0
    has_low, has_high = flag(n > 0), flag(n < NNAR - 1)
    for face, at, there in (
        (zb, jnp.where(even, 0, 2), jnp.where(even, has_low, has_high)),
        (za, jnp.where(even, 2, 0), jnp.where(even, has_high, has_low)),
    ):
        for k in range(2):
            halo[at + k, 8 : 8 + BX] = face[k * BX : (k + 1) * BX] * there
    low = jnp.where(even, zb[ROUGH:EARLY], za[ROUGH:EARLY])
    high = jnp.where(even, za[ROUGH:EARLY], zb[ROUGH:EARLY])
    for k, v in enumerate((low, low, high, high)):
        wide = spread(v[:, (k % 2) * CY : (k % 2 + 1) * CY])
        sides[k] = wide
        lines[8 + 4 * (k % 2) + 2 * (k // 2) : 9 + 4 * (k % 2) + 2 * (k // 2)] = wide[0:1]
        lines[9 + 4 * (k % 2) + 2 * (k // 2) : 10 + 4 * (k % 2) + 2 * (k // 2)] = wide[CX - 1 : CX]
    t, e = coarse[2], coarse[3]
    still = base[...]
    for v, there in ((low, has_low), (high, has_high)):
        tn, en = v[:, 2 * CY : 3 * CY] * there, v[:, 3 * CY :] * there
        still = still + (1.0 + 0.5 * (e + en)) * (tn - t)
    for z in range(NPL):
        fx[z, 7:8] = jnp.zeros((1, NY), F32)
        fx[z, 8 + BX : 9 + BX] = jnp.zeros((1, NY), F32)
    for z in (1, 2):
        fx[z, 8 : 8 + BX] = fx12[z - 1]
    planes = [(halo, 0), (halo, 1), (own, 0), (own, 1), (own, 2), (own, 3), (halo, 2), (halo, 3)]

    def get(k, rows):
        ref, z = planes[k]
        return ref[z, rows]

    def fluxes(c, carry):
        r0 = 8 * c
        here, at, after = pl.ds(r0, 8), pl.ds(r0 + 8, 8), pl.ds(r0 + 16, 8)
        for side, (zz, there) in enumerate(((0, has_low), (5, has_high))):
            v = get(zz + 1, at)
            dz = get(zz + 2, at) - get(zz, at)
            dx = x_up(v, get(zz + 1, after)) - x_down(v, get(zz + 1, here))
            dy = y_up(v) - y_down(v)
            c2, s2 = (
                jnp.where(
                    rows_of(v) < 4, sides[k, 2 * c : 2 * c + 1], sides[k, 2 * c + 1 : 2 * c + 2]
                )
                for k in (2 * side, 2 * side + 1)
            )
            an = weigh(dz, dx, dy, c2, s2)
            fzout[side, here] = (0.25 * there) * (an * an * dz)
        for side, z in enumerate((0, NPL - 1)):
            dz = get(z + 3, at) - get(z + 1, at)
            dx, dy = dxy[side, 0, here], dxy[side, 1, here]
            an = weigh(dz, dx, dy, fine[0, here], fine[1, here])
            wt = an * an
            quarter = 0.25 * wt
            fz03[side, here] = quarter * dz
            fx[z, at] = quarter * dx
            fy = quarter * dy
            bent[side, here] = known[z, here] + (y_up(fy) - y_down(fy))
            scale03[side, here] = DT * inverse(wt)
        return carry

    for c in range(BX // 8):
        fluxes(c, 0)

    for side in range(2):
        for row in (0, BX - 1):
            fzout[side, row : row + 1] = jnp.zeros((1, NY), F32)
    flux_z = [(fzout, 0), (fz03, 0), (fz12, 0), (fz12, 1), (fz03, 1), (fzout, 1)]
    rest = [(bent, 0), (known, 1), (known, 2), (bent, 1)]
    scales = [(scale03, 0), (scale12, 0), (scale12, 1), (scale03, 1)]

    for c in range(BX // 8):
        here, at, after = pl.ds(8 * c, 8), pl.ds(8 * c + 8, 8), pl.ds(8 * c + 16, 8)
        total = jnp.zeros((8, NY), F32)
        for z in range(NPL):
            p, f = own[z, at], fx[z, at]
            spread_z = flux_z[z + 2][0][flux_z[z + 2][1], here] - flux_z[z][0][flux_z[z][1], here]
            spread_x = x_up(f, fx[z, after]) - x_down(f, fx[z, here])
            factor = scales[z][0][scales[z][1], here]
            rise = factor * (rest[z][0][rest[z][1], here] + spread_z + spread_x)
            total = total + rise
            if c in (0, BX // 8 - 1):
                row, line = (0, z) if c == 0 else (7, NPL + z)
                lines[line : line + 1] = factor[row : row + 1]
            fresh[z, here] = p + rise
        total = total + pltpu.roll(total, 1, 0)
        total = total + pltpu.roll(total, 2, 0)
        change[2 * c : 2 * c + 1] = total[3:4]
        change[2 * c + 1 : 2 * c + 2] = total[7:8]
    spectral[...] = dot(still, consts[SY_AT]) + dot(change[...], consts[MEAN_AT])


def rim_kernel(
    own, rims, x_chip, x_core, zb, za, lb, la, spectral_in, lines, consts, fresh_in,
    fresh, spectral,
):
    n, w = lax.axis_index("narrow"), lax.axis_index("wide")
    even = lax.rem(n, 2) == 0
    has_left, has_right = flag(w > 0), flag(w < NWIDE - 1)
    has_low, has_high = flag(n > 0), flag(n < NNAR - 1)
    inner = x_sides(x_chip, x_core, slice(4, 8))

    def beyond(b, a, rows, high):
        if high:
            return jnp.where(even, a[rows], b[rows]) * has_high
        return jnp.where(even, b[rows], a[rows]) * has_low

    def corner(high, s):
        return beyond(lb, la, slice(CORNERS + s, CORNERS + s + 1), high)

    def outer(high, plane, x):
        return beyond(zb, za, slice(plane * BX + x, plane * BX + x + 1), high)

    rim = (7, 8 + BX)
    values = [[], [], [], [], []]
    for s in range(2):
        for z in range(NPL):
            at = slice(rim[s], rim[s] + 1)
            here = own[z, at]
            below = own[z - 1, at] if z > 0 else corner(False, s)
            above = own[z + 1, at] if z < NPL - 1 else corner(True, s)
            side = inner[s][z : z + 1]
            x_lo, x_hi = (own[z, 7 + BX : 8 + BX], side) if s else (side, own[z, 8:9])
            for rows, v in zip(values, (here, below, above, x_lo, x_hi)):
                rows.append(v)
    for high in (False, True):
        for s in range(2):
            x, near = (BX - 1, BX - 2) if s else (0, 1)
            mine = own[NPL - 1 if high else 0, 8 + x : 9 + x]
            here, behind = outer(high, 0 if high else 1, x), outer(high, 1 if high else 0, x)
            beside, past = outer(high, 0 if high else 1, near), corner(high, s)
            below, above = (mine, behind) if high else (behind, mine)
            x_lo, x_hi = (beside, past) if s else (past, beside)
            for rows, v in zip(values, (here, below, above, x_lo, x_hi)):
                rows.append(v)
    here, below, above, x_lo, x_hi = (
        jnp.concatenate(rows + [jnp.zeros((4, NY), F32)], 0) for rows in values
    )
    c2, s2 = (
        jnp.concatenate(
            [jnp.broadcast_to(rims[k : k + 1], (NPL, NY)), jnp.broadcast_to(rims[k + 2 : k + 3], (NPL, NY)),
             lines[8 + 4 * k : 12 + 4 * k], jnp.zeros((4, NY), F32)], 0,
        )
        for k in (0, 1)
    )
    dz, dx, dy = above - below, x_hi - x_lo, y_up(here) - y_down(here)
    an = weigh(dz, dx, dy, c2, s2)
    quarter = 0.25 * (an * an)
    row = rows_of(here[0:8])
    x_part = quarter[0:8] * dx[0:8] * jnp.where(row < NPL, -has_left, has_right)
    z_flux = quarter[8:16] * dz[8:16]
    z_part = jnp.zeros((8, NY), F32)
    for high in (False, True):
        for s in range(2):
            line = z_flux[2 * high + s : 2 * high + s + 1]
            line = line * has_high if high else -has_low * line
            z_part = jnp.where(row == NPL * s + (NPL - 1 if high else 0), line, z_part)
    rise = lines[0:8] * (x_part + z_part)
    for c in range(2):
        for z in range(NPL):
            add = rise[NPL * c + z : NPL * c + z + 1]
            at = (BX - 1) * c
            fresh[z, at : at + 1] = fresh_in[z, at : at + 1] + add
    sums = [jnp.sum(rise[NPL * c : NPL * (c + 1)], axis=0, keepdims=True) for c in range(2)]
    more = dot(jnp.concatenate(sums + [jnp.zeros((14, NY), F32)], 0), consts[MEAN_AT])
    first = rows_of(spectral_in)
    moved = spectral_in[...] + jnp.where(
        first == 0, more[0:1], jnp.where(first == CX - 1, more[1:2], 0.0)
    )
    spectral[...] = moved


def solute_kernel(state, own, x_chip, x_core, zb, za, lb, la, fresh, out, sown, grown, sems):
    phase_out = [
        pltpu.make_async_copy(fresh.at[z], out.at[0, z], sems.at[8 + z]) for z in range(NPL)
    ]
    for copy in phase_out:
        copy.start()
    n = lax.axis_index("narrow")
    even = lax.rem(n, 2) == 0
    left, right = x_sides(x_chip, x_core, slice(8, 12))
    has_low, has_high = flag(n > 0), flag(n < NNAR - 1)
    for z in range(NPL):
        sown[z, 8 : 8 + BX] = state[1, z]
        sown[z, 7:8] = left[z : z + 1]
        sown[z, 8 + BX : 9 + BX] = right[z : z + 1]

    def step(c):
        r0 = 8 * c
        here, at, after = pl.ds(r0, 8), pl.ds(r0 + 8, 8), pl.ds(r0 + 16, 8)

        beyond = pl.ds(r0 + BX, 8)
        ps = (
            [has_low * jnp.where(even, zb[beyond], za[beyond])]
            + [own[z, at] for z in range(NPL)]
            + [has_high * jnp.where(even, za[here], zb[here])]
        )
        if r0 < SPLIT:
            (b, a), there = (zb, za), pl.ds(EARLY + r0, 8)
        else:
            (b, a), there = (lb, la), pl.ds(r0 - SPLIT, 8)
        ss = (
            [has_low * jnp.where(even, b[there], a[there])]
            + [sown[z, at] for z in range(NPL)]
            + [has_high * jnp.where(even, a[there], b[there])]
        )
        for z in range(NPL):
            p, s = ps[z + 1], ss[z + 1]
            q = 0.55 - 0.25 * p
            near = [
                (ps[z], ss[z]),
                (ps[z + 2], ss[z + 2]),
                (x_up(p, own[z, after]), x_up(s, sown[z, after])),
                (x_down(p, own[z, here]), x_down(s, sown[z, here])),
                (y_up(p), y_up(s)),
                (y_down(p), y_down(s)),
            ]
            total = jnp.zeros_like(p)
            for pn, sn in near:
                total = total + (q - 0.25 * pn) * (sn - s)
            grown[z, here] = s + DT * total + (0.5 + 0.425 * s) * (fresh[z, here] - p)
        store(c).start()

    def store(c):
        rows = pl.ds(8 * c, 8)
        return pltpu.make_async_copy(grown.at[:, rows], out.at[1, :, rows], sems.at[c])

    for c in range(BX // 8):
        step(c)
    for c in range(BX // 8):
        store(c).wait()
    for copy in phase_out:
        copy.wait()


def eliminate(state, f, consts, first):
    states = []
    for i, v in enumerate(f):
        inv = consts[INV_AT + 8 * (first + i) : INV_AT + 8 * (first + i) + 8]
        state = inv * v if state is None else inv * v + (KBAR * inv) * state
        states.append(state)
    return states


def back(x, states, consts, first):
    values = []
    for i in range(len(states) - 1, -1, -1):
        inv = consts[INV_AT + 8 * (first + i) : INV_AT + 8 * (first + i) + 8]
        x = states[i] + (KBAR * inv) * x
        values.append(x)
    return values[::-1]


def mode_kernel(planes, consts, f, to_chip, to_core, to_next, modes):
    half = NNAR // 2
    folded = [
        [planes[m] + planes[NNAR - 1 - m] for m in range(half)],
        [planes[m] - planes[NNAR - 1 - m] for m in range(half)],
    ]
    for k in range(NNAR):
        total = float(SZ[k, 0]) * folded[k % 2][0]
        for m in range(1, half):
            total = total + float(SZ[k, m]) * folded[k % 2][m]
        modes[k * CX : (k + 1) * CX] = total
    values = [modes[pl.ds(j, 8, stride=CX), :] for j in range(CX)]
    for j in range(CX):
        f[j] = values[j]
    mirrored = values[::-1]
    right_margin = eliminate(None, values[12:], consts, 0)[-1]
    left_margin = eliminate(None, mirrored[12:], consts, 0)[-1]
    right_core = eliminate(None, values, consts, 4)[-1]
    left_core = eliminate(None, mirrored, consts, 4)[-1]
    core0 = lax.rem(lax.axis_index("wide"), 2) == 0
    to_core[0:8] = jnp.where(core0, right_margin, left_margin)
    to_core[8:16] = jnp.where(core0, right_core, left_core)
    to_chip[0:8] = jnp.where(core0, left_margin, right_margin)
    to_chip[8:16] = jnp.where(core0, left_core, right_core)
    to_next[...] = to_chip[0:8]


def pass_kernel(to_chip, by_core, consts, message):
    message[0:8] = to_chip[0:8]
    message[8:16] = to_chip[8:16] + consts[PASS_AT] * by_core[0:8]


def solve_kernel(f, by_chip, by_core, by_next, coarse, consts, out, rows):
    n, w = lax.axis_index("narrow"), lax.axis_index("wide")
    core0 = lax.rem(w, 2) == 0
    has_left, has_right = flag(w > 0), flag(w < NWIDE - 1)
    beyond = consts[PASS_AT] * by_next[...] * jnp.where(core0, flag(w < NWIDE - 2), flag(w > 1))
    other = jnp.concatenate([by_core[0:8], by_core[8:16] + beyond], 0)
    left = jnp.where(core0, by_chip[...], other) * has_left
    right = jnp.where(core0, other, by_chip[...]) * has_right
    values = [f[j] for j in range(CX)]
    mirrored = values[::-1]
    half = CX // 2

    low = eliminate(left[0:8], values[:half], consts, 4)
    high = eliminate(right[0:8], mirrored[:half], consts, 4)
    link = KBAR * consts[INV_AT + 8 * 11 : INV_AT + 8 * 12]
    x_low = consts[MEET_AT] * (low[-1] + link * high[-1])
    x_high = consts[MEET_AT] * (high[-1] + link * low[-1])
    x = back(x_low, low[:-1], consts, 4) + [x_low]
    x += (back(x_high, high[:-1], consts, 4) + [x_high])[::-1]

    for here, near, there in (
        (range(4), left, has_left),
        (range(CX - 1, CX - 5, -1), right, has_right),
    ):
        states = eliminate(near[8:16], [values[j] for j in here], consts, 20)
        found = back(states[-1], states[:-1], consts, 20) + [states[-1]]
        for j, v in zip(here, found):
            x[j] = x[j] + there * v

    weight = consts[pl.ds(pl.multiple_of(SZ_AT + 8 * n, 8), 8)]
    for j in range(CX):
        rows[j : j + 1] = jnp.sum(x[j] * weight, axis=0, keepdims=True)
    out[0] = coarse[2] + dot(rows[...], consts[SY_AT])


def kernel(body, outs, scratch=(), far=(), far_outs=(), aliases=None, mib=16):
    many = isinstance(outs, (list, tuple))

    def call(*args):
        return pl.pallas_call(
            body,
            out_shape=outs,
            in_specs=[HBM if i in far else VMEM for i in range(len(args))],
            out_specs=[HBM if i in far_outs else VMEM for i in range(len(outs))] if many else (HBM if far_outs else VMEM),
            input_output_aliases=aliases or {},
            scratch_shapes=list(scratch),
            compiler_params=params(mib),
            name=body.__name__,
        )(*args)

    return call


def afar(v):
    return pltpu.with_memory_space_constraint(v, pltpu.HBM)


def on_device(state_in, ids, frozen, temp, angles):
    inputs = [afar(v) for v in (state_in, ids, frozen, temp, angles.reshape(1, -1))]
    face_b, face_a, state, coarse = kernel(
        stage_kernel,
        [sds(FACE, NY)] * 2 + [sds(2, NPL, BX, NY), sds(4, CX, CY)],
        [
            pltpu.VMEM((1, CX, CY), jnp.int32),
            pltpu.VMEM((1, CX, CY), jnp.int32),
            pltpu.VMEM((1, CX, CY), F32),
            pltpu.VMEM((1, 64), F32),
            pltpu.SemaphoreType.DMA((6,)),
        ],
        far=range(5),
    )(*inputs)
    zb = lax.ppermute(face_b, BOTH, PAIR_B)
    za = lax.ppermute(face_a, "narrow", PAIR_A)
    to_chip, to_core = kernel(column_kernel, [sds(16, NY)] * 2)(state, coarse)
    x_chip = lax.ppermute(to_chip, BOTH, CHIPS)
    x_core = lax.ppermute(to_core, "wide", CORES)
    fine = kernel(spread_kernel, sds(3, BX, NY))(coarse)
    shapes = [
        sds(NPL, BX + 16, NY), sds(2, BX, NY), sds(2, BX, NY), sds(NPL, BX, NY), sds(2, BX, NY),
        sds(2, 2, BX, NY),
    ]
    *inside, consts = kernel(
        inside_kernel, shapes + [sds(*CONSTS.shape)], [pltpu.SemaphoreType.DMA], far=(2,)
    )(state, fine, afar(jnp.asarray(CONSTS)))
    late_b, late_a = kernel(late_kernel, [sds(LATE, NY)] * 2)(state, x_chip, x_core, inside[0])
    lb = lax.ppermute(late_b, BOTH, PAIR_B)
    la = lax.ppermute(late_a, "narrow", PAIR_A)
    own, fx12, fz12, known, scale12, dxy, rims, base = kernel(
        edge_kernel,
        shapes + [sds(8, NY), sds(CX, CY)],
        aliases={5 + i: i for i in range(6)},
    )(state, coarse, fine, x_chip, x_core, *inside)
    fresh, spectral, lines = kernel(
        phase_kernel,
        [sds(NPL, BX, NY), sds(CX, CY), sds(16, NY)],
        [
            pltpu.VMEM((4, CX, NY), F32),
            pltpu.VMEM((4, BX + 16, NY), F32),
            pltpu.VMEM((NPL, BX + 16, NY), F32),
            pltpu.VMEM((2, BX, NY), F32),
            pltpu.VMEM((2, BX, NY), F32),
            pltpu.VMEM((2, BX, NY), F32),
            pltpu.VMEM((2, BX, NY), F32),
            pltpu.VMEM((CX, NY), F32),
        ],
    )(coarse, own, fine, fx12, fz12, known, scale12, dxy, zb, za, base, consts)
    fresh, spectral = kernel(
        rim_kernel, [sds(NPL, BX, NY), sds(CX, CY)], aliases={11: 0}
    )(own, rims, x_chip, x_core, zb, za, lb, la, spectral, lines, consts, fresh)
    planes = lax.all_to_all(jnp.broadcast_to(spectral[None], (NNAR, CX, CY)), "narrow", 0, 0)
    state_new = kernel(
        solute_kernel,
        sds(2, NPL, BX, NY),
        [
            pltpu.VMEM((NPL, BX + 16, NY), F32),
            pltpu.VMEM((NPL, BX, NY), F32),
            pltpu.SemaphoreType.DMA((BX // 8 + NPL,)),
        ],
        far_outs=(0,),
    )(state, own, x_chip, x_core, zb, za, lb, la, fresh)
    f, to_chip, to_core, to_next = kernel(
        mode_kernel,
        [sds(CX, 8, CY), sds(16, CY), sds(16, CY), sds(8, CY)],
        [pltpu.VMEM((NNAR * CX, CY), F32)],
    )(planes, consts)
    by_core = lax.ppermute(to_core, "wide", CORES)
    by_next = lax.ppermute(to_next, BOTH, INWARD)
    by_chip = lax.ppermute(kernel(pass_kernel, sds(16, CY))(to_chip, by_core, consts), BOTH, CHIPS_LAST)
    adjusted = kernel(solve_kernel, sds(1, CX, CY), [pltpu.VMEM((CX, CY), F32)])(
        f, by_chip, by_core, by_next, coarse, consts
    )
    return state_new, adjusted


def solution(mesh):
    return jax.shard_map(
        on_device,
        mesh=mesh,
        in_specs=(
            P(None, "narrow", "wide", None),
            P("narrow", "wide", None),
            P("narrow", "wide", None),
            P("narrow", "wide", None),
            P(),
        ),
        out_specs=(P(None, "narrow", "wide", None), P("narrow", "wide", None)),
        check_vma=False,
    )
```

```python
import functools

import jax
import jax.numpy as jnp
import numpy as np
from jax import lax
from jax.experimental import pallas as pl
from jax.experimental.pallas import tpu as pltpu
from jax.sharding import PartitionSpec as P

F32 = jnp.float32
NNAR, NWIDE = 8, 32
NPL, BX, NY = 4, 64, 512
SPLIT = 16
ROUGH, EARLY, FACE = 128, 144, 144 + SPLIT
CORNERS, LATE = 64 - SPLIT, 72 - SPLIT
CX, CY = 16, 128
SUBX = 24
SIGMA, KBAR = 0.05, 0.75
DT = 0.15
VMEM = pl.BlockSpec(memory_space=pltpu.VMEM)
HBM = pl.BlockSpec(memory_space=pltpu.HBM)


def sds(*shape):
    return jax.ShapeDtypeStruct(shape, F32)


def params(mib):
    return pltpu.CompilerParams(vmem_limit_bytes=mib * 1024 * 1024)


def sine(points):
    k = np.arange(1, points + 1)
    return np.sqrt(2.0 / (points + 1)) * np.sin(np.pi * np.outer(k, k) / (points + 1))


def level(points):
    return 2.0 - 2.0 * np.cos(np.pi * np.arange(1, points + 1) / (points + 1))


SZ, SY = sine(8), sine(CY)
MEAN_Y = np.repeat(SY, 4, axis=0) / 64.0
SZ_ROWS = np.repeat(SZ[:, :, None], CY, 2)


def elimination():
    diag = SIGMA + KBAR * (level(8)[:, None] + level(CY)[None, :] + 2.0)
    inv = [1.0 / diag]
    for _ in range(SUBX - 1):
        inv.append(1.0 / (diag - KBAR * KBAR * inv[-1]))
    return np.stack(inv)


INVERSE = elimination()


LINK = KBAR * INVERSE
PASS = np.prod(LINK[4:20], axis=0)
MEET = 1.0 / (1.0 - LINK[11] ** 2)

CONSTS = np.concatenate(
    [SY, MEAN_Y, INVERSE.reshape(-1, CY), SZ_ROWS.reshape(-1, CY), PASS, MEET]
).astype(np.float32)
SY_AT, MEAN_AT, INV_AT, SZ_AT = slice(0, 128), slice(128, 640), 640, 640 + 8 * SUBX
PASS_AT = slice(SZ_AT + 64, SZ_AT + 72)
MEET_AT = slice(SZ_AT + 72, SZ_AT + 80)


def flat(n, w):
    return n * NWIDE + w


def everywhere(step):
    return [(flat(n, w), flat(*step(n, w))) for n in range(NNAR) for w in range(NWIDE)]


def swap_b(n, w):
    return (n, w ^ 1) if n in (0, NNAR - 1) else (((n + 1) ^ 1) - 1, w)


def swap_chips(n, w):
    if w in (0, NWIDE - 1):
        return (n ^ 4, w) if n % 4 in (1, 2) else (n, NWIDE - 1 - w)
    return n, ((w + 1) ^ 1) - 1


def swap_chips_last(n, w):
    return (n ^ 1, w) if w in (0, NWIDE - 1) else (n, ((w + 1) ^ 1) - 1)


def inward(n, w):
    to = w + 2 if w % 2 else w - 2
    return n, to if 0 <= to < NWIDE else w ^ 1


BOTH = ("narrow", "wide")
PAIR_A = [(i, i ^ 1) for i in range(NNAR)]
CORES = [(i, i ^ 1) for i in range(NWIDE)]
PAIR_B, CHIPS = everywhere(swap_b), everywhere(swap_chips)
INWARD, CHIPS_LAST = everywhere(inward), everywhere(swap_chips_last)


def lanes(v):
    return lax.broadcasted_iota(jnp.int32, v.shape, v.ndim - 1)


def rows_of(v):
    return lax.broadcasted_iota(jnp.int32, v.shape, len(v.shape) - 2)


def y_up(v):
    n = v.shape[-1]
    return jnp.where(lanes(v) == n - 1, 0.0, pltpu.roll(v, n - 1, v.ndim - 1))


def y_down(v):
    return jnp.where(lanes(v) == 0, 0.0, pltpu.roll(v, 1, v.ndim - 1))


def x_up(v, after):
    return pltpu.roll(jnp.where(rows_of(v) == 0, after, v), 7, v.ndim - 2)


def x_down(v, before):
    return pltpu.roll(jnp.where(rows_of(v) == 7, before, v), 1, v.ndim - 2)


def inverse(v):
    guess = pl.reciprocal(v, approx=True)
    return guess * (2.0 - v * guess)


def weigh(dz, dx, dy, c2, s2):
    q0, a, b = dz * dz, dx * dx, dy * dy
    r = a + b
    uv = s2 * (b - a) + c2 * (dx * dy)
    num = q0 * q0 + r * r - 2.0 * (uv * uv)
    over = inverse(q0 + r + 4.0)
    return 0.55 + 0.6 * (num * (over * over))


def flag(cond):
    return jnp.where(cond, 1.0, 0.0).astype(F32)


def spread(v):
    lane = lax.shift_right_logical(lanes(v), 2)
    return jnp.concatenate(
        [jnp.take_along_axis(v, lane + 32 * j, axis=1) for j in range(NY // CY)], 1
    )


def halves(v):
    high = v.astype(jnp.bfloat16)
    return high, (v - high.astype(F32)).astype(jnp.bfloat16)


def dot(a, b):
    (a1, a2), (b1, b2) = halves(a), halves(b)
    mul = functools.partial(jnp.dot, preferred_element_type=F32)
    return mul(a1, b1) + (mul(a1, b2) + mul(a2, b1))


def stage_kernel(
    state_in, ids_in, frozen_in, temp_in, angles_in,
    face_b, face_a, state, coarse,
    ids, frozen, temp, angles, sems,
):
    copies = [
        pltpu.make_async_copy(src, dst, sems.at[i])
        for i, (src, dst) in enumerate(
            [
                (state_in.at[0], state.at[0]),
                (state_in.at[1], state.at[1]),
                (ids_in, ids),
                (frozen_in, frozen),
                (temp_in, temp),
                (angles_in, angles),
            ]
        )
    ]
    for copy in copies[2:] + copies[:2]:
        copy.start()
    for copy in copies[2:]:
        copy.wait()
    table = jnp.concatenate([angles[...], angles[...]], 1)
    c = jnp.take_along_axis(jnp.broadcast_to(jnp.cos(table), (CX, CY)), ids[0], axis=1)
    s = jnp.take_along_axis(jnp.broadcast_to(jnp.sin(table), (CX, CY)), ids[0], axis=1)
    coarse[0] = c * c - s * s
    coarse[1] = c * s
    coarse[2] = temp[0]
    coarse[3] = -0.5 * frozen[0].astype(F32)
    even = lax.rem(lax.axis_index("narrow"), 2) == 0
    for ref in (face_b, face_a):
        for k in range(4):
            ref[ROUGH:EARLY, k * CY : (k + 1) * CY] = coarse[k]
    copies[0].wait()
    for ref, top in ((face_b, jnp.logical_not(even)), (face_a, even)):
        first = jnp.where(top, 2, 0)
        ref[0:BX] = state[0, first]
        ref[BX : 2 * BX] = state[0, first + 1]
    copies[1].wait()
    for ref, top in ((face_b, jnp.logical_not(even)), (face_a, even)):
        ref[EARLY:FACE] = state[1, jnp.where(top, 3, 0), 0:SPLIT]


def column_kernel(state, coarse, x_chip, x_core):
    core0 = lax.rem(lax.axis_index("wide"), 2) == 0
    for ref, low in ((x_chip, core0), (x_core, jnp.logical_not(core0))):
        for z in range(NPL):
            for at, ch, first, last in ((0, 0, 0, BX - 1), (4, 0, 1, BX - 2), (8, 1, 0, BX - 1)):
                ref[at + z : at + z + 1] = jnp.where(
                    low, state[ch, z, first : first + 1], state[ch, z, last : last + 1]
                )
        for k in range(4):
            ref[12:13, k * CY : (k + 1) * CY] = jnp.where(
                low, coarse[k, 0:1], coarse[k, CX - 1 : CX]
            )
        ref[13:16] = jnp.zeros((3, NY), F32)


def x_sides(x_chip, x_core, rows):
    w = lax.axis_index("wide")
    core0 = lax.rem(w, 2) == 0
    left = jnp.where(core0, x_chip[rows], x_core[rows]) * flag(w > 0)
    right = jnp.where(core0, x_core[rows], x_chip[rows]) * flag(w < NWIDE - 1)
    return left, right


def late_kernel(state, x_chip, x_core, own, late_b, late_a):
    even = lax.rem(lax.axis_index("narrow"), 2) == 0
    left, right = x_sides(x_chip, x_core, slice(0, 8))
    for ref, top in ((late_b, jnp.logical_not(even)), (late_a, even)):
        ref[0:CORNERS] = state[1, jnp.where(top, 3, 0), SPLIT:BX]
        ref[CORNERS : CORNERS + 1] = jnp.where(top, left[3:4], left[0:1])
        ref[CORNERS + 1 : CORNERS + 2] = jnp.where(top, right[3:4], right[0:1])
        ref[CORNERS + 2 : LATE] = jnp.zeros((LATE - CORNERS - 2, NY), F32)


def widen(ref, at, rough):
    for k in range(CX):
        ref[at, 4 * k : 4 * k + 4] = jnp.broadcast_to(rough[k : k + 1], (4, NY))


def spread_kernel(coarse, fine):
    for k in range(3):
        widen(fine, k, spread(coarse[k]))


def local_terms(c, state, own, fine, fx, fz, known, scale, dxy):
    r0 = 8 * c
    here, at, after = pl.ds(r0, 8), pl.ds(r0 + 8, 8), pl.ds(r0 + 16, 8)
    for z in range(NPL):
        v = own[z, at]
        dx = x_up(v, own[z, after]) - x_down(v, own[z, here])
        dy = y_up(v) - y_down(v)
        m = 1.0 - v * v
        drive = m * (v - 1.5 * (state[1, z, here] + fine[2, here]) * m)
        if z in (0, NPL - 1):
            known[z, here] = drive
            dxy[z // 2, 0, here] = dx
            dxy[z // 2, 1, here] = dy
            continue
        dz = own[z + 1, at] - own[z - 1, at]
        an = weigh(dz, dx, dy, fine[0, here], fine[1, here])
        wt = an * an
        quarter = 0.25 * wt
        fz[z - 1, here] = quarter * dz
        fx[z - 1, here] = quarter * dx
        fy = quarter * dy
        known[z, here] = (y_up(fy) - y_down(fy)) + drive
        scale[z - 1, here] = DT * inverse(wt)


def inside_kernel(state, fine, consts_in, own, fx, fz, known, scale, dxy, consts, sem):
    fetch = pltpu.make_async_copy(consts_in, consts, sem)
    fetch.start()
    for z in range(NPL):
        own[z, 8 : 8 + BX] = state[0, z]

    def chunk(c, carry):
        local_terms(c, state, own, fine, fx, fz, known, scale, dxy)
        return carry

    for c in range(1, BX // 8 - 1):
        chunk(c, 0)
    fetch.wait()


def edge_kernel(
    state, coarse, fine, x_chip, x_core, own_in, fx_in, fz_in, known_in, scale_in, dxy_in,
    own, fx, fz, known, scale, dxy, rims, base,
):
    left, right = x_sides(x_chip, x_core, slice(0, 4))
    for z in range(NPL):
        own[z, 7:8] = left[z : z + 1]
        own[z, 8 + BX : 9 + BX] = right[z : z + 1]
    left, right = x_sides(x_chip, x_core, slice(12, 13))
    rows = [side[:, k * CY : (k + 1) * CY] for side in (left, right) for k in (0, 1)]
    rims[...] = spread(jnp.concatenate(rows + rows, 0))
    for c in (0, BX // 8 - 1):
        local_terms(c, state, own, fine, fx, fz, known, scale, dxy)
    t, e = coarse[2], coarse[3]
    row = rows_of(t)
    down, up = [], []
    for k, v in ((2, t), (3, e)):
        before, after = left[:, k * CY : (k + 1) * CY], right[:, k * CY : (k + 1) * CY]
        down.append(jnp.where(row == 0, before, pltpu.roll(v, 1, 0)))
        up.append(jnp.where(row == CX - 1, after, pltpu.roll(v, CX - 1, 0)))
    near = [tuple(down), tuple(up), (y_up(t), y_up(e)), (y_down(t), y_down(e))]
    total = jnp.zeros_like(t)
    for tn, en in near:
        total = total + (1.0 + 0.5 * (e + en)) * (tn - t)
    base[...] = total


def phase_kernel(
    coarse, own, fine, fx12, fz12, known, scale12, dxy, zb, za, base, consts,
    fresh, spectral, lines,
    sides, halo, fx, fz03, fzout, bent, scale03, change,
):
    n = lax.axis_index("narrow")
    even = lax.rem(n, 2) == 0
    has_low, has_high = flag(n > 0), flag(n < NNAR - 1)
    for face, at, there in (
        (zb, jnp.where(even, 0, 2), jnp.where(even, has_low, has_high)),
        (za, jnp.where(even, 2, 0), jnp.where(even, has_high, has_low)),
    ):
        for k in range(2):
            halo[at + k, 8 : 8 + BX] = face[k * BX : (k + 1) * BX] * there
    low = jnp.where(even, zb[ROUGH:EARLY], za[ROUGH:EARLY])
    high = jnp.where(even, za[ROUGH:EARLY], zb[ROUGH:EARLY])
    for k, v in enumerate((low, low, high, high)):
        wide = spread(v[:, (k % 2) * CY : (k % 2 + 1) * CY])
        sides[k] = wide
        lines[8 + 4 * (k % 2) + 2 * (k // 2) : 9 + 4 * (k % 2) + 2 * (k // 2)] = wide[0:1]
        lines[9 + 4 * (k % 2) + 2 * (k // 2) : 10 + 4 * (k % 2) + 2 * (k // 2)] = wide[CX - 1 : CX]
    t, e = coarse[2], coarse[3]
    still = base[...]
    for v, there in ((low, has_low), (high, has_high)):
        tn, en = v[:, 2 * CY : 3 * CY] * there, v[:, 3 * CY :] * there
        still = still + (1.0 + 0.5 * (e + en)) * (tn - t)
    for z in range(NPL):
        fx[z, 7:8] = jnp.zeros((1, NY), F32)
        fx[z, 8 + BX : 9 + BX] = jnp.zeros((1, NY), F32)
    for z in (1, 2):
        fx[z, 8 : 8 + BX] = fx12[z - 1]
    planes = [(halo, 0), (halo, 1), (own, 0), (own, 1), (own, 2), (own, 3), (halo, 2), (halo, 3)]

    def get(k, rows):
        ref, z = planes[k]
        return ref[z, rows]

    def fluxes(c, carry):
        r0 = 8 * c
        here, at, after = pl.ds(r0, 8), pl.ds(r0 + 8, 8), pl.ds(r0 + 16, 8)
        for side, (zz, there) in enumerate(((0, has_low), (5, has_high))):
            v = get(zz + 1, at)
            dz = get(zz + 2, at) - get(zz, at)
            dx = x_up(v, get(zz + 1, after)) - x_down(v, get(zz + 1, here))
            dy = y_up(v) - y_down(v)
            c2, s2 = (
                jnp.where(
                    rows_of(v) < 4, sides[k, 2 * c : 2 * c + 1], sides[k, 2 * c + 1 : 2 * c + 2]
                )
                for k in (2 * side, 2 * side + 1)
            )
            an = weigh(dz, dx, dy, c2, s2)
            fzout[side, here] = (0.25 * there) * (an * an * dz)
        for side, z in enumerate((0, NPL - 1)):
            dz = get(z + 3, at) - get(z + 1, at)
            dx, dy = dxy[side, 0, here], dxy[side, 1, here]
            an = weigh(dz, dx, dy, fine[0, here], fine[1, here])
            wt = an * an
            quarter = 0.25 * wt
            fz03[side, here] = quarter * dz
            fx[z, at] = quarter * dx
            fy = quarter * dy
            bent[side, here] = known[z, here] + (y_up(fy) - y_down(fy))
            scale03[side, here] = DT * inverse(wt)
        return carry

    for c in range(BX // 8):
        fluxes(c, 0)

    for side in range(2):
        for row in (0, BX - 1):
            fzout[side, row : row + 1] = jnp.zeros((1, NY), F32)
    flux_z = [(fzout, 0), (fz03, 0), (fz12, 0), (fz12, 1), (fz03, 1), (fzout, 1)]
    rest = [(bent, 0), (known, 1), (known, 2), (bent, 1)]
    scales = [(scale03, 0), (scale12, 0), (scale12, 1), (scale03, 1)]

    for c in range(BX // 8):
        here, at, after = pl.ds(8 * c, 8), pl.ds(8 * c + 8, 8), pl.ds(8 * c + 16, 8)
        total = jnp.zeros((8, NY), F32)
        for z in range(NPL):
            p, f = own[z, at], fx[z, at]
            spread_z = flux_z[z + 2][0][flux_z[z + 2][1], here] - flux_z[z][0][flux_z[z][1], here]
            spread_x = x_up(f, fx[z, after]) - x_down(f, fx[z, here])
            factor = scales[z][0][scales[z][1], here]
            rise = factor * (rest[z][0][rest[z][1], here] + spread_z + spread_x)
            total = total + rise
            if c in (0, BX // 8 - 1):
                row, line = (0, z) if c == 0 else (7, NPL + z)
                lines[line : line + 1] = factor[row : row + 1]
            fresh[z, here] = p + rise
        total = total + pltpu.roll(total, 1, 0)
        total = total + pltpu.roll(total, 2, 0)
        change[2 * c : 2 * c + 1] = total[3:4]
        change[2 * c + 1 : 2 * c + 2] = total[7:8]
    spectral[...] = dot(still, consts[SY_AT]) + dot(change[...], consts[MEAN_AT])


def rim_kernel(
    own, rims, x_chip, x_core, zb, za, lb, la, spectral_in, lines, consts, fresh_in,
    fresh, spectral,
):
    n, w = lax.axis_index("narrow"), lax.axis_index("wide")
    even = lax.rem(n, 2) == 0
    has_left, has_right = flag(w > 0), flag(w < NWIDE - 1)
    has_low, has_high = flag(n > 0), flag(n < NNAR - 1)
    inner = x_sides(x_chip, x_core, slice(4, 8))

    def beyond(b, a, rows, high):
        if high:
            return jnp.where(even, a[rows], b[rows]) * has_high
        return jnp.where(even, b[rows], a[rows]) * has_low

    def corner(high, s):
        return beyond(lb, la, slice(CORNERS + s, CORNERS + s + 1), high)

    def outer(high, plane, x):
        return beyond(zb, za, slice(plane * BX + x, plane * BX + x + 1), high)

    rim = (7, 8 + BX)
    values = [[], [], [], [], []]
    for s in range(2):
        for z in range(NPL):
            at = slice(rim[s], rim[s] + 1)
            here = own[z, at]
            below = own[z - 1, at] if z > 0 else corner(False, s)
            above = own[z + 1, at] if z < NPL - 1 else corner(True, s)
            side = inner[s][z : z + 1]
            x_lo, x_hi = (own[z, 7 + BX : 8 + BX], side) if s else (side, own[z, 8:9])
            for rows, v in zip(values, (here, below, above, x_lo, x_hi)):
                rows.append(v)
    for high in (False, True):
        for s in range(2):
            x, near = (BX - 1, BX - 2) if s else (0, 1)
            mine = own[NPL - 1 if high else 0, 8 + x : 9 + x]
            here, behind = outer(high, 0 if high else 1, x), outer(high, 1 if high else 0, x)
            beside, past = outer(high, 0 if high else 1, near), corner(high, s)
            below, above = (mine, behind) if high else (behind, mine)
            x_lo, x_hi = (beside, past) if s else (past, beside)
            for rows, v in zip(values, (here, below, above, x_lo, x_hi)):
                rows.append(v)
    here, below, above, x_lo, x_hi = (
        jnp.concatenate(rows + [jnp.zeros((4, NY), F32)], 0) for rows in values
    )
    c2, s2 = (
        jnp.concatenate(
            [jnp.broadcast_to(rims[k : k + 1], (NPL, NY)), jnp.broadcast_to(rims[k + 2 : k + 3], (NPL, NY)),
             lines[8 + 4 * k : 12 + 4 * k], jnp.zeros((4, NY), F32)], 0,
        )
        for k in (0, 1)
    )
    dz, dx, dy = above - below, x_hi - x_lo, y_up(here) - y_down(here)
    an = weigh(dz, dx, dy, c2, s2)
    quarter = 0.25 * (an * an)
    row = rows_of(here[0:8])
    x_part = quarter[0:8] * dx[0:8] * jnp.where(row < NPL, -has_left, has_right)
    z_flux = quarter[8:16] * dz[8:16]
    z_part = jnp.zeros((8, NY), F32)
    for high in (False, True):
        for s in range(2):
            line = z_flux[2 * high + s : 2 * high + s + 1]
            line = line * has_high if high else -has_low * line
            z_part = jnp.where(row == NPL * s + (NPL - 1 if high else 0), line, z_part)
    rise = lines[0:8] * (x_part + z_part)
    for c in range(2):
        for z in range(NPL):
            add = rise[NPL * c + z : NPL * c + z + 1]
            at = (BX - 1) * c
            fresh[z, at : at + 1] = fresh_in[z, at : at + 1] + add
    sums = [jnp.sum(rise[NPL * c : NPL * (c + 1)], axis=0, keepdims=True) for c in range(2)]
    more = dot(jnp.concatenate(sums + [jnp.zeros((14, NY), F32)], 0), consts[MEAN_AT])
    first = rows_of(spectral_in)
    moved = spectral_in[...] + jnp.where(
        first == 0, more[0:1], jnp.where(first == CX - 1, more[1:2], 0.0)
    )
    spectral[...] = moved


def solute_kernel(state, own, x_chip, x_core, zb, za, lb, la, fresh, out, sown, grown, sems):
    phase_out = [
        pltpu.make_async_copy(fresh.at[z], out.at[0, z], sems.at[8 + z]) for z in range(NPL)
    ]
    for copy in phase_out:
        copy.start()
    n = lax.axis_index("narrow")
    even = lax.rem(n, 2) == 0
    left, right = x_sides(x_chip, x_core, slice(8, 12))
    has_low, has_high = flag(n > 0), flag(n < NNAR - 1)
    for z in range(NPL):
        sown[z, 8 : 8 + BX] = state[1, z]
        sown[z, 7:8] = left[z : z + 1]
        sown[z, 8 + BX : 9 + BX] = right[z : z + 1]

    def step(c):
        r0 = 8 * c
        here, at, after = pl.ds(r0, 8), pl.ds(r0 + 8, 8), pl.ds(r0 + 16, 8)

        beyond = pl.ds(r0 + BX, 8)
        ps = (
            [has_low * jnp.where(even, zb[beyond], za[beyond])]
            + [own[z, at] for z in range(NPL)]
            + [has_high * jnp.where(even, za[here], zb[here])]
        )
        if r0 < SPLIT:
            (b, a), there = (zb, za), pl.ds(EARLY + r0, 8)
        else:
            (b, a), there = (lb, la), pl.ds(r0 - SPLIT, 8)
        ss = (
            [has_low * jnp.where(even, b[there], a[there])]
            + [sown[z, at] for z in range(NPL)]
            + [has_high * jnp.where(even, a[there], b[there])]
        )
        for z in range(NPL):
            p, s = ps[z + 1], ss[z + 1]
            q = 0.55 - 0.25 * p
            near = [
                (ps[z], ss[z]),
                (ps[z + 2], ss[z + 2]),
                (x_up(p, own[z, after]), x_up(s, sown[z, after])),
                (x_down(p, own[z, here]), x_down(s, sown[z, here])),
                (y_up(p), y_up(s)),
                (y_down(p), y_down(s)),
            ]
            total = jnp.zeros_like(p)
            for pn, sn in near:
                total = total + (q - 0.25 * pn) * (sn - s)
            grown[z, here] = s + DT * total + (0.5 + 0.425 * s) * (fresh[z, here] - p)
        store(c).start()

    def store(c):
        rows = pl.ds(8 * c, 8)
        return pltpu.make_async_copy(grown.at[:, rows], out.at[1, :, rows], sems.at[c])

    for c in range(BX // 8):
        step(c)
    for c in range(BX // 8):
        store(c).wait()
    for copy in phase_out:
        copy.wait()


def eliminate(state, f, consts, first):
    states = []
    for i, v in enumerate(f):
        inv = consts[INV_AT + 8 * (first + i) : INV_AT + 8 * (first + i) + 8]
        state = inv * v if state is None else inv * v + (KBAR * inv) * state
        states.append(state)
    return states


def back(x, states, consts, first):
    values = []
    for i in range(len(states) - 1, -1, -1):
        inv = consts[INV_AT + 8 * (first + i) : INV_AT + 8 * (first + i) + 8]
        x = states[i] + (KBAR * inv) * x
        values.append(x)
    return values[::-1]


def mode_kernel(planes, consts, f, to_chip, to_core, to_next, modes):
    half = NNAR // 2
    folded = [
        [planes[m] + planes[NNAR - 1 - m] for m in range(half)],
        [planes[m] - planes[NNAR - 1 - m] for m in range(half)],
    ]
    for k in range(NNAR):
        total = float(SZ[k, 0]) * folded[k % 2][0]
        for m in range(1, half):
            total = total + float(SZ[k, m]) * folded[k % 2][m]
        modes[k * CX : (k + 1) * CX] = total
    values = [modes[pl.ds(j, 8, stride=CX), :] for j in range(CX)]
    for j in range(CX):
        f[j] = values[j]
    mirrored = values[::-1]
    right_margin = eliminate(None, values[12:], consts, 0)[-1]
    left_margin = eliminate(None, mirrored[12:], consts, 0)[-1]
    right_core = eliminate(None, values, consts, 4)[-1]
    left_core = eliminate(None, mirrored, consts, 4)[-1]
    core0 = lax.rem(lax.axis_index("wide"), 2) == 0
    to_core[0:8] = jnp.where(core0, right_margin, left_margin)
    to_core[8:16] = jnp.where(core0, right_core, left_core)
    to_chip[0:8] = jnp.where(core0, left_margin, right_margin)
    to_chip[8:16] = jnp.where(core0, left_core, right_core)
    to_next[...] = to_chip[0:8]


def pass_kernel(to_chip, by_core, consts, message):
    message[0:8] = to_chip[0:8]
    message[8:16] = to_chip[8:16] + consts[PASS_AT] * by_core[0:8]


def solve_kernel(f, by_chip, by_core, by_next, coarse, consts, out, rows):
    n, w = lax.axis_index("narrow"), lax.axis_index("wide")
    core0 = lax.rem(w, 2) == 0
    has_left, has_right = flag(w > 0), flag(w < NWIDE - 1)
    beyond = consts[PASS_AT] * by_next[...] * jnp.where(core0, flag(w < NWIDE - 2), flag(w > 1))
    other = jnp.concatenate([by_core[0:8], by_core[8:16] + beyond], 0)
    left = jnp.where(core0, by_chip[...], other) * has_left
    right = jnp.where(core0, other, by_chip[...]) * has_right
    values = [f[j] for j in range(CX)]
    mirrored = values[::-1]
    half = CX // 2

    low = eliminate(left[0:8], values[:half], consts, 4)
    high = eliminate(right[0:8], mirrored[:half], consts, 4)
    link = KBAR * consts[INV_AT + 8 * 11 : INV_AT + 8 * 12]
    x_low = consts[MEET_AT] * (low[-1] + link * high[-1])
    x_high = consts[MEET_AT] * (high[-1] + link * low[-1])
    x = back(x_low, low[:-1], consts, 4) + [x_low]
    x += (back(x_high, high[:-1], consts, 4) + [x_high])[::-1]

    for here, near, there in (
        (range(4), left, has_left),
        (range(CX - 1, CX - 5, -1), right, has_right),
    ):
        states = eliminate(near[8:16], [values[j] for j in here], consts, 20)
        found = back(states[-1], states[:-1], consts, 20) + [states[-1]]
        for j, v in zip(here, found):
            x[j] = x[j] + there * v

    weight = consts[pl.ds(pl.multiple_of(SZ_AT + 8 * n, 8), 8)]
    for j in range(CX):
        rows[j : j + 1] = jnp.sum(x[j] * weight, axis=0, keepdims=True)
    out[0] = coarse[2] + dot(rows[...], consts[SY_AT])


def kernel(body, outs, scratch=(), far=(), far_outs=(), aliases=None, mib=16):
    many = isinstance(outs, (list, tuple))

    def call(*args):
        return pl.pallas_call(
            body,
            out_shape=outs,
            in_specs=[HBM if i in far else VMEM for i in range(len(args))],
            out_specs=[HBM if i in far_outs else VMEM for i in range(len(outs))] if many else (HBM if far_outs else VMEM),
            input_output_aliases=aliases or {},
            scratch_shapes=list(scratch),
            compiler_params=params(mib),
            name=body.__name__,
        )(*args)

    return call


def afar(v):
    return pltpu.with_memory_space_constraint(v, pltpu.HBM)


def on_device(state_in, ids, frozen, temp, angles):
    inputs = [afar(v) for v in (state_in, ids, frozen, temp, angles.reshape(1, -1))]
    face_b, face_a, state, coarse = kernel(
        stage_kernel,
        [sds(FACE, NY)] * 2 + [sds(2, NPL, BX, NY), sds(4, CX, CY)],
        [
            pltpu.VMEM((1, CX, CY), jnp.int32),
            pltpu.VMEM((1, CX, CY), jnp.int32),
            pltpu.VMEM((1, CX, CY), F32),
            pltpu.VMEM((1, 64), F32),
            pltpu.SemaphoreType.DMA((6,)),
        ],
        far=range(5),
    )(*inputs)
    zb = lax.ppermute(face_b, BOTH, PAIR_B)
    za = lax.ppermute(face_a, "narrow", PAIR_A)
    to_chip, to_core = kernel(column_kernel, [sds(16, NY)] * 2)(state, coarse)
    x_chip = lax.ppermute(to_chip, BOTH, CHIPS)
    x_core = lax.ppermute(to_core, "wide", CORES)
    fine = kernel(spread_kernel, sds(3, BX, NY))(coarse)
    shapes = [
        sds(NPL, BX + 16, NY), sds(2, BX, NY), sds(2, BX, NY), sds(NPL, BX, NY), sds(2, BX, NY),
        sds(2, 2, BX, NY),
    ]
    *inside, consts = kernel(
        inside_kernel, shapes + [sds(*CONSTS.shape)], [pltpu.SemaphoreType.DMA], far=(2,)
    )(state, fine, afar(jnp.asarray(CONSTS)))
    late_b, late_a = kernel(late_kernel, [sds(LATE, NY)] * 2)(state, x_chip, x_core, inside[0])
    lb = lax.ppermute(late_b, BOTH, PAIR_B)
    la = lax.ppermute(late_a, "narrow", PAIR_A)
    own, fx12, fz12, known, scale12, dxy, rims, base = kernel(
        edge_kernel,
        shapes + [sds(8, NY), sds(CX, CY)],
        aliases={5 + i: i for i in range(6)},
    )(state, coarse, fine, x_chip, x_core, *inside)
    fresh, spectral, lines = kernel(
        phase_kernel,
        [sds(NPL, BX, NY), sds(CX, CY), sds(16, NY)],
        [
            pltpu.VMEM((4, CX, NY), F32),
            pltpu.VMEM((4, BX + 16, NY), F32),
            pltpu.VMEM((NPL, BX + 16, NY), F32),
            pltpu.VMEM((2, BX, NY), F32),
            pltpu.VMEM((2, BX, NY), F32),
            pltpu.VMEM((2, BX, NY), F32),
            pltpu.VMEM((2, BX, NY), F32),
            pltpu.VMEM((CX, NY), F32),
        ],
    )(coarse, own, fine, fx12, fz12, known, scale12, dxy, zb, za, base, consts)
    fresh, spectral = kernel(
        rim_kernel, [sds(NPL, BX, NY), sds(CX, CY)], aliases={11: 0}
    )(own, rims, x_chip, x_core, zb, za, lb, la, spectral, lines, consts, fresh)
    planes = lax.all_to_all(jnp.broadcast_to(spectral[None], (NNAR, CX, CY)), "narrow", 0, 0)
    state_new = kernel(
        solute_kernel,
        sds(2, NPL, BX, NY),
        [
            pltpu.VMEM((NPL, BX + 16, NY), F32),
            pltpu.VMEM((NPL, BX, NY), F32),
            pltpu.SemaphoreType.DMA((BX // 8 + NPL,)),
        ],
        far_outs=(0,),
    )(state, own, x_chip, x_core, zb, za, lb, la, fresh)
    f, to_chip, to_core, to_next = kernel(
        mode_kernel,
        [sds(CX, 8, CY), sds(16, CY), sds(16, CY), sds(8, CY)],
        [pltpu.VMEM((NNAR * CX, CY), F32)],
    )(planes, consts)
    by_core = lax.ppermute(to_core, "wide", CORES)
    by_next = lax.ppermute(to_next, BOTH, INWARD)
    by_chip = lax.ppermute(kernel(pass_kernel, sds(16, CY))(to_chip, by_core, consts), BOTH, CHIPS_LAST)
    adjusted = kernel(solve_kernel, sds(1, CX, CY), [pltpu.VMEM((CX, CY), F32)])(
        f, by_chip, by_core, by_next, coarse, consts
    )
    return state_new, adjusted


def solution(mesh):
    return jax.shard_map(
        on_device,
        mesh=mesh,
        in_specs=(
            P(None, "narrow", "wide", None),
            P("narrow", "wide", None),
            P("narrow", "wide", None),
            P("narrow", "wide", None),
            P(),
        ),
        out_specs=(P(None, "narrow", "wide", None), P("narrow", "wide", None)),
        check_vma=False,
    )
```

```python
import functools

import jax
import jax.numpy as jnp
import numpy as np
from jax import lax
from jax.experimental import pallas as pl
from jax.experimental.pallas import tpu as pltpu
from jax.sharding import PartitionSpec as P

F32 = jnp.float32
NNAR, NWIDE = 8, 32
NPL, BX, NY = 4, 64, 512
SPLIT = 24
ROUGH, EARLY, FACE = 128, 144, 144 + SPLIT
CORNERS, LATE = 64 - SPLIT, 72 - SPLIT
CX, CY = 16, 128
SUBX = 24
SIGMA, KBAR = 0.05, 0.75
DT = 0.15
VMEM = pl.BlockSpec(memory_space=pltpu.VMEM)
HBM = pl.BlockSpec(memory_space=pltpu.HBM)


def sds(*shape):
    return jax.ShapeDtypeStruct(shape, F32)


def params(mib):
    return pltpu.CompilerParams(vmem_limit_bytes=mib * 1024 * 1024)


def sine(points):
    k = np.arange(1, points + 1)
    return np.sqrt(2.0 / (points + 1)) * np.sin(np.pi * np.outer(k, k) / (points + 1))


def level(points):
    return 2.0 - 2.0 * np.cos(np.pi * np.arange(1, points + 1) / (points + 1))


SZ, SY = sine(8), sine(CY)
MEAN_Y = np.repeat(SY, 4, axis=0) / 64.0
SZ_ROWS = np.repeat(SZ[:, :, None], CY, 2)


def elimination():
    diag = SIGMA + KBAR * (level(8)[:, None] + level(CY)[None, :] + 2.0)
    inv = [1.0 / diag]
    for _ in range(SUBX - 1):
        inv.append(1.0 / (diag - KBAR * KBAR * inv[-1]))
    return np.stack(inv)


INVERSE = elimination()


LINK = KBAR * INVERSE
PASS = np.prod(LINK[4:20], axis=0)
MEET = 1.0 / (1.0 - LINK[11] ** 2)

CONSTS = np.concatenate(
    [SY, MEAN_Y, INVERSE.reshape(-1, CY), SZ_ROWS.reshape(-1, CY), PASS, MEET]
).astype(np.float32)
SY_AT, MEAN_AT, INV_AT, SZ_AT = slice(0, 128), slice(128, 640), 640, 640 + 8 * SUBX
PASS_AT = slice(SZ_AT + 64, SZ_AT + 72)
MEET_AT = slice(SZ_AT + 72, SZ_AT + 80)


def flat(n, w):
    return n * NWIDE + w


def everywhere(step):
    return [(flat(n, w), flat(*step(n, w))) for n in range(NNAR) for w in range(NWIDE)]


def swap_b(n, w):
    return (n, w ^ 1) if n in (0, NNAR - 1) else (((n + 1) ^ 1) - 1, w)


def swap_chips(n, w):
    if w in (0, NWIDE - 1):
        return (n ^ 4, w) if n % 4 in (1, 2) else (n, NWIDE - 1 - w)
    return n, ((w + 1) ^ 1) - 1


def swap_chips_last(n, w):
    return (n ^ 1, w) if w in (0, NWIDE - 1) else (n, ((w + 1) ^ 1) - 1)


def inward(n, w):
    to = w + 2 if w % 2 else w - 2
    return n, to if 0 <= to < NWIDE else w ^ 1


BOTH = ("narrow", "wide")
PAIR_A = [(i, i ^ 1) for i in range(NNAR)]
CORES = [(i, i ^ 1) for i in range(NWIDE)]
PAIR_B, CHIPS = everywhere(swap_b), everywhere(swap_chips)
INWARD, CHIPS_LAST = everywhere(inward), everywhere(swap_chips_last)


def lanes(v):
    return lax.broadcasted_iota(jnp.int32, v.shape, v.ndim - 1)


def rows_of(v):
    return lax.broadcasted_iota(jnp.int32, v.shape, len(v.shape) - 2)


def y_up(v):
    n = v.shape[-1]
    return jnp.where(lanes(v) == n - 1, 0.0, pltpu.roll(v, n - 1, v.ndim - 1))


def y_down(v):
    return jnp.where(lanes(v) == 0, 0.0, pltpu.roll(v, 1, v.ndim - 1))


def x_up(v, after):
    return pltpu.roll(jnp.where(rows_of(v) == 0, after, v), 7, v.ndim - 2)


def x_down(v, before):
    return pltpu.roll(jnp.where(rows_of(v) == 7, before, v), 1, v.ndim - 2)


def inverse(v):
    guess = pl.reciprocal(v, approx=True)
    return guess * (2.0 - v * guess)


def weigh(dz, dx, dy, c2, s2):
    q0, a, b = dz * dz, dx * dx, dy * dy
    r = a + b
    uv = s2 * (b - a) + c2 * (dx * dy)
    num = q0 * q0 + r * r - 2.0 * (uv * uv)
    over = inverse(q0 + r + 4.0)
    return 0.55 + 0.6 * (num * (over * over))


def flag(cond):
    return jnp.where(cond, 1.0, 0.0).astype(F32)


def spread(v):
    lane = lax.shift_right_logical(lanes(v), 2)
    return jnp.concatenate(
        [jnp.take_along_axis(v, lane + 32 * j, axis=1) for j in range(NY // CY)], 1
    )


def halves(v):
    high = v.astype(jnp.bfloat16)
    return high, (v - high.astype(F32)).astype(jnp.bfloat16)


def dot(a, b):
    (a1, a2), (b1, b2) = halves(a), halves(b)
    mul = functools.partial(jnp.dot, preferred_element_type=F32)
    return mul(a1, b1) + (mul(a1, b2) + mul(a2, b1))


def stage_kernel(
    state_in, ids_in, frozen_in, temp_in, angles_in,
    face_b, face_a, state, coarse,
    ids, frozen, temp, angles, sems,
):
    copies = [
        pltpu.make_async_copy(src, dst, sems.at[i])
        for i, (src, dst) in enumerate(
            [
                (state_in.at[0], state.at[0]),
                (state_in.at[1], state.at[1]),
                (ids_in, ids),
                (frozen_in, frozen),
                (temp_in, temp),
                (angles_in, angles),
            ]
        )
    ]
    for copy in copies[2:] + copies[:2]:
        copy.start()
    for copy in copies[2:]:
        copy.wait()
    table = jnp.concatenate([angles[...], angles[...]], 1)
    c = jnp.take_along_axis(jnp.broadcast_to(jnp.cos(table), (CX, CY)), ids[0], axis=1)
    s = jnp.take_along_axis(jnp.broadcast_to(jnp.sin(table), (CX, CY)), ids[0], axis=1)
    coarse[0] = c * c - s * s
    coarse[1] = c * s
    coarse[2] = temp[0]
    coarse[3] = -0.5 * frozen[0].astype(F32)
    even = lax.rem(lax.axis_index("narrow"), 2) == 0
    for ref in (face_b, face_a):
        for k in range(4):
            ref[ROUGH:EARLY, k * CY : (k + 1) * CY] = coarse[k]
    copies[0].wait()
    for ref, top in ((face_b, jnp.logical_not(even)), (face_a, even)):
        first = jnp.where(top, 2, 0)
        ref[0:BX] = state[0, first]
        ref[BX : 2 * BX] = state[0, first + 1]
    copies[1].wait()
    for ref, top in ((face_b, jnp.logical_not(even)), (face_a, even)):
        ref[EARLY:FACE] = state[1, jnp.where(top, 3, 0), 0:SPLIT]


def column_kernel(state, coarse, x_chip, x_core):
    core0 = lax.rem(lax.axis_index("wide"), 2) == 0
    for ref, low in ((x_chip, core0), (x_core, jnp.logical_not(core0))):
        for z in range(NPL):
            for at, ch, first, last in ((0, 0, 0, BX - 1), (4, 0, 1, BX - 2), (8, 1, 0, BX - 1)):
                ref[at + z : at + z + 1] = jnp.where(
                    low, state[ch, z, first : first + 1], state[ch, z, last : last + 1]
                )
        for k in range(4):
            ref[12:13, k * CY : (k + 1) * CY] = jnp.where(
                low, coarse[k, 0:1], coarse[k, CX - 1 : CX]
            )
        ref[13:16] = jnp.zeros((3, NY), F32)


def x_sides(x_chip, x_core, rows):
    w = lax.axis_index("wide")
    core0 = lax.rem(w, 2) == 0
    left = jnp.where(core0, x_chip[rows], x_core[rows]) * flag(w > 0)
    right = jnp.where(core0, x_core[rows], x_chip[rows]) * flag(w < NWIDE - 1)
    return left, right


def late_kernel(state, x_chip, x_core, own, late_b, late_a):
    even = lax.rem(lax.axis_index("narrow"), 2) == 0
    left, right = x_sides(x_chip, x_core, slice(0, 8))
    for ref, top in ((late_b, jnp.logical_not(even)), (late_a, even)):
        ref[0:CORNERS] = state[1, jnp.where(top, 3, 0), SPLIT:BX]
        ref[CORNERS : CORNERS + 1] = jnp.where(top, left[3:4], left[0:1])
        ref[CORNERS + 1 : CORNERS + 2] = jnp.where(top, right[3:4], right[0:1])
        ref[CORNERS + 2 : LATE] = jnp.zeros((LATE - CORNERS - 2, NY), F32)


def widen(ref, at, rough):
    for k in range(CX):
        ref[at, 4 * k : 4 * k + 4] = jnp.broadcast_to(rough[k : k + 1], (4, NY))


def local_terms(c, state, own, fine, fx, fz, known, scale, dxy):
    r0 = 8 * c
    here, at, after = pl.ds(r0, 8), pl.ds(r0 + 8, 8), pl.ds(r0 + 16, 8)
    for z in range(NPL):
        v = own[z, at]
        dx = x_up(v, own[z, after]) - x_down(v, own[z, here])
        dy = y_up(v) - y_down(v)
        m = 1.0 - v * v
        drive = m * (v - 1.5 * (state[1, z, here] + fine[2, here]) * m)
        if z in (0, NPL - 1):
            known[z, here] = drive
            dxy[z // 2, 0, here] = dx
            dxy[z // 2, 1, here] = dy
            continue
        dz = own[z + 1, at] - own[z - 1, at]
        an = weigh(dz, dx, dy, fine[0, here], fine[1, here])
        wt = an * an
        quarter = 0.25 * wt
        fz[z - 1, here] = quarter * dz
        fx[z - 1, here] = quarter * dx
        fy = quarter * dy
        known[z, here] = (y_up(fy) - y_down(fy)) + drive
        scale[z - 1, here] = DT * inverse(wt)


def inside_kernel(state, coarse, consts_in, own, fx, fz, known, scale, dxy, fine, consts, sem):
    fetch = pltpu.make_async_copy(consts_in, consts, sem)
    fetch.start()
    for k in range(3):
        widen(fine, k, spread(coarse[k]))
    for z in range(NPL):
        own[z, 8 : 8 + BX] = state[0, z]

    def chunk(c, carry):
        local_terms(c, state, own, fine, fx, fz, known, scale, dxy)
        return carry

    for c in range(1, BX // 8 - 1):
        chunk(c, 0)
    fetch.wait()


def edge_kernel(
    state, coarse, fine, x_chip, x_core, own_in, fx_in, fz_in, known_in, scale_in, dxy_in,
    own, fx, fz, known, scale, dxy, rims, base,
):
    left, right = x_sides(x_chip, x_core, slice(0, 4))
    for z in range(NPL):
        own[z, 7:8] = left[z : z + 1]
        own[z, 8 + BX : 9 + BX] = right[z : z + 1]
    left, right = x_sides(x_chip, x_core, slice(12, 13))
    rows = [side[:, k * CY : (k + 1) * CY] for side in (left, right) for k in (0, 1)]
    rims[...] = spread(jnp.concatenate(rows + rows, 0))
    for c in (0, BX // 8 - 1):
        local_terms(c, state, own, fine, fx, fz, known, scale, dxy)
    t, e = coarse[2], coarse[3]
    row = rows_of(t)
    down, up = [], []
    for k, v in ((2, t), (3, e)):
        before, after = left[:, k * CY : (k + 1) * CY], right[:, k * CY : (k + 1) * CY]
        down.append(jnp.where(row == 0, before, pltpu.roll(v, 1, 0)))
        up.append(jnp.where(row == CX - 1, after, pltpu.roll(v, CX - 1, 0)))
    near = [tuple(down), tuple(up), (y_up(t), y_up(e)), (y_down(t), y_down(e))]
    total = jnp.zeros_like(t)
    for tn, en in near:
        total = total + (1.0 + 0.5 * (e + en)) * (tn - t)
    base[...] = total


def phase_kernel(
    coarse, own, fine, fx12, fz12, known, scale12, dxy, zb, za, base, consts,
    fresh, spectral, lines,
    sides, halo, fx, fz03, fzout, bent, scale03, change,
):
    n = lax.axis_index("narrow")
    even = lax.rem(n, 2) == 0
    has_low, has_high = flag(n > 0), flag(n < NNAR - 1)
    for face, at, there in (
        (zb, jnp.where(even, 0, 2), jnp.where(even, has_low, has_high)),
        (za, jnp.where(even, 2, 0), jnp.where(even, has_high, has_low)),
    ):
        for k in range(2):
            halo[at + k, 8 : 8 + BX] = face[k * BX : (k + 1) * BX] * there
    low = jnp.where(even, zb[ROUGH:EARLY], za[ROUGH:EARLY])
    high = jnp.where(even, za[ROUGH:EARLY], zb[ROUGH:EARLY])
    for k, v in enumerate((low, low, high, high)):
        wide = spread(v[:, (k % 2) * CY : (k % 2 + 1) * CY])
        sides[k] = wide
        lines[8 + 4 * (k % 2) + 2 * (k // 2) : 9 + 4 * (k % 2) + 2 * (k // 2)] = wide[0:1]
        lines[9 + 4 * (k % 2) + 2 * (k // 2) : 10 + 4 * (k % 2) + 2 * (k // 2)] = wide[CX - 1 : CX]
    t, e = coarse[2], coarse[3]
    still = base[...]
    for v, there in ((low, has_low), (high, has_high)):
        tn, en = v[:, 2 * CY : 3 * CY] * there, v[:, 3 * CY :] * there
        still = still + (1.0 + 0.5 * (e + en)) * (tn - t)
    for z in range(NPL):
        fx[z, 7:8] = jnp.zeros((1, NY), F32)
        fx[z, 8 + BX : 9 + BX] = jnp.zeros((1, NY), F32)
    for z in (1, 2):
        fx[z, 8 : 8 + BX] = fx12[z - 1]
    planes = [(halo, 0), (halo, 1), (own, 0), (own, 1), (own, 2), (own, 3), (halo, 2), (halo, 3)]

    def get(k, rows):
        ref, z = planes[k]
        return ref[z, rows]

    def fluxes(c, carry):
        r0 = 8 * c
        here, at, after = pl.ds(r0, 8), pl.ds(r0 + 8, 8), pl.ds(r0 + 16, 8)
        for side, (zz, there) in enumerate(((0, has_low), (5, has_high))):
            v = get(zz + 1, at)
            dz = get(zz + 2, at) - get(zz, at)
            dx = x_up(v, get(zz + 1, after)) - x_down(v, get(zz + 1, here))
            dy = y_up(v) - y_down(v)
            c2, s2 = (
                jnp.where(
                    rows_of(v) < 4, sides[k, 2 * c : 2 * c + 1], sides[k, 2 * c + 1 : 2 * c + 2]
                )
                for k in (2 * side, 2 * side + 1)
            )
            an = weigh(dz, dx, dy, c2, s2)
            fzout[side, here] = (0.25 * there) * (an * an * dz)
        for side, z in enumerate((0, NPL - 1)):
            dz = get(z + 3, at) - get(z + 1, at)
            dx, dy = dxy[side, 0, here], dxy[side, 1, here]
            an = weigh(dz, dx, dy, fine[0, here], fine[1, here])
            wt = an * an
            quarter = 0.25 * wt
            fz03[side, here] = quarter * dz
            fx[z, at] = quarter * dx
            fy = quarter * dy
            bent[side, here] = known[z, here] + (y_up(fy) - y_down(fy))
            scale03[side, here] = DT * inverse(wt)
        return carry

    for c in range(BX // 8):
        fluxes(c, 0)

    for side in range(2):
        for row in (0, BX - 1):
            fzout[side, row : row + 1] = jnp.zeros((1, NY), F32)
    flux_z = [(fzout, 0), (fz03, 0), (fz12, 0), (fz12, 1), (fz03, 1), (fzout, 1)]
    rest = [(bent, 0), (known, 1), (known, 2), (bent, 1)]
    scales = [(scale03, 0), (scale12, 0), (scale12, 1), (scale03, 1)]

    for c in range(BX // 8):
        here, at, after = pl.ds(8 * c, 8), pl.ds(8 * c + 8, 8), pl.ds(8 * c + 16, 8)
        total = jnp.zeros((8, NY), F32)
        for z in range(NPL):
            p, f = own[z, at], fx[z, at]
            spread_z = flux_z[z + 2][0][flux_z[z + 2][1], here] - flux_z[z][0][flux_z[z][1], here]
            spread_x = x_up(f, fx[z, after]) - x_down(f, fx[z, here])
            factor = scales[z][0][scales[z][1], here]
            rise = factor * (rest[z][0][rest[z][1], here] + spread_z + spread_x)
            total = total + rise
            if c in (0, BX // 8 - 1):
                row, line = (0, z) if c == 0 else (7, NPL + z)
                lines[line : line + 1] = factor[row : row + 1]
            fresh[z, here] = p + rise
        total = total + pltpu.roll(total, 1, 0)
        total = total + pltpu.roll(total, 2, 0)
        change[2 * c : 2 * c + 1] = total[3:4]
        change[2 * c + 1 : 2 * c + 2] = total[7:8]
    spectral[...] = dot(still, consts[SY_AT]) + dot(change[...], consts[MEAN_AT])


def rim_kernel(
    own, rims, x_chip, x_core, zb, za, lb, la, spectral_in, lines, consts, fresh_in,
    fresh, spectral,
):
    n, w = lax.axis_index("narrow"), lax.axis_index("wide")
    even = lax.rem(n, 2) == 0
    has_left, has_right = flag(w > 0), flag(w < NWIDE - 1)
    has_low, has_high = flag(n > 0), flag(n < NNAR - 1)
    inner = x_sides(x_chip, x_core, slice(4, 8))

    def beyond(b, a, rows, high):
        if high:
            return jnp.where(even, a[rows], b[rows]) * has_high
        return jnp.where(even, b[rows], a[rows]) * has_low

    def corner(high, s):
        return beyond(lb, la, slice(CORNERS + s, CORNERS + s + 1), high)

    def outer(high, plane, x):
        return beyond(zb, za, slice(plane * BX + x, plane * BX + x + 1), high)

    rim = (7, 8 + BX)
    values = [[], [], [], [], []]
    for s in range(2):
        for z in range(NPL):
            at = slice(rim[s], rim[s] + 1)
            here = own[z, at]
            below = own[z - 1, at] if z > 0 else corner(False, s)
            above = own[z + 1, at] if z < NPL - 1 else corner(True, s)
            side = inner[s][z : z + 1]
            x_lo, x_hi = (own[z, 7 + BX : 8 + BX], side) if s else (side, own[z, 8:9])
            for rows, v in zip(values, (here, below, above, x_lo, x_hi)):
                rows.append(v)
    for high in (False, True):
        for s in range(2):
            x, near = (BX - 1, BX - 2) if s else (0, 1)
            mine = own[NPL - 1 if high else 0, 8 + x : 9 + x]
            here, behind = outer(high, 0 if high else 1, x), outer(high, 1 if high else 0, x)
            beside, past = outer(high, 0 if high else 1, near), corner(high, s)
            below, above = (mine, behind) if high else (behind, mine)
            x_lo, x_hi = (beside, past) if s else (past, beside)
            for rows, v in zip(values, (here, below, above, x_lo, x_hi)):
                rows.append(v)
    here, below, above, x_lo, x_hi = (
        jnp.concatenate(rows + [jnp.zeros((4, NY), F32)], 0) for rows in values
    )
    c2, s2 = (
        jnp.concatenate(
            [jnp.broadcast_to(rims[k : k + 1], (NPL, NY)), jnp.broadcast_to(rims[k + 2 : k + 3], (NPL, NY)),
             lines[8 + 4 * k : 12 + 4 * k], jnp.zeros((4, NY), F32)], 0,
        )
        for k in (0, 1)
    )
    dz, dx, dy = above - below, x_hi - x_lo, y_up(here) - y_down(here)
    an = weigh(dz, dx, dy, c2, s2)
    quarter = 0.25 * (an * an)
    row = rows_of(here[0:8])
    x_part = quarter[0:8] * dx[0:8] * jnp.where(row < NPL, -has_left, has_right)
    z_flux = quarter[8:16] * dz[8:16]
    z_part = jnp.zeros((8, NY), F32)
    for high in (False, True):
        for s in range(2):
            line = z_flux[2 * high + s : 2 * high + s + 1]
            line = line * has_high if high else -has_low * line
            z_part = jnp.where(row == NPL * s + (NPL - 1 if high else 0), line, z_part)
    rise = lines[0:8] * (x_part + z_part)
    for c in range(2):
        for z in range(NPL):
            add = rise[NPL * c + z : NPL * c + z + 1]
            at = (BX - 1) * c
            fresh[z, at : at + 1] = fresh_in[z, at : at + 1] + add
    sums = [jnp.sum(rise[NPL * c : NPL * (c + 1)], axis=0, keepdims=True) for c in range(2)]
    more = dot(jnp.concatenate(sums + [jnp.zeros((14, NY), F32)], 0), consts[MEAN_AT])
    first = rows_of(spectral_in)
    moved = spectral_in[...] + jnp.where(
        first == 0, more[0:1], jnp.where(first == CX - 1, more[1:2], 0.0)
    )
    spectral[...] = moved


def solute_kernel(state, own, x_chip, x_core, zb, za, lb, la, fresh, out, sown, grown, sems):
    phase_out = [
        pltpu.make_async_copy(fresh.at[z], out.at[0, z], sems.at[8 + z]) for z in range(NPL)
    ]
    for copy in phase_out:
        copy.start()
    n = lax.axis_index("narrow")
    even = lax.rem(n, 2) == 0
    left, right = x_sides(x_chip, x_core, slice(8, 12))
    has_low, has_high = flag(n > 0), flag(n < NNAR - 1)
    for z in range(NPL):
        sown[z, 8 : 8 + BX] = state[1, z]
        sown[z, 7:8] = left[z : z + 1]
        sown[z, 8 + BX : 9 + BX] = right[z : z + 1]

    def step(c):
        r0 = 8 * c
        here, at, after = pl.ds(r0, 8), pl.ds(r0 + 8, 8), pl.ds(r0 + 16, 8)

        beyond = pl.ds(r0 + BX, 8)
        ps = (
            [has_low * jnp.where(even, zb[beyond], za[beyond])]
            + [own[z, at] for z in range(NPL)]
            + [has_high * jnp.where(even, za[here], zb[here])]
        )
        if r0 < SPLIT:
            (b, a), there = (zb, za), pl.ds(EARLY + r0, 8)
        else:
            (b, a), there = (lb, la), pl.ds(r0 - SPLIT, 8)
        ss = (
            [has_low * jnp.where(even, b[there], a[there])]
            + [sown[z, at] for z in range(NPL)]
            + [has_high * jnp.where(even, a[there], b[there])]
        )
        for z in range(NPL):
            p, s = ps[z + 1], ss[z + 1]
            q = 0.55 - 0.25 * p
            near = [
                (ps[z], ss[z]),
                (ps[z + 2], ss[z + 2]),
                (x_up(p, own[z, after]), x_up(s, sown[z, after])),
                (x_down(p, own[z, here]), x_down(s, sown[z, here])),
                (y_up(p), y_up(s)),
                (y_down(p), y_down(s)),
            ]
            total = jnp.zeros_like(p)
            for pn, sn in near:
                total = total + (q - 0.25 * pn) * (sn - s)
            grown[z, here] = s + DT * total + (0.5 + 0.425 * s) * (fresh[z, here] - p)
        store(c).start()

    def store(c):
        rows = pl.ds(8 * c, 8)
        return pltpu.make_async_copy(grown.at[:, rows], out.at[1, :, rows], sems.at[c])

    for c in range(BX // 8):
        step(c)
    for c in range(BX // 8):
        store(c).wait()
    for copy in phase_out:
        copy.wait()


def eliminate(state, f, consts, first):
    states = []
    for i, v in enumerate(f):
        inv = consts[INV_AT + 8 * (first + i) : INV_AT + 8 * (first + i) + 8]
        state = inv * v if state is None else inv * v + (KBAR * inv) * state
        states.append(state)
    return states


def back(x, states, consts, first):
    values = []
    for i in range(len(states) - 1, -1, -1):
        inv = consts[INV_AT + 8 * (first + i) : INV_AT + 8 * (first + i) + 8]
        x = states[i] + (KBAR * inv) * x
        values.append(x)
    return values[::-1]


def mode_kernel(planes, consts, f, to_chip, to_core, to_next, modes):
    half = NNAR // 2
    folded = [
        [planes[m] + planes[NNAR - 1 - m] for m in range(half)],
        [planes[m] - planes[NNAR - 1 - m] for m in range(half)],
    ]
    for k in range(NNAR):
        total = float(SZ[k, 0]) * folded[k % 2][0]
        for m in range(1, half):
            total = total + float(SZ[k, m]) * folded[k % 2][m]
        modes[k * CX : (k + 1) * CX] = total
    values = [modes[pl.ds(j, 8, stride=CX), :] for j in range(CX)]
    for j in range(CX):
        f[j] = values[j]
    mirrored = values[::-1]
    right_margin = eliminate(None, values[12:], consts, 0)[-1]
    left_margin = eliminate(None, mirrored[12:], consts, 0)[-1]
    right_core = eliminate(None, values, consts, 4)[-1]
    left_core = eliminate(None, mirrored, consts, 4)[-1]
    core0 = lax.rem(lax.axis_index("wide"), 2) == 0
    to_core[0:8] = jnp.where(core0, right_margin, left_margin)
    to_core[8:16] = jnp.where(core0, right_core, left_core)
    to_chip[0:8] = jnp.where(core0, left_margin, right_margin)
    to_chip[8:16] = jnp.where(core0, left_core, right_core)
    to_next[...] = to_chip[0:8]


def pass_kernel(to_chip, by_core, consts, message):
    message[0:8] = to_chip[0:8]
    message[8:16] = to_chip[8:16] + consts[PASS_AT] * by_core[0:8]


def solve_kernel(f, by_chip, by_core, by_next, coarse, consts, out, rows):
    n, w = lax.axis_index("narrow"), lax.axis_index("wide")
    core0 = lax.rem(w, 2) == 0
    has_left, has_right = flag(w > 0), flag(w < NWIDE - 1)
    beyond = consts[PASS_AT] * by_next[...] * jnp.where(core0, flag(w < NWIDE - 2), flag(w > 1))
    other = jnp.concatenate([by_core[0:8], by_core[8:16] + beyond], 0)
    left = jnp.where(core0, by_chip[...], other) * has_left
    right = jnp.where(core0, other, by_chip[...]) * has_right
    values = [f[j] for j in range(CX)]
    mirrored = values[::-1]
    half = CX // 2

    low = eliminate(left[0:8], values[:half], consts, 4)
    high = eliminate(right[0:8], mirrored[:half], consts, 4)
    link = KBAR * consts[INV_AT + 8 * 11 : INV_AT + 8 * 12]
    x_low = consts[MEET_AT] * (low[-1] + link * high[-1])
    x_high = consts[MEET_AT] * (high[-1] + link * low[-1])
    x = back(x_low, low[:-1], consts, 4) + [x_low]
    x += (back(x_high, high[:-1], consts, 4) + [x_high])[::-1]

    for here, near, there in (
        (range(4), left, has_left),
        (range(CX - 1, CX - 5, -1), right, has_right),
    ):
        states = eliminate(near[8:16], [values[j] for j in here], consts, 20)
        found = back(states[-1], states[:-1], consts, 20) + [states[-1]]
        for j, v in zip(here, found):
            x[j] = x[j] + there * v

    weight = consts[pl.ds(pl.multiple_of(SZ_AT + 8 * n, 8), 8)]
    for j in range(CX):
        rows[j : j + 1] = jnp.sum(x[j] * weight, axis=0, keepdims=True)
    out[0] = coarse[2] + dot(rows[...], consts[SY_AT])


def kernel(body, outs, scratch=(), far=(), far_outs=(), aliases=None, mib=16):
    many = isinstance(outs, (list, tuple))

    def call(*args):
        return pl.pallas_call(
            body,
            out_shape=outs,
            in_specs=[HBM if i in far else VMEM for i in range(len(args))],
            out_specs=[HBM if i in far_outs else VMEM for i in range(len(outs))] if many else (HBM if far_outs else VMEM),
            input_output_aliases=aliases or {},
            scratch_shapes=list(scratch),
            compiler_params=params(mib),
            name=body.__name__,
        )(*args)

    return call


def afar(v):
    return pltpu.with_memory_space_constraint(v, pltpu.HBM)


def on_device(state_in, ids, frozen, temp, angles):
    inputs = [afar(v) for v in (state_in, ids, frozen, temp, angles.reshape(1, -1))]
    face_b, face_a, state, coarse = kernel(
        stage_kernel,
        [sds(FACE, NY)] * 2 + [sds(2, NPL, BX, NY), sds(4, CX, CY)],
        [
            pltpu.VMEM((1, CX, CY), jnp.int32),
            pltpu.VMEM((1, CX, CY), jnp.int32),
            pltpu.VMEM((1, CX, CY), F32),
            pltpu.VMEM((1, 64), F32),
            pltpu.SemaphoreType.DMA((6,)),
        ],
        far=range(5),
    )(*inputs)
    zb = lax.ppermute(face_b, BOTH, PAIR_B)
    za = lax.ppermute(face_a, "narrow", PAIR_A)
    to_chip, to_core = kernel(column_kernel, [sds(16, NY)] * 2)(state, coarse)
    x_chip = lax.ppermute(to_chip, BOTH, CHIPS)
    x_core = lax.ppermute(to_core, "wide", CORES)
    shapes = [
        sds(NPL, BX + 16, NY), sds(2, BX, NY), sds(2, BX, NY), sds(NPL, BX, NY), sds(2, BX, NY),
        sds(2, 2, BX, NY),
    ]
    *inside, fine, consts = kernel(
        inside_kernel, shapes + [sds(3, BX, NY), sds(*CONSTS.shape)], [pltpu.SemaphoreType.DMA], far=(2,)
    )(state, coarse, afar(jnp.asarray(CONSTS)))
    late_b, late_a = kernel(late_kernel, [sds(LATE, NY)] * 2)(state, x_chip, x_core, inside[0])
    lb = lax.ppermute(late_b, BOTH, PAIR_B)
    la = lax.ppermute(late_a, "narrow", PAIR_A)
    own, fx12, fz12, known, scale12, dxy, rims, base = kernel(
        edge_kernel,
        shapes + [sds(8, NY), sds(CX, CY)],
        aliases={5 + i: i for i in range(6)},
    )(state, coarse, fine, x_chip, x_core, *inside)
    fresh, spectral, lines = kernel(
        phase_kernel,
        [sds(NPL, BX, NY), sds(CX, CY), sds(16, NY)],
        [
            pltpu.VMEM((4, CX, NY), F32),
            pltpu.VMEM((4, BX + 16, NY), F32),
            pltpu.VMEM((NPL, BX + 16, NY), F32),
            pltpu.VMEM((2, BX, NY), F32),
            pltpu.VMEM((2, BX, NY), F32),
            pltpu.VMEM((2, BX, NY), F32),
            pltpu.VMEM((2, BX, NY), F32),
            pltpu.VMEM((CX, NY), F32),
        ],
    )(coarse, own, fine, fx12, fz12, known, scale12, dxy, zb, za, base, consts)
    fresh, spectral = kernel(
        rim_kernel, [sds(NPL, BX, NY), sds(CX, CY)], aliases={11: 0}
    )(own, rims, x_chip, x_core, zb, za, lb, la, spectral, lines, consts, fresh)
    planes = lax.all_to_all(jnp.broadcast_to(spectral[None], (NNAR, CX, CY)), "narrow", 0, 0)
    state_new = kernel(
        solute_kernel,
        sds(2, NPL, BX, NY),
        [
            pltpu.VMEM((NPL, BX + 16, NY), F32),
            pltpu.VMEM((NPL, BX, NY), F32),
            pltpu.SemaphoreType.DMA((BX // 8 + NPL,)),
        ],
        far_outs=(0,),
    )(state, own, x_chip, x_core, zb, za, lb, la, fresh)
    f, to_chip, to_core, to_next = kernel(
        mode_kernel,
        [sds(CX, 8, CY), sds(16, CY), sds(16, CY), sds(8, CY)],
        [pltpu.VMEM((NNAR * CX, CY), F32)],
    )(planes, consts)
    by_core = lax.ppermute(to_core, "wide", CORES)
    by_next = lax.ppermute(to_next, BOTH, INWARD)
    by_chip = lax.ppermute(kernel(pass_kernel, sds(16, CY))(to_chip, by_core, consts), BOTH, CHIPS_LAST)
    adjusted = kernel(solve_kernel, sds(1, CX, CY), [pltpu.VMEM((CX, CY), F32)])(
        f, by_chip, by_core, by_next, coarse, consts
    )
    return state_new, adjusted


def solution(mesh):
    return jax.shard_map(
        on_device,
        mesh=mesh,
        in_specs=(
            P(None, "narrow", "wide", None),
            P("narrow", "wide", None),
            P("narrow", "wide", None),
            P("narrow", "wide", None),
            P(),
        ),
        out_specs=(P(None, "narrow", "wide", None), P("narrow", "wide", None)),
        check_vma=False,
    )
```
